32 devices in a mesh: dp: 8 (over y, x, core), expert: 4 (over z).
Axes of the slice: x: 2, y: 2, z: 4, core: 2. Of those that a mesh axis runs over, the one named last changes fastest.
Arguments:
- tokens: bfloat16 [8192, 1536], P(('dp', 'expert')), may hold values from -6 to 6
- first_gain: float32 [1536], replicated, may hold values from 0.5 to 1.5
- query_weight: bfloat16 [1536, 1536], replicated, may hold values from -2 to 2
- key_weight: bfloat16 [1536, 512], replicated, may hold values from -2 to 2
- value_weight: bfloat16 [1536, 512], replicated, may hold values from -0.15625 to 0.15625
- output_weight: bfloat16 [1536, 1536], replicated, may hold values from -1.5 to 1.5
- second_gain: float32 [1536], replicated, may hold values from 0.5 to 1.5
- router_weight: bfloat16 [1536, 20], replicated, may hold values from -0.078125 to 0.078125
- gate_weight: bfloat16 [20, 1536, 512], P('expert'), may hold values from -0.15625 to 0.15625
- up_weight: bfloat16 [20, 1536, 512], P('expert'), may hold values from -0.15625 to 0.15625
- down_weight: bfloat16 [20, 1536, 512], P('expert'), may hold values from -3 to 3
- cotangent: bfloat16 [8192, 1536], P(('dp', 'expert')), may hold values from -6 to 6
- routes: int32 [8192, 8], P(('dp', 'expert')), may hold values from 0 to 19, all different within a row; in each aligned block of 256 rows (0 to 255, 256 to 511, ...) at most 115 rows name the same one
- segments: int32 [8192], P(('dp', 'expert')), may hold values from 0 to 4, as said below
- threshold: float32 [24], replicated, may hold values from 5 to 10
Outputs:
- block_out: bfloat16 [8192, 1536], P(('dp', 'expert'))
- input_grad: float32 [8192, 1536], P(('dp', 'expert'))
- first_gain_grad: float32 [1536], P(('dp', 'expert'))
- query_grad: float32 [1536, 1536], P(('dp', 'expert'))
- key_grad: float32 [1536, 512], P(('dp', 'expert'))
- value_grad: float32 [1536, 512], P(('dp', 'expert'))
- projection_grad: float32 [1536, 1536], P(('dp', 'expert'))
- second_gain_grad: float32 [1536], P(('dp', 'expert'))
- router_grad: float32 [1536, 20], P(('dp', 'expert'))
- gate_grad: float32 [20, 1536, 512], P('expert', 'dp')
- up_grad: float32 [20, 1536, 512], P('expert', 'dp')
- down_grad: float32 [20, 1536, 512], P('expert', 'dp')
- head_scale: float32 [24], replicated
- query_clipped: bfloat16 [1536, 1536], P(('dp', 'expert'))
- key_clipped: bfloat16 [1536, 512], P(('dp', 'expert'))
The draws below stay inside these ranges and needn't reach their ends.
Inputs may be any that keep to these rules, and one draw needn't show every extreme that they name: `routes`: among the tokens of one device (aligned blocks of 256 tokens) no expert is named more than 115 times, and some expert reaches 115 in some block; a token's 8 experts differ. `segments`: segment numbers never fall within a sequence of 1024 tokens, are 0 at each sequence's first token, and each sequence holds all of 0 to 4.
All inputs are finite; a program needn't handle non-finite values.
Results may differ from the reference program's by a relative error of at most 0.018.
Values may be sent and summed in bfloat16 or wider, within the bound.
No kernel may reach another device: no remote copies, remote signals or barrier semaphores. Data moves between devices by JAX's collectives and lax.ppermute only.
A program may use at most 320 MiB of HBM per device.

```python
import math
import jax
import jax.numpy as jnp
import numpy as np
from jax import lax

D = 1536
HEADS = 24
KV_HEADS = 8
HDIM = 64
FF = 512
TOPK = 8
TOK_DEV = 256
DOCS = 5
SEQ = 1024
EXPERTS = 20
TOKENS = 8192
CAP = 115


def draw_segments(key, part):
    seq_count = TOKENS // SEQ
    seq_keys = jax.random.split(key, seq_count)

    def one_sequence(seq_key):
        shuffled = jax.random.permutation(seq_key, SEQ - 1) + 1
        cut_points = jnp.sort(shuffled[:DOCS - 1])
        position_ids = jnp.arange(SEQ, dtype=jnp.int32)
        return jnp.sum((position_ids[:, None] >= cut_points[None, :]).astype(jnp.int32), axis=1)
    return jax.vmap(one_sequence)(seq_keys).reshape(TOKENS).astype(jnp.int32)


def column_scaled(entries, scale_key, group_total, low_end, high_end):
    log_scales = jax.random.uniform(scale_key, (group_total,), jnp.float32, math.log(low_end), math.log(high_end))
    entry_scale = float(D // 12) ** (-0.5)
    scaled = entries * jnp.exp(log_scales)[None, :, None] * entry_scale
    return scaled.reshape(D, group_total * HDIM).astype(jnp.bfloat16)


def draw_query_weight(key, part):
    entry_key = jax.random.fold_in(key, 101)
    scale_key = jax.random.fold_in(key, 102)
    entries = jnp.clip(jax.random.normal(entry_key, (D, HEADS, HDIM), jnp.float32), -3.0, 3.0)
    return column_scaled(entries, scale_key, HEADS, 0.65, 1.9)


def draw_key_weight(key, part):
    entry_key = jax.random.fold_in(key, 201)
    scale_key = jax.random.fold_in(key, 202)
    entries = jnp.clip(jax.random.normal(entry_key, (D, KV_HEADS, HDIM), jnp.float32), -3.0, 3.0)
    return column_scaled(entries, scale_key, KV_HEADS, 0.7, 1.4)


def block_scale(stream_key, dims, pieces, low, largest):
    def one(dim, shards_of):
        heights = jax.random.uniform(jax.random.fold_in(jax.random.fold_in(stream_key, 6), dim), (shards_of,), jnp.float32, low / len(pieces), largest / len(pieces))
        return jnp.repeat(jnp.exp(heights), dims[dim] // shards_of).reshape((-1,) + (1,) * (len(dims) - dim - 1))

    factor_of = one(*pieces[0])
    for cut in pieces[1:]:
        factor_of = factor_of * one(*cut)
    return factor_of


def shared_out(own_key, own, number, rows, amount, top, bound, slope):
    sequence = jax.random.permutation(own_key, amount)
    crowded, usual = shares(amount, rows * top, bound, slope, True), shares(amount, rows * top, bound, slope, False)
    places = jnp.arange(amount)

    def named(sizes, rotation):
        used = int((sizes > 0).sum())
        fixed = max(1, used // 4)
        passed = fixed + (places - fixed + rotation * (used - fixed)) % max(1, amount - fixed)
        return jnp.zeros((amount,), jnp.int32).at[sequence[jnp.where(places < fixed, places, passed)]].set(jnp.asarray(sizes, jnp.int32))

    sizes = jnp.where(number % 4 == 0, named(crowded, number // 4), named(usual, number - number // 4 - 1))
    mixed = jax.random.permutation(jax.random.fold_in(own, 3), amount)
    source_of, receiver = mixed[0:amount // 2 * 2:2], mixed[1:amount // 2 * 2:2]
    slack = jnp.minimum(sizes[source_of] - 1, bound - sizes[receiver]) // 2
    slack = jnp.where((source_of == sequence[0]) | (receiver == sequence[0]) | (sizes[receiver] == 0), 0, jnp.maximum(slack, 0))
    passed = jax.random.randint(jax.random.fold_in(own, 4), (amount // 2,), 0, 1 << 20) % (slack + 1)
    sizes = sizes.at[source_of].add(-passed).at[receiver].add(passed)
    items = jnp.searchsorted(jnp.cumsum(sizes), jnp.arange(rows * top), side="right").astype(jnp.int32)
    table = items.reshape(top, rows).T
    table = table[jax.random.permutation(jax.random.fold_in(own, 1), rows)]
    rotation = jax.random.randint(jax.random.fold_in(own, 2), (rows, 1), 0, top)
    return jnp.take_along_axis(table, (jnp.arange(top)[None, :] + rotation) % top, axis=1)


def shares(number_of, total, bound, lean, full):
    portions = [(1 << 20) // math.isqrt(rank ** lean) + 1 for rank in range(1, number_of + 1)]
    largest = bound if full else min(bound, max(-(-total // number_of), total * portions[0] // sum(portions)))
    least = 1 if total - largest >= number_of - 1 else 0
    given, spare = [largest] + [least] * (number_of - 1), total - largest - least * (number_of - 1)
    while spare > 0:
        movable = [i for i in range(1, number_of) if given[i] < largest] or [i for i in range(1, number_of) if given[i] < bound]
        mass, budget = sum([portions[i] for i in movable]), spare
        for i in movable:
            addition = min(bound - given[i], max(1, budget * portions[i] // mass), spare)
            given[i] = given[i] + addition
            spare = spare - addition
    return np.array(given)


def scatter_about(key, shape, width, reach, cuts=(), kind=jnp.bfloat16):
    drawn = width * jax.random.normal(key, shape, jnp.float32)
    if cuts:
        drawn = drawn * block_scale(key, shape, cuts, -0.22, 0.18)
    return jnp.clip(drawn, -reach, reach).astype(kind)


def setup_inputs(seed: int = 0) -> dict:
    arg_keys = jax.random.split(jax.random.key(seed), 16)
    tokens = scatter_about(arg_keys[0], (TOKENS, D), 1.0, 6.0, ((0, 32),))
    first_gain = jnp.clip(1.0 + 0.1 * jax.random.normal(arg_keys[1], (D,), jnp.float32), 0.5, 1.5)
    query_weight = draw_query_weight(jax.random.fold_in(arg_keys[15], 71), 0)
    key_weight = draw_key_weight(jax.random.fold_in(arg_keys[15], 71), 0)
    value_weight = scatter_about(arg_keys[4], (D, KV_HEADS * HDIM), D ** -0.5, 0.15625)
    output_weight = scatter_about(arg_keys[5], (D, HEADS * HDIM), (max(HEADS * HDIM // 96, 1)) ** -0.5, 1.5)
    second_gain = jnp.clip(1.0 + 0.1 * jax.random.normal(arg_keys[6], (D,), jnp.float32), 0.5, 1.5)
    router_weight = scatter_about(arg_keys[7], (D, EXPERTS), (4 * D) ** -0.5, 0.078125)
    gate_weight = scatter_about(arg_keys[8], (EXPERTS, D, FF), D ** -0.5, 0.15625, ((0, 4),))
    up_weight = scatter_about(arg_keys[9], (EXPERTS, D, FF), D ** -0.5, 0.15625, ((0, 4),))
    down_weight = scatter_about(arg_keys[10], (EXPERTS, D, FF), (max(FF // 128, 1)) ** -0.5, 3.0, ((0, 4),))
    cotangent = scatter_about(arg_keys[11], (TOKENS, D), 1.0, 6.0, ((0, 32),))
    routes_keys = jax.random.split(jax.random.fold_in(arg_keys[12], 1), TOKENS // TOK_DEV)
    routes_turns = jax.random.permutation(jax.random.fold_in(arg_keys[12], 3), TOKENS // TOK_DEV)
    routes = jax.vmap(lambda own, number: shared_out(jax.random.fold_in(arg_keys[12], 2), own, number, TOK_DEV, EXPERTS, TOPK, CAP, 1))(routes_keys, routes_turns).reshape((TOKENS, TOPK))
    segments = draw_segments(jax.random.fold_in(arg_keys[15], 71), 0)
    threshold = jnp.clip(jax.random.uniform(arg_keys[14], (HEADS,), jnp.float32, 5.0, 10.0), 5.0, 10.0)
    return {"tokens": tokens, "first_gain": first_gain, "query_weight": query_weight, "key_weight": key_weight, "value_weight": value_weight, "output_weight": output_weight, "second_gain": second_gain, "router_weight": router_weight, "gate_weight": gate_weight, "up_weight": up_weight, "down_weight": down_weight, "cotangent": cotangent, "routes": routes, "segments": segments, "threshold": threshold}


HIGHEST = lax.Precision.HIGHEST
ATTENTION_SCALE = 0.015625
RESIDUAL_SCALE = 0.22
NORM_EPSILON = 1e-06
ROTARY_BASE = 10000.0
MASKED_SCORE = -1e+30

@jax.custom_vjp
def low(v):
    return lax.optimization_barrier(v.astype(jnp.bfloat16)).astype(jnp.float32)

@jax.custom_vjp
def low_back(v):
    return v

def low_keep(v):
    return (low(v), None)

def low_pass(kept, grad):
    return (grad,)

def back_keep(v):
    return (v, None)

def back_low(kept, grad):
    return (low(grad),)
low.defvjp(low_keep, low_pass)
low_back.defvjp(back_keep, back_low)

def rotary_tables(positions, head_dim):
    half_dim = head_dim // 2
    inverse = ROTARY_BASE ** (-2.0 * jnp.arange(half_dim, dtype=jnp.float32) / head_dim)
    angles = positions.astype(jnp.float32)[:, None] * inverse[None, :]
    return (jnp.cos(angles)[:, None, :], jnp.sin(angles)[:, None, :])

def rotate(row_data, cosine, sine_table):
    half_dim = row_data.shape[-1] // 2
    lower_half = row_data[..., :half_dim]
    upper_half = row_data[..., half_dim:]
    return jnp.concatenate([lower_half * cosine - upper_half * sine_table, upper_half * cosine + lower_half * sine_table], axis=-1)

def rms_norm(hidden, gain_vec):
    factor = lax.rsqrt(lax.optimization_barrier(jnp.mean(hidden * hidden, axis=-1, keepdims=True)) + NORM_EPSILON)
    return hidden * factor * gain_vec

def attend_sequence(seq_parts):
    queries, key_rows, value_rows, segment_ids = seq_parts
    seq_len = queries.shape[0]
    group_count = key_rows.shape[1]
    group_ratio = queries.shape[1] // group_count
    spot_ids = jnp.arange(seq_len, dtype=jnp.int32)
    allowed = (segment_ids[:, None] == segment_ids[None, :]) & (spot_ids[None, :] <= spot_ids[:, None])
    query_groups = queries.reshape(seq_len, group_count, group_ratio, HDIM).transpose(1, 0, 2, 3)

    def one_group(group_parts):
        query_part, key_part, value_part = group_parts
        scores = low_back(jnp.einsum('trd,sd->rts', query_part, key_part, precision=HIGHEST) * ATTENTION_SCALE)
        masked = jnp.where(allowed[None], scores, MASKED_SCORE)
        weights = low(jax.nn.softmax(masked, axis=-1))
        mixed_rows = jnp.einsum('rts,sd->trd', weights, value_part, precision=HIGHEST)
        return (mixed_rows, lax.optimization_barrier(jnp.max(masked, axis=(1, 2))))
    mixed_rows, group_top = lax.map(jax.checkpoint(one_group), (query_groups, key_rows.transpose(1, 0, 2), value_rows.transpose(1, 0, 2)))
    return (mixed_rows.transpose(1, 0, 2, 3).reshape(seq_len, group_count * group_ratio * HDIM), group_top.reshape(group_count * group_ratio))

def slot_tables(routes):
    block_count = routes.shape[0] // TOK_DEV
    flat_routes = routes.reshape(block_count, TOK_DEV * TOPK)
    expert_ids = jnp.arange(EXPERTS, dtype=jnp.int32)
    route_hits = (flat_routes[:, :, None] == expert_ids[None, None, :]).astype(jnp.int32)
    route_rank = lax.optimization_barrier(jnp.sum(jnp.cumsum(route_hits, axis=1) * route_hits, axis=2)) - 1
    block_ids = jnp.arange(block_count, dtype=jnp.int32)[:, None]
    slot_target = ((flat_routes * block_count + block_ids) * CAP + route_rank).reshape(-1).astype(jnp.int32)
    route_index = jnp.arange(block_count * TOK_DEV * TOPK, dtype=jnp.int32)
    table = jnp.full((EXPERTS * block_count * CAP,), -1, dtype=jnp.int32).at[slot_target].set(route_index)
    return table.reshape(EXPERTS, block_count * CAP)

def reference(tokens, first_gain, query_weight, key_weight, value_weight, output_weight, second_gain, router_weight, gate_weight, up_weight, down_weight, cotangent, routes, segments, threshold):
    token_count = tokens.shape[0]
    positions = jnp.arange(token_count, dtype=jnp.int32) % SEQ
    cosine, sine_table = rotary_tables(positions, HDIM)
    tables = slot_tables(routes)
    expert_ids = jnp.arange(EXPERTS, dtype=jnp.int32)
    chosen = (routes[:, :, None] == expert_ids[None, None, :]).astype(jnp.float32)
    seq_count = token_count // SEQ

    def layer_forward(hidden_in, gain_one, w_query, w_key, w_value, w_output, gain_two, w_router, w_gate, w_up, w_down):
        first_normed = low(rms_norm(hidden_in, gain_one))
        query_raw = low_back(jnp.dot(first_normed, w_query, precision=HIGHEST))
        queries = low(rotate(query_raw.reshape(token_count, HEADS, HDIM), cosine, sine_table))
        key_raw = low_back(jnp.dot(first_normed, w_key, precision=HIGHEST))
        key_rows = low(rotate(key_raw.reshape(token_count, KV_HEADS, HDIM), cosine, sine_table))
        value_rows = low(low_back(jnp.dot(first_normed, w_value, precision=HIGHEST))).reshape(token_count, KV_HEADS, HDIM)
        attended, seq_top = lax.map(attend_sequence, (queries.reshape(seq_count, SEQ, HEADS, HDIM), key_rows.reshape(seq_count, SEQ, KV_HEADS, HDIM), value_rows.reshape(seq_count, SEQ, KV_HEADS, HDIM), segments.reshape(seq_count, SEQ)))
        head_max = lax.optimization_barrier(jnp.max(seq_top, axis=0))
        attended = low(low_back(attended.reshape(token_count, HEADS * HDIM)))
        attention_out = low_back(jnp.dot(attended, w_output.T, precision=HIGHEST))
        hidden_mid = hidden_in + RESIDUAL_SCALE * attention_out
        second_normed = low(rms_norm(hidden_mid, gain_two))
        logits = low_back(jnp.dot(second_normed, w_router, precision=HIGHEST))
        picked = lax.optimization_barrier(jnp.sum(chosen * logits[:, None, :], axis=-1))
        gate_values = jax.nn.softmax(picked, axis=-1)
        gate_flat = gate_values.reshape(-1)

        def one_expert(mixture, expert_parts):
            table, gate_one, up_one, down_one = expert_parts
            occupied = table >= 0
            source_route = jnp.where(occupied, table, 0)
            owner_token = source_route // TOPK
            row_data = second_normed[owner_token] * occupied[:, None].astype(jnp.float32)
            gate_pre = low_back(jnp.dot(row_data, gate_one, precision=HIGHEST))
            up_pre = low_back(jnp.dot(row_data, up_one, precision=HIGHEST))
            expert_hidden = low(jax.nn.silu(gate_pre) * up_pre)
            expert_out = low(low_back(jnp.dot(expert_hidden, down_one.T, precision=HIGHEST)))
            route_weight = jnp.where(occupied, gate_flat[source_route], 0.0)
            return (mixture.at[owner_token].add(expert_out * route_weight[:, None]), None)
        mixture, _ = lax.scan(jax.checkpoint(one_expert), jnp.zeros_like(hidden_mid), (tables, w_gate, w_up, w_down))
        return (hidden_mid + RESIDUAL_SCALE * mixture, head_max)
    primals = (tokens.astype(jnp.float32), first_gain.astype(jnp.float32), query_weight.astype(jnp.float32), key_weight.astype(jnp.float32), value_weight.astype(jnp.float32), output_weight.astype(jnp.float32), second_gain.astype(jnp.float32), router_weight.astype(jnp.float32), gate_weight.astype(jnp.float32), up_weight.astype(jnp.float32), down_weight.astype(jnp.float32))
    block_value, pullback, head_max = jax.vjp(layer_forward, *primals, has_aux=True)
    all_grads = pullback(cotangent.astype(jnp.float32))
    head_scale = threshold / jnp.maximum(head_max, threshold)
    group_scale = lax.optimization_barrier(jnp.min(head_scale.reshape(KV_HEADS, HEADS // KV_HEADS), axis=1))
    query_clipped = (query_weight.astype(jnp.float32) * jnp.repeat(jnp.sqrt(head_scale), HDIM)[None, :]).astype(jnp.bfloat16)
    key_clipped = (key_weight.astype(jnp.float32) * jnp.repeat(jnp.sqrt(group_scale), HDIM)[None, :]).astype(jnp.bfloat16)
    return (block_value.astype(jnp.bfloat16), all_grads[0], all_grads[1], all_grads[2], all_grads[3], all_grads[4], all_grads[5], all_grads[6], all_grads[7], all_grads[8], all_grads[9], all_grads[10], head_scale, query_clipped, key_clipped)
```

```python
import functools

import jax
import jax.numpy as jnp
import numpy as np
from jax import lax
from jax.experimental import pallas as pl
from jax.experimental.pallas import tpu as pltpu
from jax.sharding import PartitionSpec as P

HDIM = 64
LANES = 128
ATTENTION_SCALE = 0.015625
RESIDUAL_SCALE = 0.22
NORM_EPSILON = 1e-06
ROTARY_BASE = 10000.0
MASKED_SCORE = -1e30
BF16 = jnp.bfloat16
F32 = jnp.float32
NN = (((1,), (0,)), ((), ()))
NT = (((1,), (1,)), ((), ()))
TN = (((0,), (0,)), ((), ()))
VMEM_LIMIT = 56 * 1024 * 1024


def dot(left, right, dims=NN):
    return lax.dot_general(left, right, dims, preferred_element_type=F32)


def round_up(count, unit):
    return (count + unit - 1) // unit * unit


def low_lanes(rows):
    return lax.broadcasted_iota(jnp.int32, (rows, LANES), 1) < HDIM


def partner_lanes(slab):
    lane = lax.broadcasted_iota(jnp.int32, slab.shape, 1) % HDIM
    half = HDIM // 2
    return jnp.where(lane < half, pltpu.roll(slab, LANES - half, 1), pltpu.roll(slab, half, 1))


def vmem():
    return pl.BlockSpec(memory_space=pltpu.VMEM)


def params(**more):
    return pltpu.CompilerParams(vmem_limit_bytes=VMEM_LIMIT, **more)


def info_kernel(expert_pad, routes_ref, segments_ref, info_ref):
    rows, top_count = routes_ref.shape
    lane = lax.broadcasted_iota(jnp.int32, (rows, LANES), 1)
    chosen = jnp.zeros((rows, LANES), F32)
    for k in range(top_count):
        chosen = chosen + jnp.where(routes_ref[:, k : k + 1] == lane, 1.0, 0.0)
    chosen = chosen.astype(BF16)
    first = lax.broadcasted_iota(jnp.int32, (rows, rows), 0)
    second = lax.broadcasted_iota(jnp.int32, (rows, rows), 1)
    earlier = jnp.where(first < second, 1.0, 0.0).astype(BF16)
    same = jnp.where(first == second, 1.0, 0.0).astype(BF16)
    rank = dot(chosen, earlier, TN)
    named = dot(chosen, same, TN)
    table = jnp.where(named > 0.5, rank, -1.0).astype(jnp.int32)
    info_ref[:expert_pad, :] = table[:expert_pad]
    info_ref[expert_pad:, :] = jnp.broadcast_to(segments_ref[...], (8, rows))


def front_kernel(tokens_ref, gain_ref, key_ref, value_ref, cos_ref, sin_ref, normed_ref, factor_ref, kv_ref):
    hidden = tokens_ref[...].astype(F32)
    factor = lax.rsqrt(jnp.mean(hidden * hidden, axis=-1, keepdims=True) + NORM_EPSILON)
    normed = (hidden * factor * gain_ref[...]).astype(BF16)
    normed_ref[...] = normed
    factor_ref[...] = factor
    keys = dot(normed, key_ref[...])
    values = dot(normed, value_ref[...])
    cosine, sine = cos_ref[...], sin_ref[...]
    low = low_lanes(hidden.shape[0])
    for i in range(keys.shape[1] // LANES):
        slab = keys[:, i * LANES : (i + 1) * LANES]
        slab = slab * cosine + partner_lanes(slab) * sine
        value_slab = values[:, i * LANES : (i + 1) * LANES]
        kv_ref[2 * i] = jnp.where(low, slab, pltpu.roll(value_slab, HDIM, 1)).astype(BF16)
        kv_ref[2 * i + 1] = jnp.where(low, pltpu.roll(slab, HDIM, 1), value_slab).astype(BF16)


def query_kernel(normed_ref, query_ref, cos_ref, sin_ref, out_ref):
    raw = dot(normed_ref[...], query_ref[...])
    cosine, sine = cos_ref[...], sin_ref[...]
    for i in range(raw.shape[1] // LANES):
        slab = raw[:, i * LANES : (i + 1) * LANES]
        slab = slab * cosine + partner_lanes(slab) * sine
        out_ref[:, i * LANES : (i + 1) * LANES] = (slab.astype(BF16).astype(F32) * ATTENTION_SCALE).astype(BF16)


def fill_bias(bias_ref, seg_column, seg_rows):
    slots, rows, keys = bias_ref.shape
    for k in range(slots):
        allowed = seg_column == seg_rows[k : k + 1, :]
        if k == 0:
            allowed = allowed & (
                lax.broadcasted_iota(jnp.int32, (rows, keys), 1)
                <= lax.broadcasted_iota(jnp.int32, (rows, keys), 0)
            )
        bias_ref[k] = jnp.where(allowed, 0.0, MASKED_SCORE)


def head_slab(block, head, upper):
    slab = block[:, (head // 2) * LANES : (head // 2 + 1) * LANES].astype(F32)
    low = low_lanes(slab.shape[0])
    if (head % 2 == 1) != upper:
        slab = pltpu.roll(slab, HDIM, 1)
    return jnp.where(low != upper, slab, 0.0)


def attend_kernel(slots, ratio, need_ref, query_ref, seg_column_ref, seg_rows_ref, *refs):
    kv_refs = refs[:slots]
    attended_ref, lse_ref, top_ref, bias_ref, stacked_ref, acc_ref, max_ref, sum_ref = refs[slots:]
    rows = query_ref.shape[0]
    low = low_lanes(rows)
    lane = lax.broadcasted_iota(jnp.int32, (rows, LANES), 1)
    need = need_ref[0]

    @pl.when(pl.program_id(0) == 0)
    def _():
        fill_bias(bias_ref, seg_column_ref[...], seg_rows_ref[...])

    outs = []
    lse_all = jnp.zeros((rows, LANES), F32)
    top_all = jnp.zeros((8, LANES), F32)
    for group in range(2):
        for r in range(ratio):
            stacked_ref[r * rows : (r + 1) * rows, :] = head_slab(
                query_ref, group * ratio + r, False
            ).astype(BF16)
        for k in range(slots):

            def step(k=k):
                kv = kv_refs[k][group]
                scores = dot(stacked_ref[...], kv, NT).reshape(ratio, rows, rows)
                scores = (scores + bias_ref[k][None]).reshape(ratio * rows, rows)
                top = jnp.max(scores, axis=-1, keepdims=True)
                if k == 0:
                    weights = jnp.exp(scores - top)
                    max_ref[...] = top
                    sum_ref[...] = jnp.sum(weights, axis=-1, keepdims=True)
                    acc_ref[...] = dot(weights.astype(BF16), kv)
                else:
                    before = max_ref[...]
                    top = jnp.maximum(top, before)
                    shrink = jnp.exp(before - top)
                    weights = jnp.exp(scores - top)
                    max_ref[...] = top
                    sum_ref[...] = sum_ref[...] * shrink + jnp.sum(weights, axis=-1, keepdims=True)
                    acc_ref[...] = acc_ref[...] * shrink + dot(weights.astype(BF16), kv)

            if k == 0:
                step()
            else:
                pl.when(k < need)(step)
        total = sum_ref[...]
        mixed = acc_ref[...] / total
        lse = max_ref[...] + jnp.log(total)
        for r in range(ratio):
            head = group * ratio + r
            outs.append(mixed[r * rows : (r + 1) * rows])
            lse_all = jnp.where(lane == head, lse[r * rows : (r + 1) * rows], lse_all)
            peak = jnp.max(max_ref[r * rows : (r + 1) * rows, :], axis=0, keepdims=True)
            top_all = jnp.where(lane[:8] == head, peak, top_all)
    for i in range(len(outs) // 2):
        attended_ref[:, i * LANES : (i + 1) * LANES] = jnp.where(
            low, pltpu.roll(outs[2 * i], HDIM, 1), outs[2 * i + 1]
        ).astype(BF16)
    lse_ref[0] = lse_all
    top_ref[0] = top_all


def attend(queries, kv_slots, seg_column, seg_rows, need, ratio):
    slots = len(kv_slots)
    rows, width = queries.shape
    groups = kv_slots[0].shape[0]
    steps = groups // 2
    block = 2 * ratio * HDIM
    return pl.pallas_call(
        functools.partial(attend_kernel, slots, ratio),
        out_shape=(
            jax.ShapeDtypeStruct((rows, width), BF16),
            jax.ShapeDtypeStruct((steps, rows, LANES), F32),
            jax.ShapeDtypeStruct((steps, 8, LANES), F32),
        ),
        grid=(steps,),
        in_specs=[
            pl.BlockSpec(memory_space=pltpu.SMEM),
            pl.BlockSpec((rows, block), lambda s: (0, s)),
            pl.BlockSpec((rows, 1), lambda s: (0, 0)),
            pl.BlockSpec(seg_rows.shape, lambda s: (0, 0)),
        ]
        + [pl.BlockSpec((2, rows, LANES), lambda s: (s, 0, 0))] * slots,
        out_specs=(
            pl.BlockSpec((rows, block), lambda s: (0, s)),
            pl.BlockSpec((1, rows, LANES), lambda s: (s, 0, 0)),
            pl.BlockSpec((1, 8, LANES), lambda s: (s, 0, 0)),
        ),
        scratch_shapes=[
            pltpu.VMEM((slots, rows, rows), F32),
            pltpu.VMEM((ratio * rows, LANES), BF16),
            pltpu.VMEM((ratio * rows, LANES), F32),
            pltpu.VMEM((ratio * rows, 1), F32),
            pltpu.VMEM((ratio * rows, 1), F32),
        ],
        compiler_params=params(),
        name="attend",
    )(need, queries, seg_column, seg_rows, *kv_slots)


def attend_back_kernel(slots, ratio, need_ref, query_ref, attended_ref, grad_ref, lse_ref, cos_ref, sin_ref, seg_column_ref, seg_rows_ref, *refs):
    kv_refs = refs[:slots]
    back_ref = refs[slots]
    dkv_refs = refs[slots + 1 : 2 * slots + 1]
    bias_ref, query_s, grad_s, acc_ref, lse_s, delta_s = refs[2 * slots + 1 :]
    rows = query_ref.shape[0]
    low = low_lanes(rows)
    need = need_ref[0]

    @pl.when(pl.program_id(0) == 0)
    def _():
        fill_bias(bias_ref, seg_column_ref[...], seg_rows_ref[...])

    outs = []
    for group in range(2):
        for r in range(ratio):
            head = group * ratio + r
            part = slice(r * rows, (r + 1) * rows)
            query_s[part, :] = head_slab(query_ref, head, False).astype(BF16)
            grad = head_slab(grad_ref, head, True)
            grad_s[part, :] = grad.astype(BF16)
            delta_s[part, :] = jnp.sum(grad * head_slab(attended_ref, head, True), axis=-1, keepdims=True)
            lse_s[part, :] = lse_ref[0, :, head : head + 1]
        for k in range(slots):

            def step(k=k):
                kv = kv_refs[k][group]
                scores = dot(query_s[...], kv, NT).reshape(ratio, rows, rows)
                scores = (scores + bias_ref[k][None]).reshape(ratio * rows, rows)
                weights = jnp.exp(scores - lse_s[...])
                weight_grad = dot(grad_s[...], kv, NT)
                score_grad = (weights * (weight_grad - delta_s[...])).astype(BF16)
                query_part = dot(score_grad, kv)
                if k == 0:
                    acc_ref[...] = query_part
                else:
                    acc_ref[...] += query_part
                dkv_refs[k][group] = (
                    dot(score_grad, query_s[...], TN) + dot(weights.astype(BF16), grad_s[...], TN)
                ).astype(BF16)

            if k == 0:
                step()
            else:
                pl.when(k < need)(step)

                @pl.when(k >= need)
                def _(k=k):
                    dkv_refs[k][group] = jnp.zeros((rows, LANES), BF16)

        for r in range(ratio):
            outs.append(acc_ref[r * rows : (r + 1) * rows, :] * ATTENTION_SCALE)
    cosine, sine = cos_ref[...], sin_ref[...]
    for i in range(len(outs) // 2):
        slab = jnp.where(low, outs[2 * i], pltpu.roll(outs[2 * i + 1], HDIM, 1))
        slab = slab * cosine - partner_lanes(slab) * sine
        back_ref[:, i * LANES : (i + 1) * LANES] = slab.astype(BF16)


def attend_back(queries, attended, grad, lse, tables, kv_slots, seg_column, seg_rows, need, ratio):
    slots = len(kv_slots)
    rows, width = queries.shape
    groups = kv_slots[0].shape[0]
    steps = groups // 2
    block = 2 * ratio * HDIM
    whole = pl.BlockSpec((rows, LANES), lambda s: (0, 0))
    wide = pl.BlockSpec((rows, block), lambda s: (0, s))
    pair = pl.BlockSpec((2, rows, LANES), lambda s: (s, 0, 0))
    out = pl.pallas_call(
        functools.partial(attend_back_kernel, slots, ratio),
        out_shape=(jax.ShapeDtypeStruct((rows, width), BF16),)
        + (jax.ShapeDtypeStruct((groups, rows, LANES), BF16),) * slots,
        grid=(steps,),
        in_specs=[
            pl.BlockSpec(memory_space=pltpu.SMEM),
            wide,
            wide,
            wide,
            pl.BlockSpec((1, rows, LANES), lambda s: (s, 0, 0)),
            whole,
            whole,
            pl.BlockSpec((rows, 1), lambda s: (0, 0)),
            pl.BlockSpec(seg_rows.shape, lambda s: (0, 0)),
        ]
        + [pair] * slots,
        out_specs=(wide,) + (pair,) * slots,
        scratch_shapes=[
            pltpu.VMEM((slots, rows, rows), F32),
            pltpu.VMEM((ratio * rows, LANES), BF16),
            pltpu.VMEM((ratio * rows, LANES), BF16),
            pltpu.VMEM((ratio * rows, LANES), F32),
            pltpu.VMEM((ratio * rows, 1), F32),
            pltpu.VMEM((ratio * rows, 1), F32),
        ],
        compiler_params=params(),
        name="attend_back",
    )(need, queries, attended, grad, lse, *tables, seg_column, seg_rows, *kv_slots)
    return out[0], out[1:]


def unpack_kernel(dkv_ref, cos_ref, sin_ref, key_ref, value_ref):
    groups, rows, _ = dkv_ref.shape
    low = low_lanes(rows)
    cosine, sine = cos_ref[...], sin_ref[...]
    for i in range(groups // 2):
        even, odd = dkv_ref[2 * i], dkv_ref[2 * i + 1]
        slab = jnp.where(low, even, pltpu.roll(odd, HDIM, 1))
        slab = slab * cosine - partner_lanes(slab) * sine
        key_ref[:, i * LANES : (i + 1) * LANES] = slab.astype(BF16)
        value_ref[:, i * LANES : (i + 1) * LANES] = jnp.where(
            low, pltpu.roll(even, HDIM, 1), odd
        ).astype(BF16)


def expert_kernel(blocks, slot_rows, local_experts, place_ref, router_ref, gate_ref, up_ref, down_ref, *refs):
    sources = 2 * blocks - 1
    normed_in, cot_in, info_in = (refs[i * sources : (i + 1) * sources] for i in range(3))
    refs = refs[3 * sources :]
    xs_ref, cs_ref, hs_ref, gate_grad_ref, up_grad_ref, hit_ref = refs[:6]
    grad_out = refs[6 : 6 + sources]
    router_grad_ref = refs[6 + sources]
    x_all, c_all, info, gates, back, grad_acc, grad_low, sems, out_sem = refs[7 + sources :]
    step = pl.program_id(0)
    rows = x_all.shape[1]
    expert_pad = router_ref.shape[0]
    first_expert = place_ref[0]
    mine = pl.ds(first_expert + step, 1)

    def source_copies(i, s):
        return (
            pltpu.make_async_copy(normed_in[s], x_all.at[i], sems.at[0, i]),
            pltpu.make_async_copy(cot_in[s], c_all.at[i], sems.at[1, i]),
            pltpu.make_async_copy(info_in[s], info.at[i], sems.at[2, i]),
        )

    @pl.when(step == 0)
    def _():
        for i in range(blocks):
            for s in range(sources):

                @pl.when(place_ref[1 + i] == s)
                def _(i=i, s=s):
                    for copy in source_copies(i, s):
                        copy.start()

        for i in range(blocks):
            for copy in source_copies(i, 0):
                copy.wait()
        for i in range(blocks):
            logits = dot(router_ref[...], x_all[i], NT)
            logits = jnp.where(info[i, :expert_pad, :] >= 0, logits, MASKED_SCORE)
            weights = jnp.exp(logits - jnp.max(logits, axis=0, keepdims=True))
            gates[i] = weights / jnp.sum(weights, axis=0, keepdims=True)
        back[...] = jnp.zeros_like(back)
        grad_acc[...] = jnp.zeros_like(grad_acc)

    slot_ids = lax.broadcasted_iota(jnp.int32, (slot_rows, rows), 0)
    gate_slots = []
    for i in range(blocks):
        hit = slot_ids == info[i, mine, :]
        part = slice(i * slot_rows, (i + 1) * slot_rows)
        gate_slots.append(
            jnp.sum(jnp.where(hit, gates[i, mine, :], 0.0), axis=-1, keepdims=True)
        )
        hit = jnp.where(hit, 1.0, 0.0).astype(BF16)
        hit_ref[0, part, :] = hit
        xs_ref[0, part, :] = dot(hit, x_all[i]).astype(BF16)
        cs_ref[0, part, :] = dot(hit, c_all[i]).astype(BF16)
    gate_slot = jnp.concatenate(gate_slots, axis=0) * RESIDUAL_SCALE
    gate_pre = dot(xs_ref[0], gate_ref[0])
    up_pre = dot(xs_ref[0], up_ref[0])
    raw_grad = dot(cs_ref[0], down_ref[0])
    sigmoid = 1.0 / (1.0 + jnp.exp(-gate_pre))
    active = gate_pre * sigmoid
    expert_hidden = (active * up_pre).astype(BF16).astype(F32)
    hs_ref[0] = (expert_hidden * gate_slot).astype(BF16)
    back_slot = jnp.sum(expert_hidden * raw_grad, axis=-1, keepdims=True) * RESIDUAL_SCALE
    hidden_grad = raw_grad * gate_slot
    gate_grad_ref[0] = (hidden_grad * up_pre * sigmoid * (1.0 + gate_pre * (1.0 - sigmoid))).astype(BF16)
    up_grad_ref[0] = (hidden_grad * active).astype(BF16)
    slot_grad = (
        dot(gate_grad_ref[0], gate_ref[0], NT) + dot(up_grad_ref[0], up_ref[0], NT)
    ).astype(BF16)
    for i in range(blocks):
        part = slice(i * slot_rows, (i + 1) * slot_rows)
        hit = hit_ref[0, part, :]
        back_row = jnp.sum(hit.astype(F32) * back_slot[part], axis=0, keepdims=True)
        back[i, mine, :] = back_row * gates[i, mine, :]
        grad_acc[i] += dot(hit, slot_grad[part], TN)

    @pl.when(step == local_experts - 1)
    def _():
        router_sum = None
        for i in range(blocks):
            share = back[i]
            logit_grad = (share - gates[i] * jnp.sum(share, axis=0, keepdims=True)).astype(BF16)
            grad_low[i] = (grad_acc[i] + dot(logit_grad, router_ref[...], TN)).astype(BF16)
            part = dot(logit_grad, x_all[i])
            router_sum = part if router_sum is None else router_sum + part
        router_grad_ref[...] = router_sum
        for i in range(blocks):
            for s in range(sources):

                @pl.when(place_ref[1 + i] == s)
                def _(i=i, s=s):
                    pltpu.make_async_copy(grad_low.at[i], grad_out[s], out_sem.at[i]).start()

        for i in range(blocks):
            pltpu.make_async_copy(grad_low.at[i], grad_out[0], out_sem.at[i]).wait()


def run_experts(place, router_t, gate_weight, up_weight, down_weight, normed, cots, infos, slot_rows):
    local_experts, width, hidden = gate_weight.shape
    sources = len(normed)
    blocks = (sources + 1) // 2
    rows = normed[0].shape[0]
    expert_pad = router_t.shape[0]
    slots = blocks * slot_rows
    anywhere = pl.BlockSpec(memory_space=pl.ANY)
    weight_spec = pl.BlockSpec((1, width, hidden), lambda e, place: (e, 0, 0))

    def slot_spec(columns):
        return pl.BlockSpec((1, slots, columns), lambda e, place: (e, 0, 0))

    def slot_shape(columns):
        return jax.ShapeDtypeStruct((local_experts, slots, columns), BF16)

    out = pl.pallas_call(
        functools.partial(expert_kernel, blocks, slot_rows, local_experts),
        out_shape=(
            slot_shape(width),
            slot_shape(width),
            slot_shape(hidden),
            slot_shape(hidden),
            slot_shape(hidden),
            slot_shape(rows),
        )
        + (jax.ShapeDtypeStruct((rows, width), BF16),) * sources
        + (jax.ShapeDtypeStruct((expert_pad, width), F32),),
        grid_spec=pltpu.PrefetchScalarGridSpec(
            num_scalar_prefetch=1,
            grid=(local_experts,),
            in_specs=[pl.BlockSpec((expert_pad, width), lambda e, place: (0, 0))]
            + [weight_spec] * 3
            + [anywhere] * (3 * sources),
            out_specs=(
                slot_spec(width),
                slot_spec(width),
                slot_spec(hidden),
                slot_spec(hidden),
                slot_spec(hidden),
                slot_spec(rows),
            )
            + (anywhere,) * sources
            + (pl.BlockSpec((expert_pad, width), lambda e, place: (0, 0)),),
            scratch_shapes=[
                pltpu.VMEM((blocks, rows, width), BF16),
                pltpu.VMEM((blocks, rows, width), BF16),
                pltpu.VMEM((blocks,) + infos[0].shape, jnp.int32),
                pltpu.VMEM((blocks, expert_pad, rows), F32),
                pltpu.VMEM((blocks, expert_pad, rows), F32),
                pltpu.VMEM((blocks, rows, width), F32),
                pltpu.VMEM((blocks, rows, width), BF16),
                pltpu.SemaphoreType.DMA((3, blocks)),
                pltpu.SemaphoreType.DMA((blocks,)),
            ],
        ),
        compiler_params=params(),
        name="experts",
    )(place, router_t, gate_weight, up_weight, down_weight, *normed, *cots, *infos)
    return out[:6], out[6 : 6 + sources], out[6 + sources]


def expert_grad_kernel(blocks, slot_rows, local_experts, owners, chunk, place_ref, down_ref, xs_ref, cs_ref, hs_ref, gate_grad_ref, up_grad_ref, hit_ref, *refs):
    keep_refs, send_refs = refs[:3], refs[3:6]
    sources = 2 * blocks - 1
    mix_out = refs[6 : 6 + sources]
    mix_acc, mix_low, out_sem = refs[6 + sources :]
    step = pl.program_id(0)
    width = xs_ref.shape[2]
    owned = width // owners
    mine = place_ref[0]
    my_pair, my_bit = mine // 2, mine % 2

    @pl.when(step == 0)
    def _():
        mix_acc[...] = jnp.zeros_like(mix_acc)

    slot_out = dot(hs_ref[0], down_ref[0], NT).astype(BF16)
    for i in range(blocks):
        part = slice(i * slot_rows, (i + 1) * slot_rows)
        mix_acc[i] += dot(hit_ref[0, part, :], slot_out[part], TN)

    pairs = ((xs_ref, gate_grad_ref), (xs_ref, up_grad_ref), (cs_ref, hs_ref))
    for w, (left_ref, right_ref) in enumerate(pairs):
        for c in range(width // chunk):
            grad = dot(left_ref[0, :, c * chunk : (c + 1) * chunk], right_ref[0], TN).astype(BF16)
            for o in range(chunk // owned):
                owner = c * (chunk // owned) + o
                piece = grad[o * owned : (o + 1) * owned]
                spot = (owner // 2) ^ my_pair

                @pl.when(my_bit == owner % 2)
                def _(w=w, spot=spot, piece=piece):
                    keep_refs[w][0, spot] = piece

                @pl.when(my_bit != owner % 2)
                def _(w=w, spot=spot, piece=piece):
                    send_refs[w][0, spot] = piece

    @pl.when(step == local_experts - 1)
    def _():
        for i in range(blocks):
            mix_low[i] = mix_acc[i].astype(BF16)
        for i in range(blocks):
            for s in range(sources):

                @pl.when(place_ref[1 + i] == s)
                def _(i=i, s=s):
                    pltpu.make_async_copy(mix_low.at[i], mix_out[s], out_sem.at[i]).start()

        for i in range(blocks):
            pltpu.make_async_copy(mix_low.at[i], mix_out[0], out_sem.at[i]).wait()


def run_expert_grads(place, down_weight, saved, rows, slot_rows, owners):
    local_experts, width, hidden = down_weight.shape
    slots = saved[0].shape[1]
    blocks = slots // slot_rows
    sources = 2 * blocks - 1
    owned = width // owners
    chunk = int(np.lcm(2 * owned, LANES))
    anywhere = pl.BlockSpec(memory_space=pl.ANY)

    def slot_spec(columns):
        return pl.BlockSpec((1, slots, columns), lambda e, place: (e, 0, 0))

    half_shape = jax.ShapeDtypeStruct((local_experts, owners // 2, owned, hidden), BF16)
    half_spec = pl.BlockSpec((1, owners // 2, owned, hidden), lambda e, place: (e, 0, 0, 0))
    out = pl.pallas_call(
        functools.partial(expert_grad_kernel, blocks, slot_rows, local_experts, owners, chunk),
        out_shape=(half_shape,) * 6 + (jax.ShapeDtypeStruct((rows, width), BF16),) * sources,
        grid_spec=pltpu.PrefetchScalarGridSpec(
            num_scalar_prefetch=1,
            grid=(local_experts,),
            in_specs=[
                pl.BlockSpec((1, width, hidden), lambda e, place: (e, 0, 0)),
                slot_spec(width),
                slot_spec(width),
                slot_spec(hidden),
                slot_spec(hidden),
                slot_spec(hidden),
                slot_spec(rows),
            ],
            out_specs=(half_spec,) * 6 + (anywhere,) * sources,
            scratch_shapes=[
                pltpu.VMEM((blocks, rows, width), F32),
                pltpu.VMEM((blocks, rows, width), BF16),
                pltpu.SemaphoreType.DMA((blocks,)),
            ],
        ),
        compiler_params=params(),
        name="expert_grads",
    )(place, down_weight, *saved)
    return out[:3], out[3:6], out[6:]


def line_up(value, size):
    return lax.ppermute(value, "expert", [(i, i + 1) for i in range(size - 1)])


def line_down(value, size):
    return lax.ppermute(value, "expert", [(i + 1, i) for i in range(size - 1)])


def line_gather(value, size):
    below, above = [], []
    up, down = value, value
    for _ in range(size - 1):
        up = line_up(up, size)
        down = line_down(down, size)
        below.append(up)
        above.append(down)
    return [value] + below + above


def add_low(*terms):
    total = terms[0].astype(F32)
    for term in terms[1:]:
        total = total + term.astype(F32)
    return total.astype(BF16)


def line_reduce(parts, size):
    down = parts[size - 1]
    up = parts[2 * size - 2]
    for k in range(1, size):
        from_above = line_down(down, size)
        from_below = line_up(up, size)
        if k < size - 1:
            down = add_low(from_above, parts[size - 1 - k])
            up = add_low(from_below, parts[2 * size - 2 - k])
    return parts[0].astype(F32) + from_above.astype(F32) + from_below.astype(F32)


def flip(value, bit, size):
    return lax.ppermute(value, "dp", [(i, i ^ bit) for i in range(size)])


def halve_rows(value, order, dp_size, dp_place):
    left = list(range(dp_size.bit_length() - 2, -1, -1))
    for bit in order:
        axis = left.index(bit)
        own = (dp_place >> bit) & 1
        keep = lax.dynamic_index_in_dim(value, own, axis, keepdims=False)
        send = lax.dynamic_index_in_dim(value, 1 - own, axis, keepdims=False)
        value = add_low(keep, flip(send, 1 << bit, dp_size))
        left.pop(axis)
    return value


def reduce_dense(partial, dp_size, dp_place, size, place):
    depth, columns = partial.shape
    bits = dp_size.bit_length() - 1
    rows = depth // (dp_size * size)
    cube = partial.astype(BF16).reshape((2,) * bits + (size, rows, columns))
    half = columns // 2 // LANES * LANES
    outs = []
    rest = list(range(1, bits))
    for part, order in ((cube[..., :half], rest), (cube[..., half:], rest[::-1])):
        block = halve_rows(part, [0] + order, dp_size, dp_place)

        def pick(index, block=block):
            return lax.dynamic_index_in_dim(block, jnp.clip(index, 0, size - 1), 0, keepdims=False)

        down, up = pick(1 + place - size), pick(place + size - 1)
        for k in range(1, size):
            from_above = line_down(down, size)
            from_below = line_up(up, size)
            if k < size - 1:
                down = add_low(from_above, pick(k + 1 + place - size))
                up = add_low(from_below, pick(place + size - k - 1))
        outs.append(pick(place).astype(F32) + from_above.astype(F32) + from_below.astype(F32))
    return jnp.concatenate(outs, axis=-1)


def reduce_experts(keep, send, dp_size):
    bits = dp_size.bit_length() - 1
    local_experts, _, rows, hidden = keep.shape
    received = flip(send, 1, dp_size)
    cube = (local_experts,) + (2,) * (bits - 1) + (rows, hidden)
    keep, received = keep.reshape(cube), received.reshape(cube)
    half = rows // 2
    outs = []
    rest = list(range(1, bits))
    for lo, hi, order in ((0, half, rest), (half, rows, rest[::-1])):
        value = (keep[..., lo:hi, :], received[..., lo:hi, :])
        left = list(range(bits - 1, 0, -1))
        for bit in order:
            axis = 1 + left.index(bit)
            send_part = add_low(*(lax.index_in_dim(v, 1, axis, keepdims=False) for v in value))
            keep_parts = tuple(lax.index_in_dim(v, 0, axis, keepdims=False) for v in value)
            value = (add_low(*keep_parts), flip(send_part, 1 << bit, dp_size))
            left.pop(axis - 1)
        outs.append(value[0].astype(F32) + value[1].astype(F32))
    return jnp.concatenate(outs, axis=1)


def reduce_top(top, dp_size, size):
    for bit in range(dp_size.bit_length() - 1):
        top = jnp.maximum(top, flip(top, 1 << bit, dp_size))
    place = lax.axis_index("expert")
    up, down = top, top
    for k in range(1, size):
        up = line_up(up, size)
        down = line_down(down, size)
        top = jnp.maximum(top, jnp.where(place >= k, up, top))
        top = jnp.maximum(top, jnp.where(place + k < size, down, top))
    return top


def arrival_order(size):
    table = np.zeros((size, size), np.int32)
    for place in range(size):
        spots = [0]
        for k in range(1, size):
            if place - k >= 0:
                spots.append(k)
            if place + k < size:
                spots.append(size - 1 + k)
        table[place] = spots
    return table


def norm_backward(hidden, factor, gain_vec, grad_in):
    scaled = grad_in * gain_vec
    hidden_grad = factor * scaled - hidden * factor**3 * jnp.mean(
        scaled * hidden, axis=-1, keepdims=True
    )
    return hidden_grad, jnp.sum(grad_in * hidden * factor, axis=0)


def local(
    tokens,
    first_gain,
    query_weight,
    key_weight,
    value_weight,
    output_weight,
    second_gain,
    router_weight,
    gate_weight,
    up_weight,
    down_weight,
    cotangent,
    routes,
    segments,
    threshold,
):
    rows, width = tokens.shape
    query_width, kv_width = query_weight.shape[1], key_weight.shape[1]
    heads, groups = query_width // HDIM, kv_width // HDIM
    ratio = heads // groups
    local_experts = gate_weight.shape[0]
    size, dp_size = lax.axis_size("expert"), lax.axis_size("dp")
    place, dp_place = lax.axis_index("expert"), lax.axis_index("dp")
    experts = local_experts * size
    expert_pad = round_up(experts, 16)
    capacity = rows * routes.shape[1] * 9 // (experts * 8)
    slot_rows = round_up(capacity, 64)

    positions = (place * rows + jnp.arange(rows, dtype=jnp.int32)).astype(F32)
    half = HDIM // 2
    inverse = ROTARY_BASE ** (-2.0 * jnp.arange(half, dtype=F32) / HDIM)
    angles = positions[:, None] * jnp.tile(inverse, LANES // half)[None, :]
    sign = jnp.where(jnp.arange(LANES) % HDIM < half, -1.0, 1.0).astype(F32)
    tables = (jnp.cos(angles), jnp.sin(angles) * sign[None, :])

    info = pl.pallas_call(
        functools.partial(info_kernel, expert_pad),
        out_shape=jax.ShapeDtypeStruct((expert_pad + 8, rows), jnp.int32),
        in_specs=[vmem()] * 2,
        out_specs=vmem(),
        compiler_params=params(),
        name="info",
    )(routes, segments.reshape(1, rows))
    infos = line_gather(info, size)

    normed, first_factor, kv_own = pl.pallas_call(
        front_kernel,
        out_shape=(
            jax.ShapeDtypeStruct((rows, width), BF16),
            jax.ShapeDtypeStruct((rows, 1), F32),
            jax.ShapeDtypeStruct((groups, rows, LANES), BF16),
        ),
        in_specs=[vmem()] * 6,
        out_specs=(vmem(),) * 3,
        compiler_params=params(),
        name="front",
    )(tokens, first_gain.reshape(1, width), key_weight, value_weight, *tables)
    kv_slots = [kv_own]
    for _ in range(size - 1):
        kv_slots.append(line_up(kv_slots[-1], size))
    cots = line_gather(cotangent, size)

    query_block = 512
    queries = pl.pallas_call(
        query_kernel,
        out_shape=jax.ShapeDtypeStruct((rows, query_width), BF16),
        grid=(query_width // query_block,),
        in_specs=[
            pl.BlockSpec((rows, width), lambda s: (0, 0)),
            pl.BlockSpec((width, query_block), lambda s: (0, s)),
            pl.BlockSpec((rows, LANES), lambda s: (0, 0)),
            pl.BlockSpec((rows, LANES), lambda s: (0, 0)),
        ],
        out_specs=pl.BlockSpec((rows, query_block), lambda s: (0, s)),
        compiler_params=params(),
        name="queries",
    )(normed, query_weight, *tables)

    seg_rows = jnp.concatenate([infos[k][expert_pad : expert_pad + 1] for k in range(size)], axis=0)
    reach = jnp.arange(size, dtype=jnp.int32)
    wanted = (reach <= place) & (seg_rows[:, -1] >= segments[0])
    need = jnp.sum(wanted.astype(jnp.int32)).reshape(1)
    seg_rows = jnp.where((reach <= place)[:, None], seg_rows, -1)
    seg_column = segments.reshape(rows, 1)

    attended, lse, top = attend(queries, kv_slots, seg_column, seg_rows, need, ratio)
    head_top = reduce_top(top[:, 0, : 2 * ratio].reshape(1, heads), dp_size, size).reshape(heads)

    hidden_in = tokens.astype(F32)
    hidden_mid = hidden_in + RESIDUAL_SCALE * dot(attended, output_weight, NT)
    second_factor = lax.rsqrt(jnp.mean(hidden_mid * hidden_mid, axis=-1, keepdims=True) + NORM_EPSILON)
    second_normed = (hidden_mid * second_factor * second_gain).astype(BF16)
    normed_blocks = line_gather(second_normed, size)

    router_t = jnp.pad(router_weight.T, ((0, expert_pad - experts), (0, 0)))
    order = lax.dynamic_index_in_dim(jnp.asarray(arrival_order(size)), place, 0, keepdims=False)
    expert_place = jnp.concatenate([(place * local_experts).reshape(1), order]).astype(jnp.int32)
    saved, grad_blocks, router_part = run_experts(
        expert_place, router_t, gate_weight, up_weight, down_weight, normed_blocks, cots, infos, slot_rows
    )
    normed_grad = line_reduce(grad_blocks, size)

    grad_place = jnp.concatenate([dp_place.reshape(1), order]).astype(jnp.int32)
    keep, send, mix_blocks = run_expert_grads(grad_place, down_weight, saved, rows, slot_rows, dp_size)
    expert_sums = [reduce_experts(k, s, dp_size) for k, s in zip(keep, send)]
    block_out = (hidden_mid + line_reduce(mix_blocks, size)).astype(BF16)

    out_grad = cotangent.astype(F32)
    mid_back, second_gain_part = norm_backward(hidden_mid, second_factor, second_gain, normed_grad)
    mid_grad = out_grad + mid_back
    branch_grad = (RESIDUAL_SCALE * mid_grad).astype(BF16)
    attended_grad = dot(branch_grad, output_weight).astype(BF16)
    projection_part = dot(branch_grad, attended, TN)
    projection_grad = reduce_dense(projection_part, dp_size, dp_place, size, place)

    query_back, dkv = attend_back(
        queries, attended, attended_grad, lse, tables, kv_slots, seg_column, seg_rows, need, ratio
    )
    down = dkv[size - 1]
    for k in range(1, size):
        from_above = line_down(down, size)
        if k < size - 1:
            down = add_low(from_above, dkv[size - 1 - k])
    dkv_sum = dkv[0].astype(F32) + from_above.astype(F32)
    key_back, value_back = pl.pallas_call(
        unpack_kernel,
        out_shape=(jax.ShapeDtypeStruct((rows, kv_width), BF16),) * 2,
        in_specs=[vmem()] * 3,
        out_specs=(vmem(),) * 2,
        compiler_params=params(),
        name="unpack",
    )(dkv_sum, *tables)

    first_grad = dot(query_back, query_weight, NT)
    first_grad = first_grad + dot(key_back, key_weight, NT)
    first_grad = first_grad + dot(value_back, value_weight, NT)
    input_back, first_gain_part = norm_backward(hidden_in, first_factor, first_gain, first_grad)
    input_grad = mid_grad + input_back
    small = jnp.concatenate(
        [router_part[:experts], second_gain_part[None], first_gain_part[None]], axis=0
    )
    small = jnp.pad(small, ((0, LANES - small.shape[0]), (0, 0))).T
    query_grad = reduce_dense(dot(normed, query_back, TN), dp_size, dp_place, size, place)
    rest_grad = reduce_dense(
        jnp.concatenate(
            [dot(normed, key_back, TN).astype(BF16), dot(normed, value_back, TN).astype(BF16), small.astype(BF16)],
            axis=1,
        ),
        dp_size,
        dp_place,
        size,
        place,
    )
    key_grad = rest_grad[:, :kv_width]
    value_grad = rest_grad[:, kv_width : 2 * kv_width]
    small_grad = rest_grad[:, 2 * kv_width :]

    head_scale = threshold / jnp.maximum(head_top, threshold)
    group_scale = jnp.min(head_scale.reshape(groups, ratio), axis=1)
    row_count = width // (dp_size * size)
    row_start = (dp_place * size + place) * row_count
    query_rows = lax.dynamic_slice_in_dim(query_weight, row_start, row_count, 0).astype(F32)
    key_rows = lax.dynamic_slice_in_dim(key_weight, row_start, row_count, 0).astype(F32)
    query_clipped = (query_rows * jnp.repeat(jnp.sqrt(head_scale), HDIM)[None, :]).astype(BF16)
    key_clipped = (key_rows * jnp.repeat(jnp.sqrt(group_scale), HDIM)[None, :]).astype(BF16)
    return (
        block_out,
        input_grad,
        small_grad[:, experts + 1],
        query_grad,
        key_grad,
        value_grad,
        projection_grad,
        small_grad[:, experts],
        small_grad[:, :experts],
        expert_sums[0],
        expert_sums[1],
        expert_sums[2],
        head_scale,
        query_clipped,
        key_clipped,
    )


def solution(mesh):
    row = P(("dp", "expert"), None)
    vector = P(("dp", "expert"))
    expert_in = P("expert", None, None)
    expert_out = P("expert", "dp", None)
    return jax.shard_map(
        local,
        mesh=mesh,
        in_specs=(row,) + (P(),) * 7 + (expert_in,) * 3 + (row, row, vector, P()),
        out_specs=(row, row, vector)
        + (row,) * 4
        + (vector, row)
        + (expert_out,) * 3
        + (P(), row, row),
        check_vma=False,
    )
```

```python
import functools

import jax
import jax.numpy as jnp
import numpy as np
from jax import lax
from jax.experimental import pallas as pl
from jax.experimental.pallas import tpu as pltpu
from jax.sharding import PartitionSpec as P

HDIM = 64
LANES = 128
ATTENTION_SCALE = 0.015625
RESIDUAL_SCALE = 0.22
NORM_EPSILON = 1e-06
ROTARY_BASE = 10000.0
MASKED_SCORE = -1e30
BF16 = jnp.bfloat16
F32 = jnp.float32
NN = (((1,), (0,)), ((), ()))
NT = (((1,), (1,)), ((), ()))
TN = (((0,), (0,)), ((), ()))
VMEM_LIMIT = 56 * 1024 * 1024


def dot(left, right, dims=NN):
    return lax.dot_general(left, right, dims, preferred_element_type=F32)


def round_up(count, unit):
    return (count + unit - 1) // unit * unit


def low_lanes(rows):
    return lax.broadcasted_iota(jnp.int32, (rows, LANES), 1) < HDIM


def partner_lanes(slab):
    lane = lax.broadcasted_iota(jnp.int32, slab.shape, 1) % HDIM
    half = HDIM // 2
    return jnp.where(lane < half, pltpu.roll(slab, LANES - half, 1), pltpu.roll(slab, half, 1))


def vmem():
    return pl.BlockSpec(memory_space=pltpu.VMEM)


def params(**more):
    return pltpu.CompilerParams(vmem_limit_bytes=VMEM_LIMIT, **more)


def cost(microseconds):
    return pl.CostEstimate(flops=int(microseconds * 1e6), bytes_accessed=0, transcendentals=0)


def rotary_tables(length):
    half = HDIM // 2
    inverse = np.float32(ROTARY_BASE) ** (np.float32(-2.0) * np.arange(half, dtype=np.float32) / np.float32(HDIM))
    angles = np.arange(length, dtype=np.float32)[:, None] * np.tile(inverse, LANES // half)[None, :]
    angles = angles.astype(np.float32).astype(np.float64)
    sign = np.where(np.arange(LANES) % HDIM < half, -1.0, 1.0)
    return np.cos(angles).astype(np.float32), (np.sin(angles) * sign).astype(np.float32)


def extend_kernel(cotangent_ref, routes_ref, out_ref):
    rows, top_count = routes_ref.shape
    width = cotangent_ref.shape[1]
    lane = lax.broadcasted_iota(jnp.int32, (rows, LANES), 1)
    chosen = jnp.zeros((rows, LANES), F32)
    for k in range(top_count):
        chosen = chosen + jnp.where(routes_ref[:, k : k + 1] == lane, 1.0, 0.0)
    first = lax.broadcasted_iota(jnp.int32, (rows, rows), 0)
    second = lax.broadcasted_iota(jnp.int32, (rows, rows), 1)
    earlier = jnp.where(second < first, 1.0, 0.0).astype(BF16)
    rank = dot(earlier, chosen.astype(BF16))
    out_ref[:, :width] = cotangent_ref[...]
    out_ref[:, width:] = jnp.where(chosen > 0.5, rank, -1.0).astype(BF16)


def front_kernel(tokens_ref, gain_ref, key_ref, value_ref, cos_ref, sin_ref, segments_ref, normed_ref, factor_ref, kv_ref):
    hidden = tokens_ref[...].astype(F32)
    factor = lax.rsqrt(jnp.mean(hidden * hidden, axis=-1, keepdims=True) + NORM_EPSILON)
    normed = (hidden * factor * gain_ref[...]).astype(BF16)
    normed_ref[...] = normed
    factor_ref[...] = factor
    keys = dot(normed, key_ref[...])
    values = dot(normed, value_ref[...])
    cosine, sine = cos_ref[...], sin_ref[...]
    rows = hidden.shape[0]
    low = low_lanes(rows)
    for i in range(keys.shape[1] // LANES):
        slab = keys[:, i * LANES : (i + 1) * LANES]
        slab = slab * cosine + partner_lanes(slab) * sine
        value_slab = values[:, i * LANES : (i + 1) * LANES]
        even, odd = 2 * i * rows, (2 * i + 1) * rows
        kv_ref[even : even + rows, :] = jnp.where(low, slab, pltpu.roll(value_slab, HDIM, 1)).astype(BF16)
        kv_ref[odd : odd + rows, :] = jnp.where(low, pltpu.roll(slab, HDIM, 1), value_slab).astype(BF16)
    kv_ref[keys.shape[1] // HDIM * rows :, :] = segments_ref[...]


def query_kernel(normed_ref, query_ref, cos_ref, sin_ref, out_ref):
    raw = dot(normed_ref[...], query_ref[...])
    cosine, sine = cos_ref[...], sin_ref[...]
    for i in range(raw.shape[1] // LANES):
        slab = raw[:, i * LANES : (i + 1) * LANES]
        slab = slab * cosine + partner_lanes(slab) * sine
        out_ref[:, i * LANES : (i + 1) * LANES] = (slab.astype(BF16).astype(F32) * ATTENTION_SCALE).astype(BF16)


def fill_bias(bias_ref, need_ref, place_ref, seg_column, seg_refs):
    slots, rows, keys = bias_ref.shape
    for k in range(slots):
        for j in range(keys // LANES):
            lanes = slice(j * LANES, (j + 1) * LANES)
            allowed = seg_column == seg_refs[k][j : j + 1, :].astype(F32)
            if k == 0:
                allowed = allowed & (
                    lax.broadcasted_iota(jnp.int32, (rows, LANES), 1) + j * LANES
                    <= lax.broadcasted_iota(jnp.int32, (rows, LANES), 0)
                )
            bias_ref[k, :, lanes] = jnp.where(allowed, 0.0, MASKED_SCORE)
    first = jnp.min(seg_column)
    need = jnp.int32(1)
    for k in range(1, slots):
        last = jnp.max(seg_refs[k][: keys // LANES, :].astype(F32))
        need = jnp.where((last >= first) & (k <= place_ref[0]), k + 1, need)
    need_ref[0] = need


def head_slab(block, head, upper):
    slab = block[:, (head // 2) * LANES : (head // 2 + 1) * LANES].astype(F32)
    low = low_lanes(slab.shape[0])
    if (head % 2 == 1) != upper:
        slab = pltpu.roll(slab, HDIM, 1)
    return jnp.where(low != upper, slab, 0.0)


def attend_kernel(slots, ratio, place_ref, query_ref, seg_column_ref, *refs):
    kv_refs, seg_refs = refs[:slots], refs[slots : 2 * slots]
    attended_ref, lse_ref, top_ref, bias_ref, stacked_ref, acc_ref, max_ref, sum_ref, need_ref = refs[2 * slots :]
    rows = query_ref.shape[0]
    low = low_lanes(rows)
    lane = lax.broadcasted_iota(jnp.int32, (rows, LANES), 1)

    @pl.when(pl.program_id(0) == 0)
    def _():
        fill_bias(bias_ref, need_ref, place_ref, seg_column_ref[...], seg_refs)

    need = need_ref[0]

    outs = []
    lse_all = jnp.zeros((rows, LANES), F32)
    top_all = jnp.zeros((8, LANES), F32)
    for group in range(2):
        for r in range(ratio):
            stacked_ref[r * rows : (r + 1) * rows, :] = head_slab(
                query_ref, group * ratio + r, False
            ).astype(BF16)
        for k in range(slots):

            def step(k=k):
                kv = kv_refs[k][group * rows : (group + 1) * rows, :]
                scores = dot(stacked_ref[...], kv, NT).reshape(ratio, rows, rows)
                scores = (scores + bias_ref[k][None]).reshape(ratio * rows, rows)
                top = jnp.max(scores, axis=-1, keepdims=True)
                if k == 0:
                    weights = jnp.exp(scores - top)
                    max_ref[...] = top
                    sum_ref[...] = jnp.sum(weights, axis=-1, keepdims=True)
                    acc_ref[...] = dot(weights.astype(BF16), kv)
                else:
                    before = max_ref[...]
                    top = jnp.maximum(top, before)
                    shrink = jnp.exp(before - top)
                    weights = jnp.exp(scores - top)
                    max_ref[...] = top
                    sum_ref[...] = sum_ref[...] * shrink + jnp.sum(weights, axis=-1, keepdims=True)
                    acc_ref[...] = acc_ref[...] * shrink + dot(weights.astype(BF16), kv)

            if k == 0:
                step()
            else:
                pl.when(k < need)(step)
        total = sum_ref[...]
        mixed = acc_ref[...] / total
        lse = max_ref[...] + jnp.log(total)
        for r in range(ratio):
            head = group * ratio + r
            outs.append(mixed[r * rows : (r + 1) * rows])
            lse_all = jnp.where(lane == head, lse[r * rows : (r + 1) * rows], lse_all)
            peak = jnp.max(max_ref[r * rows : (r + 1) * rows, :], axis=0, keepdims=True)
            top_all = jnp.where(lane[:8] == head, peak, top_all)
    for i in range(len(outs) // 2):
        attended_ref[:, i * LANES : (i + 1) * LANES] = jnp.where(
            low, pltpu.roll(outs[2 * i], HDIM, 1), outs[2 * i + 1]
        ).astype(BF16)
    lse_ref[0] = lse_all
    top_ref[0] = top_all


def kv_specs(slots, groups, rows):
    return [pl.BlockSpec((2 * rows, LANES), lambda s: (s, 0))] * slots + [
        pl.BlockSpec((16, LANES), lambda s: (groups * rows // 16, 0))
    ] * slots


def attend(queries, kv_slots, seg_column, place, groups):
    slots = len(kv_slots)
    rows, width = queries.shape
    ratio = width // HDIM // groups
    steps = groups // 2
    block = 2 * ratio * HDIM
    return pl.pallas_call(
        functools.partial(attend_kernel, slots, ratio),
        out_shape=(
            jax.ShapeDtypeStruct((rows, width), BF16),
            jax.ShapeDtypeStruct((steps, rows, LANES), F32),
            jax.ShapeDtypeStruct((steps, 8, LANES), F32),
        ),
        grid=(steps,),
        in_specs=[
            pl.BlockSpec(memory_space=pltpu.SMEM),
            pl.BlockSpec((rows, block), lambda s: (0, s)),
            pl.BlockSpec((rows, 1), lambda s: (0, 0)),
        ]
        + kv_specs(slots, groups, rows),
        out_specs=(
            pl.BlockSpec((rows, block), lambda s: (0, s)),
            pl.BlockSpec((1, rows, LANES), lambda s: (s, 0, 0)),
            pl.BlockSpec((1, 8, LANES), lambda s: (s, 0, 0)),
        ),
        scratch_shapes=[
            pltpu.VMEM((slots, rows, rows), F32),
            pltpu.VMEM((ratio * rows, LANES), BF16),
            pltpu.VMEM((ratio * rows, LANES), F32),
            pltpu.VMEM((ratio * rows, 1), F32),
            pltpu.VMEM((ratio * rows, 1), F32),
            pltpu.SMEM((1,), jnp.int32),
        ],
        compiler_params=params(),
        cost_estimate=cost(20),
        name="attend",
    )(place, queries, seg_column, *kv_slots, *kv_slots)


def attend_back_kernel(slots, ratio, place_ref, query_ref, attended_ref, grad_ref, lse_ref, cos_ref, sin_ref, seg_column_ref, *refs):
    kv_refs, seg_refs = refs[:slots], refs[slots : 2 * slots]
    refs = refs[2 * slots :]
    back_ref, dkv_refs = refs[0], refs[1 : slots + 1]
    bias_ref, query_s, grad_s, acc_ref, lse_s, delta_s, need_ref = refs[slots + 1 :]
    rows = query_ref.shape[0]
    low = low_lanes(rows)

    @pl.when(pl.program_id(0) == 0)
    def _():
        fill_bias(bias_ref, need_ref, place_ref, seg_column_ref[...], seg_refs)

    need = need_ref[0]

    outs = []
    for group in range(2):
        for r in range(ratio):
            head = group * ratio + r
            part = slice(r * rows, (r + 1) * rows)
            query_s[part, :] = head_slab(query_ref, head, False).astype(BF16)
            grad = head_slab(grad_ref, head, True)
            grad_s[part, :] = grad.astype(BF16)
            delta_s[part, :] = jnp.sum(grad * head_slab(attended_ref, head, True), axis=-1, keepdims=True)
            lse_s[part, :] = lse_ref[0, :, head : head + 1]
        for k in range(slots):

            def step(k=k):
                kv = kv_refs[k][group * rows : (group + 1) * rows, :]
                scores = dot(query_s[...], kv, NT).reshape(ratio, rows, rows)
                scores = (scores + bias_ref[k][None]).reshape(ratio * rows, rows)
                weights = jnp.exp(scores - lse_s[...])
                weight_grad = dot(grad_s[...], kv, NT)
                score_grad = (weights * (weight_grad - delta_s[...])).astype(BF16)
                query_part = dot(score_grad, kv)
                if k == 0:
                    acc_ref[...] = query_part
                else:
                    acc_ref[...] += query_part
                dkv_refs[k][group * rows : (group + 1) * rows, :] = (
                    dot(score_grad, query_s[...], TN) + dot(weights.astype(BF16), grad_s[...], TN)
                ).astype(BF16)

            if k == 0:
                step()
            else:
                pl.when(k < need)(step)

                @pl.when(k >= need)
                def _(k=k):
                    dkv_refs[k][group * rows : (group + 1) * rows, :] = jnp.zeros((rows, LANES), BF16)

        for r in range(ratio):
            outs.append(acc_ref[r * rows : (r + 1) * rows, :] * ATTENTION_SCALE)
    cosine, sine = cos_ref[...], sin_ref[...]
    for i in range(len(outs) // 2):
        slab = jnp.where(low, outs[2 * i], pltpu.roll(outs[2 * i + 1], HDIM, 1))
        slab = slab * cosine - partner_lanes(slab) * sine
        back_ref[:, i * LANES : (i + 1) * LANES] = slab.astype(BF16)


def attend_back(queries, attended, grad, lse, tables, kv_slots, seg_column, place, groups):
    slots = len(kv_slots)
    rows, width = queries.shape
    ratio = width // HDIM // groups
    steps = groups // 2
    block = 2 * ratio * HDIM
    whole = pl.BlockSpec((rows, LANES), lambda s: (0, 0))
    wide = pl.BlockSpec((rows, block), lambda s: (0, s))
    out = pl.pallas_call(
        functools.partial(attend_back_kernel, slots, ratio),
        out_shape=(jax.ShapeDtypeStruct((rows, width), BF16),)
        + (jax.ShapeDtypeStruct((groups * rows, LANES), BF16),) * slots,
        grid=(steps,),
        in_specs=[
            pl.BlockSpec(memory_space=pltpu.SMEM),
            wide,
            wide,
            wide,
            pl.BlockSpec((1, rows, LANES), lambda s: (s, 0, 0)),
            whole,
            whole,
            pl.BlockSpec((rows, 1), lambda s: (0, 0)),
        ]
        + kv_specs(slots, groups, rows),
        out_specs=(wide,) + (pl.BlockSpec((2 * rows, LANES), lambda s: (s, 0)),) * slots,
        scratch_shapes=[
            pltpu.VMEM((slots, rows, rows), F32),
            pltpu.VMEM((ratio * rows, LANES), BF16),
            pltpu.VMEM((ratio * rows, LANES), BF16),
            pltpu.VMEM((ratio * rows, LANES), F32),
            pltpu.VMEM((ratio * rows, 1), F32),
            pltpu.VMEM((ratio * rows, 1), F32),
            pltpu.SMEM((1,), jnp.int32),
        ],
        compiler_params=params(),
        cost_estimate=cost(2),
        name="attend_back",
    )(place, queries, attended, grad, lse, *tables, seg_column, *kv_slots, *kv_slots)
    return out[0], out[1:]


def unpack_kernel(own_ref, above_ref, cos_ref, sin_ref, key_ref, value_ref):
    rows = cos_ref.shape[0]
    low = low_lanes(rows)
    cosine, sine = cos_ref[...], sin_ref[...]
    for i in range(key_ref.shape[1] // LANES):
        even, odd = (
            own_ref[g * rows : (g + 1) * rows, :].astype(F32) + above_ref[g * rows : (g + 1) * rows, :].astype(F32)
            for g in (2 * i, 2 * i + 1)
        )
        slab = jnp.where(low, even, pltpu.roll(odd, HDIM, 1))
        slab = slab * cosine - partner_lanes(slab) * sine
        key_ref[:, i * LANES : (i + 1) * LANES] = slab.astype(BF16)
        value_ref[:, i * LANES : (i + 1) * LANES] = jnp.where(
            low, pltpu.roll(even, HDIM, 1), odd
        ).astype(BF16)


def expert_kernel(blocks, slot_rows, local_experts, place_ref, router_ref, gate_ref, up_ref, down_ref, *refs):
    sources = 2 * blocks - 1
    normed_in, cot_in = refs[:sources], refs[sources : 2 * sources]
    refs = refs[2 * sources :]
    xs_ref, cs_ref, hs_ref, gate_grad_ref, up_grad_ref, hit_ref = refs[:6]
    grad_out, router_grad_ref = refs[6:8]
    x_all, c_all, info, gates, back, grad_acc, grad_low, sems, out_sem = refs[8:]
    step = pl.program_id(0)
    rows, width = x_all.shape[1:]
    expert_pad = router_ref.shape[0]
    first_expert = place_ref[0]
    mine = pl.ds(first_expert + step, 1)

    def source_copies(i, s):
        return (
            pltpu.make_async_copy(normed_in[s], x_all.at[i], sems.at[0, i]),
            pltpu.make_async_copy(cot_in[s], c_all.at[i], sems.at[1, i]),
        )

    @pl.when(step == 0)
    def _():
        for i in range(blocks):
            for s in range(sources):

                @pl.when(place_ref[1 + i] == s)
                def _(i=i, s=s):
                    for copy in source_copies(i, s):
                        copy.start()

        for i in range(blocks):
            for copy in source_copies(i, 0):
                copy.wait()
        same = jnp.where(
            lax.broadcasted_iota(jnp.int32, (rows, rows), 0) == lax.broadcasted_iota(jnp.int32, (rows, rows), 1),
            1.0,
            0.0,
        ).astype(BF16)
        for i in range(blocks):
            info[i] = dot(c_all[i, :, width:], same, TN)
            logits = dot(router_ref[...], x_all[i], NT)
            logits = jnp.where(info[i, :expert_pad, :] >= 0, logits, MASKED_SCORE)
            weights = jnp.exp(logits - jnp.max(logits, axis=0, keepdims=True))
            gates[i] = weights / jnp.sum(weights, axis=0, keepdims=True)
        back[...] = jnp.zeros_like(back)
        grad_acc[...] = jnp.zeros_like(grad_acc)

    slot_ids = lax.broadcasted_iota(jnp.int32, (slot_rows, rows), 0).astype(F32)
    gate_slots = []
    for i in range(blocks):
        hit = slot_ids == info[i, mine, :]
        part = slice(i * slot_rows, (i + 1) * slot_rows)
        gate_slots.append(
            jnp.sum(jnp.where(hit, gates[i, mine, :], 0.0), axis=-1, keepdims=True)
        )
        hit = jnp.where(hit, 1.0, 0.0).astype(BF16)
        hit_ref[0, part, :] = hit
        xs_ref[0, part, :] = dot(hit, x_all[i]).astype(BF16)
        cs_ref[0, part, :] = dot(hit, c_all[i, :, :width]).astype(BF16)
    gate_slot = jnp.concatenate(gate_slots, axis=0) * RESIDUAL_SCALE
    gate_pre = dot(xs_ref[0], gate_ref[0])
    up_pre = dot(xs_ref[0], up_ref[0])
    raw_grad = dot(cs_ref[0], down_ref[0])
    sigmoid = 1.0 / (1.0 + jnp.exp(-gate_pre))
    active = gate_pre * sigmoid
    expert_hidden = (active * up_pre).astype(BF16).astype(F32)
    hs_ref[0] = (expert_hidden * gate_slot).astype(BF16)
    back_slot = jnp.sum(expert_hidden * raw_grad, axis=-1, keepdims=True) * RESIDUAL_SCALE
    hidden_grad = raw_grad * gate_slot
    gate_grad_ref[0] = (hidden_grad * up_pre * sigmoid * (1.0 + gate_pre * (1.0 - sigmoid))).astype(BF16)
    up_grad_ref[0] = (hidden_grad * active).astype(BF16)
    slot_grad = (
        dot(gate_grad_ref[0], gate_ref[0], NT) + dot(up_grad_ref[0], up_ref[0], NT)
    ).astype(BF16)
    for i in range(blocks):
        part = slice(i * slot_rows, (i + 1) * slot_rows)
        hit = hit_ref[0, part, :]
        back_row = jnp.sum(hit.astype(F32) * back_slot[part], axis=0, keepdims=True)
        back[i, mine, :] = back_row * gates[i, mine, :]
        grad_acc[i] += dot(hit, slot_grad[part], TN)

    @pl.when(step == local_experts - 1)
    def _():
        router_sum = None
        for i in range(blocks):
            share = back[i]
            logit_grad = (share - gates[i] * jnp.sum(share, axis=0, keepdims=True)).astype(BF16)
            grad_low[i] = (grad_acc[i] + dot(logit_grad, router_ref[...], TN)).astype(BF16)
            part = dot(logit_grad, x_all[i])
            router_sum = part if router_sum is None else router_sum + part
        router_grad_ref[...] = router_sum

        def copy(i):
            return pltpu.make_async_copy(grad_low.at[i], grad_out.at[place_ref[1 + blocks + i]], out_sem.at[i])

        for i in range(blocks):
            copy(i).start()
        for i in range(blocks):
            copy(i).wait()


def run_experts(place, router_t, gate_weight, up_weight, down_weight, normed, cots, slot_rows):
    local_experts, width, hidden = gate_weight.shape
    sources = len(normed)
    blocks = (sources + 1) // 2
    rows = normed[0].shape[0]
    expert_pad = router_t.shape[0]
    slots = blocks * slot_rows
    anywhere = pl.BlockSpec(memory_space=pl.ANY)
    weight_spec = pl.BlockSpec((1, width, hidden), lambda e, place: (e, 0, 0))

    def slot_spec(columns):
        return pl.BlockSpec((1, slots, columns), lambda e, place: (e, 0, 0))

    def slot_shape(columns):
        return jax.ShapeDtypeStruct((local_experts, slots, columns), BF16)

    out = pl.pallas_call(
        functools.partial(expert_kernel, blocks, slot_rows, local_experts),
        out_shape=(
            slot_shape(width),
            slot_shape(width),
            slot_shape(hidden),
            slot_shape(hidden),
            slot_shape(hidden),
            slot_shape(rows),
        )
        + (jax.ShapeDtypeStruct((blocks, rows, width), BF16), jax.ShapeDtypeStruct((expert_pad, width), F32)),
        grid_spec=pltpu.PrefetchScalarGridSpec(
            num_scalar_prefetch=1,
            grid=(local_experts,),
            in_specs=[pl.BlockSpec((expert_pad, width), lambda e, place: (0, 0))]
            + [weight_spec] * 3
            + [anywhere] * (2 * sources),
            out_specs=(
                slot_spec(width),
                slot_spec(width),
                slot_spec(hidden),
                slot_spec(hidden),
                slot_spec(hidden),
                slot_spec(rows),
            )
            + (anywhere, pl.BlockSpec((expert_pad, width), lambda e, place: (0, 0))),
            scratch_shapes=[
                pltpu.VMEM((blocks, rows, width), BF16),
                pltpu.VMEM((blocks, rows, width + LANES), BF16),
                pltpu.VMEM((blocks, LANES, rows), F32),
                pltpu.VMEM((blocks, expert_pad, rows), F32),
                pltpu.VMEM((blocks, expert_pad, rows), F32),
                pltpu.VMEM((blocks, rows, width), F32),
                pltpu.VMEM((blocks, rows, width), BF16),
                pltpu.SemaphoreType.DMA((2, blocks)),
                pltpu.SemaphoreType.DMA((blocks,)),
            ],
        ),
        compiler_params=params(),
        cost_estimate=cost(45),
        name="experts",
    )(place, router_t, gate_weight, up_weight, down_weight, *normed, *cots)
    return out[:6], out[6], out[7]


def mixture_kernel(blocks, slot_rows, local_experts, order_ref, down_ref, hs_ref, hit_ref, mix_out, mix_acc, mix_low, out_sem):
    step = pl.program_id(0)

    @pl.when(step == 0)
    def _():
        mix_acc[...] = jnp.zeros_like(mix_acc)

    slot_out = dot(hs_ref[0], down_ref[0], NT).astype(BF16)
    for i in range(blocks):
        part = slice(i * slot_rows, (i + 1) * slot_rows)
        mix_acc[i] += dot(hit_ref[0, part, :], slot_out[part], TN)

    @pl.when(step == local_experts - 1)
    def _():
        def copy(i):
            return pltpu.make_async_copy(mix_low.at[i], mix_out.at[order_ref[i]], out_sem.at[i])

        for i in range(blocks):
            mix_low[i] = mix_acc[i].astype(BF16)
            copy(i).start()
        for i in range(blocks):
            copy(i).wait()


def run_mixture(order, down_weight, saved, slot_rows):
    hs, hit = saved[2], saved[5]
    local_experts, width, hidden = down_weight.shape
    slots, rows = hit.shape[1:]
    blocks = slots // slot_rows
    return pl.pallas_call(
        functools.partial(mixture_kernel, blocks, slot_rows, local_experts),
        out_shape=jax.ShapeDtypeStruct((blocks, rows, width), BF16),
        grid_spec=pltpu.PrefetchScalarGridSpec(
            num_scalar_prefetch=1,
            grid=(local_experts,),
            in_specs=[
                pl.BlockSpec((1, width, hidden), lambda e, order: (e, 0, 0)),
                pl.BlockSpec((1, slots, hidden), lambda e, order: (e, 0, 0)),
                pl.BlockSpec((1, slots, rows), lambda e, order: (e, 0, 0)),
            ],
            out_specs=pl.BlockSpec(memory_space=pl.ANY),
            scratch_shapes=[
                pltpu.VMEM((blocks, rows, width), F32),
                pltpu.VMEM((blocks, rows, width), BF16),
                pltpu.SemaphoreType.DMA((blocks,)),
            ],
        ),
        compiler_params=params(),
        cost_estimate=cost(10),
        name="mixture",
    )(order, down_weight, hs, hit)


def turn_rows(block, sides_ref, owned):
    width = block.shape[1]
    chunk = int(np.lcm(2 * owned, LANES))
    for c in range(width // chunk):
        turned = block[:, c * chunk : (c + 1) * chunk].T
        for o in range(chunk // owned):
            owner = c * (chunk // owned) + o
            spot = owner // 2 * owned
            sides_ref[owner % 2, spot : spot + owned, :] = turned[o * owned : (o + 1) * owned]


def expert_grad_kernel(xs_ref, cs_ref, hs_ref, gate_grad_ref, up_grad_ref, out_ref, turned):
    owners, owned = out_ref.shape[0], out_ref.shape[3]
    for left_ref, rights in ((xs_ref, ((0, gate_grad_ref), (1, up_grad_ref))), (cs_ref, ((2, hs_ref),))):
        turned[...] = left_ref[0].T
        for w, right_ref in rights:
            grad = dot(turned[...], right_ref[0]).astype(BF16)
            for o in range(owners):
                out_ref[o, w, 0] = grad[o * owned : (o + 1) * owned]


def run_expert_grads(saved, owners):
    xs, cs, hs, gate_grad, up_grad, _ = saved
    local_experts, slots, width = xs.shape
    hidden = hs.shape[2]
    owned = width // owners
    wide = pl.BlockSpec((1, slots, width), lambda e: (e, 0, 0))
    narrow = pl.BlockSpec((1, slots, hidden), lambda e: (e, 0, 0))
    return pl.pallas_call(
        expert_grad_kernel,
        out_shape=jax.ShapeDtypeStruct((owners, 3, local_experts, owned, hidden), BF16),
        grid=(local_experts,),
        in_specs=[wide, wide, narrow, narrow, narrow],
        out_specs=pl.BlockSpec((owners, 3, 1, owned, hidden), lambda e: (0, 0, e, 0, 0)),
        scratch_shapes=[pltpu.VMEM((width, slots), BF16)],
        compiler_params=params(),
        cost_estimate=cost(30),
        name="expert_grads",
    )(xs, cs, hs, gate_grad, up_grad)


def dense_grad_kernel(pairs, place_ref, *refs):
    lefts, rights = refs[:pairs], refs[pairs : 2 * pairs]
    smalls = refs[2 * pairs : -3]
    keep_ref, send_ref, sides = refs[-3:]
    owned = keep_ref.shape[1]
    bit = place_ref[0] % 2
    column = 0
    for i in range(pairs):
        if i == 0 or lefts[i] is not lefts[i - 1]:
            turn_rows(lefts[i][...], sides, owned)
        columns = rights[i].shape[1]
        for out_ref, side in ((send_ref, 1 - bit), (keep_ref, bit)):
            grad = dot(sides[side], rights[i][...]).astype(BF16)
            for q in range(keep_ref.shape[0]):
                out_ref[q, :, column : column + columns] = grad[q * owned : (q + 1) * owned]
        column += columns
    if smalls:
        rows = jnp.concatenate([ref[...] for ref in smalls], axis=0)
        rows = jnp.concatenate([rows, jnp.zeros((LANES - rows.shape[0], rows.shape[1]), F32)], axis=0)
        turned = rows.T.astype(BF16)
        for owner in range(2 * keep_ref.shape[0]):
            piece = turned[owner * owned : (owner + 1) * owned]

            @pl.when(bit == owner % 2)
            def _(owner=owner, piece=piece):
                keep_ref[owner // 2, :, column:] = piece

            @pl.when(bit != owner % 2)
            def _(owner=owner, piece=piece):
                send_ref[owner // 2, :, column:] = piece


def dense_grads(dp_word, pairs, owners, smalls=()):
    rows, width = pairs[0][0].shape
    columns = sum(right.shape[1] for _, right in pairs) + (LANES if smalls else 0)
    return pl.pallas_call(
        functools.partial(dense_grad_kernel, len(pairs)),
        out_shape=(jax.ShapeDtypeStruct((owners // 2, width // owners, columns), BF16),) * 2,
        in_specs=[pl.BlockSpec(memory_space=pltpu.SMEM)] + [vmem()] * (2 * len(pairs) + len(smalls)),
        out_specs=(vmem(),) * 2,
        scratch_shapes=[pltpu.VMEM((2, width // 2, rows), BF16)],
        compiler_params=params(),
        cost_estimate=cost(4),
        name="dense_grads",
    )(dp_word, *(left for left, _ in pairs), *(right for _, right in pairs), *smalls)


def line_up(value, size):
    return lax.ppermute(value, "expert", [(i, i + 1) for i in range(size - 1)])


def line_down(value, size):
    return lax.ppermute(value, "expert", [(i + 1, i) for i in range(size - 1)])


def line_gather(value, size):
    below, above = [], []
    up, down = value, value
    for _ in range(size - 1):
        up = line_up(up, size)
        down = line_down(down, size)
        below.append(up)
        above.append(down)
    return [value] + below + above


def add_low(*terms):
    total = terms[0].astype(F32)
    for term in terms[1:]:
        total = total + term.astype(F32)
    return total.astype(BF16)


def flip(value, bit, size):
    return lax.ppermute(value, "dp", [(i, i ^ bit) for i in range(size)])


def halve(terms, bit, left, dp_place):
    axis = left.index(bit)
    own = (dp_place >> bit) & 1
    return tuple(
        add_low(*(lax.dynamic_index_in_dim(t, side, axis, keepdims=False) for t in terms)) for side in (own, 1 - own)
    )


def start_spread(routes):
    return [
        tuple(t.reshape((2,) * (t.shape[0].bit_length() - 1) + t.shape[1:]) for t in terms) for terms in routes
    ]


def step_spread(routes, stage, dp_size, dp_place):
    bits = list(range(1, dp_size.bit_length() - 1))
    kept, sent = [], []
    for terms, order in zip(routes, (bits, bits[::-1])):
        left = [bit for bit in bits[::-1] if bit not in order[:stage]]
        keep, send = halve(terms, order[stage], left, dp_place)
        kept.append(keep)
        sent.append(flip(send, 1 << order[stage], dp_size))
    sent = lax.optimization_barrier(tuple(sent))
    return list(zip(kept, sent))


def start_dense(terms):
    half = terms[0].shape[2] // 2 // LANES * LANES
    return start_spread([tuple(t[..., :half] for t in terms), tuple(t[..., half:] for t in terms)])


def finish_dense(routes, size):
    block = jnp.concatenate([add_low(*terms) for terms in routes], axis=-1)
    parts = lax.all_to_all(block.reshape(size, -1, block.shape[-1]), "expert", 0, 0, tiled=True)
    return jnp.sum(parts.astype(F32), axis=0)


def reduce_top(top, dp_size, size):
    for bit in range(dp_size.bit_length() - 1):
        top = jnp.maximum(top, flip(top, 1 << bit, dp_size))
    for bit in range(size.bit_length() - 1):
        top = jnp.maximum(top, lax.ppermute(top, "expert", [(i, i ^ (1 << bit)) for i in range(size)]))
    return top


def arrival_order(size):
    sources, places = np.zeros((size, size), np.int32), np.zeros((size, size), np.int32)
    for place in range(size):
        spots = [(0, place)]
        for k in range(1, size):
            if place - k >= 0:
                spots.append((k, place - k))
            if place + k < size:
                spots.append((size - 1 + k, place + k))
        sources[place], places[place] = zip(*spots)
    return sources, places


def norm_backward(hidden, factor, gain_vec, grad_in):
    scaled = grad_in * gain_vec
    hidden_grad = factor * scaled - hidden * factor**3 * jnp.mean(
        scaled * hidden, axis=-1, keepdims=True
    )
    return hidden_grad, jnp.sum(grad_in * hidden * factor, axis=0)


def local(
    tokens,
    first_gain,
    query_weight,
    key_weight,
    value_weight,
    output_weight,
    second_gain,
    router_weight,
    gate_weight,
    up_weight,
    down_weight,
    cotangent,
    routes,
    segments,
    threshold,
):
    rows, width = tokens.shape
    query_width, kv_width = query_weight.shape[1], key_weight.shape[1]
    heads, groups = query_width // HDIM, kv_width // HDIM
    ratio = heads // groups
    local_experts = gate_weight.shape[0]
    size, dp_size = lax.axis_size("expert"), lax.axis_size("dp")
    place, dp_place = lax.axis_index("expert"), lax.axis_index("dp")
    experts = local_experts * size
    expert_pad = round_up(experts, 16)
    capacity = rows * routes.shape[1] * 9 // (experts * 8)
    slot_rows = round_up(capacity, 64)

    tables = tuple(
        lax.dynamic_slice_in_dim(jnp.asarray(table), place * rows, rows, 0) for table in rotary_tables(rows * size)
    )
    seg_block = jnp.pad(segments.reshape(rows // LANES, LANES).astype(BF16), ((0, 16 - rows // LANES), (0, 0)))

    normed, first_factor, kv_own = pl.pallas_call(
        front_kernel,
        out_shape=(
            jax.ShapeDtypeStruct((rows, width), BF16),
            jax.ShapeDtypeStruct((rows, 1), F32),
            jax.ShapeDtypeStruct((groups * rows + 16, LANES), BF16),
        ),
        in_specs=[vmem()] * 7,
        out_specs=(vmem(),) * 3,
        compiler_params=params(),
        cost_estimate=cost(4),
        name="front",
    )(tokens, first_gain.reshape(1, width), key_weight, value_weight, *tables, seg_block)
    kv_slots = [kv_own]
    for _ in range(size - 1):
        kv_slots.append(line_up(kv_slots[-1], size))

    cot_own = pl.pallas_call(
        extend_kernel,
        out_shape=jax.ShapeDtypeStruct((rows, width + LANES), BF16),
        in_specs=[vmem()] * 2,
        out_specs=vmem(),
        compiler_params=params(),
        cost_estimate=cost(2),
        name="extend",
    )(cotangent, routes)
    cots = line_gather(cot_own, size)

    query_block = 512
    queries = pl.pallas_call(
        query_kernel,
        out_shape=jax.ShapeDtypeStruct((rows, query_width), BF16),
        grid=(query_width // query_block,),
        in_specs=[
            pl.BlockSpec((rows, width), lambda s: (0, 0)),
            pl.BlockSpec((width, query_block), lambda s: (0, s)),
            pl.BlockSpec((rows, LANES), lambda s: (0, 0)),
            pl.BlockSpec((rows, LANES), lambda s: (0, 0)),
        ],
        out_specs=pl.BlockSpec((rows, query_block), lambda s: (0, s)),
        compiler_params=params(),
        cost_estimate=cost(5),
        name="queries",
    )(normed, query_weight, *tables)

    seg_column = segments.reshape(rows, 1).astype(F32)
    place_word = place.reshape(1).astype(jnp.int32)
    attended, lse, top = attend(queries, kv_slots, seg_column, place_word, groups)
    head_top = reduce_top(top, dp_size, size)[:, 0, : 2 * ratio].reshape(heads)

    hidden_in = tokens.astype(F32)
    hidden_mid = hidden_in + RESIDUAL_SCALE * dot(attended, output_weight, NT)
    second_factor = lax.rsqrt(jnp.mean(hidden_mid * hidden_mid, axis=-1, keepdims=True) + NORM_EPSILON)
    second_normed = (hidden_mid * second_factor * second_gain).astype(BF16)
    normed_blocks = line_gather(second_normed, size)

    router_t = jnp.pad(router_weight.T, ((0, expert_pad - experts), (0, 0)))
    sources, blocks_of = (jnp.asarray(table)[place] for table in arrival_order(size))
    expert_place = jnp.concatenate([(place * local_experts).reshape(1), sources, blocks_of]).astype(jnp.int32)
    expert_place, head_top = lax.optimization_barrier((expert_place, head_top))
    saved, grad_blocks, router_part = run_experts(
        expert_place, router_t, gate_weight, up_weight, down_weight, normed_blocks, cots, slot_rows
    )
    grad_blocks = lax.all_to_all(grad_blocks, "expert", 0, 0, tiled=True)

    dp_word = dp_place.reshape(1).astype(jnp.int32)
    expert_sums = run_expert_grads(saved, dp_size)
    mixture = run_mixture(blocks_of, down_weight, saved, slot_rows)
    mixture, grad_blocks, expert_sums = lax.optimization_barrier((mixture, grad_blocks, expert_sums))
    normed_grad = jnp.sum(grad_blocks.astype(F32), axis=0)
    expert_sums = lax.psum_scatter(expert_sums, "dp", scatter_dimension=0, tiled=True)[0].astype(F32)
    mixture = lax.all_to_all(mixture, "expert", 0, 0, tiled=True)

    out_grad = cotangent.astype(F32)
    mid_back, second_gain_part = norm_backward(hidden_mid, second_factor, second_gain, normed_grad)
    mid_grad = out_grad + mid_back
    branch_grad = (RESIDUAL_SCALE * mid_grad).astype(BF16)
    attended_grad = dot(branch_grad, output_weight).astype(BF16)
    query_back, dkv = attend_back(
        queries, attended, attended_grad, lse, tables, kv_slots, seg_column, place_word, groups
    )
    keep, send = dense_grads(dp_word, [(branch_grad, attended), (normed, query_back)], dp_size)
    wide = start_dense((keep, flip(send, 1, dp_size)))
    stages = dp_size.bit_length() - 2
    down = dkv[size - 1]
    for k in range(1, size):
        from_above = line_down(down, size)
        if k == 1:
            from_above, mixture = lax.optimization_barrier((from_above, mixture))
        if k == size - 2:
            from_above, wide = lax.optimization_barrier((from_above, wide))
            wide = step_spread(wide, 0, dp_size, dp_place)
        if k < size - 1:
            down = add_low(from_above, dkv[size - 1 - k])
    from_above, wide = lax.optimization_barrier((from_above, wide))
    for stage in range(1, stages):
        wide = step_spread(wide, stage, dp_size, dp_place)
    block_out = (hidden_mid + jnp.sum(mixture.astype(F32), axis=0)).astype(BF16)
    key_back, value_back = pl.pallas_call(
        unpack_kernel,
        out_shape=(jax.ShapeDtypeStruct((rows, kv_width), BF16),) * 2,
        in_specs=[vmem()] * 4,
        out_specs=(vmem(),) * 2,
        compiler_params=params(),
        cost_estimate=cost(2),
        name="unpack",
    )(dkv[0], from_above, *tables)

    first_grad = dot(query_back, query_weight, NT)
    first_grad = first_grad + dot(key_back, key_weight, NT)
    first_grad = first_grad + dot(value_back, value_weight, NT)
    input_back, first_gain_part = norm_backward(hidden_in, first_factor, first_gain, first_grad)
    input_grad = mid_grad + input_back
    keep, send = dense_grads(
        dp_word,
        [(normed, key_back), (normed, value_back)],
        dp_size,
        (router_part, second_gain_part[None], first_gain_part[None]),
    )
    keep, send, wide = lax.optimization_barrier((keep, send, wide))
    rest = start_dense((keep, flip(send, 1, dp_size)))
    for stage in range(stages):
        rest = step_spread(rest, stage, dp_size, dp_place)
    wide_grad, rest_grad = finish_dense(wide, size), finish_dense(rest, size)
    projection_grad, query_grad = wide_grad[:, :query_width], wide_grad[:, query_width:]
    key_grad = rest_grad[:, :kv_width]
    value_grad = rest_grad[:, kv_width : 2 * kv_width]
    small_grad = rest_grad[:, 2 * kv_width :]

    head_scale = threshold / jnp.maximum(head_top, threshold)
    group_scale = jnp.min(head_scale.reshape(groups, ratio), axis=1)
    row_count = width // (dp_size * size)
    row_start = (dp_place * size + place) * row_count
    query_rows = lax.dynamic_slice_in_dim(query_weight, row_start, row_count, 0).astype(F32)
    key_rows = lax.dynamic_slice_in_dim(key_weight, row_start, row_count, 0).astype(F32)
    query_clipped = (query_rows * jnp.repeat(jnp.sqrt(head_scale), HDIM)[None, :]).astype(BF16)
    key_clipped = (key_rows * jnp.repeat(jnp.sqrt(group_scale), HDIM)[None, :]).astype(BF16)
    return (
        block_out,
        input_grad,
        small_grad[:, expert_pad + 1],
        query_grad,
        key_grad,
        value_grad,
        projection_grad,
        small_grad[:, expert_pad],
        small_grad[:, :experts],
        expert_sums[0],
        expert_sums[1],
        expert_sums[2],
        head_scale,
        query_clipped,
        key_clipped,
    )


def solution(mesh):
    row = P(("dp", "expert"), None)
    vector = P(("dp", "expert"))
    expert_in = P("expert", None, None)
    expert_out = P("expert", "dp", None)
    return jax.shard_map(
        local,
        mesh=mesh,
        in_specs=(row,) + (P(),) * 7 + (expert_in,) * 3 + (row, row, vector, P()),
        out_specs=(row, row, vector)
        + (row,) * 4
        + (vector, row)
        + (expert_out,) * 3
        + (P(), row, row),
        check_vma=False,
    )
```

```python
import functools

import jax
import jax.numpy as jnp
import numpy as np
from jax import lax
from jax.experimental import pallas as pl
from jax.experimental.pallas import tpu as pltpu
from jax.sharding import PartitionSpec as P

HDIM = 64
LANES = 128
ATTENTION_SCALE = 0.015625
RESIDUAL_SCALE = 0.22
NORM_EPSILON = 1e-06
ROTARY_BASE = 10000.0
MASKED_SCORE = -1e30
BF16 = jnp.bfloat16
F32 = jnp.float32
NN = (((1,), (0,)), ((), ()))
NT = (((1,), (1,)), ((), ()))
TN = (((0,), (0,)), ((), ()))
VMEM_LIMIT = 60 * 1024 * 1024
COLUMNS = 512


def dot(left, right, dims=NN):
    return lax.dot_general(left, right, dims, preferred_element_type=F32)


def round_up(count, unit):
    return (count + unit - 1) // unit * unit


def low_lanes(rows):
    return lax.broadcasted_iota(jnp.int32, (rows, LANES), 1) < HDIM


def partner_lanes(slab):
    lane = lax.broadcasted_iota(jnp.int32, slab.shape, 1) % HDIM
    half = HDIM // 2
    return jnp.where(lane < half, pltpu.roll(slab, LANES - half, 1), pltpu.roll(slab, half, 1))


def vmem():
    return pl.BlockSpec(memory_space=pltpu.VMEM)


def params(**more):
    return pltpu.CompilerParams(vmem_limit_bytes=VMEM_LIMIT, **more)


def cost(microseconds):
    return pl.CostEstimate(flops=int(microseconds * 1e6), bytes_accessed=0, transcendentals=0)


def rotary_tables(length):
    half = HDIM // 2
    inverse = np.float32(ROTARY_BASE) ** (np.float32(-2.0) * np.arange(half, dtype=np.float32) / np.float32(HDIM))
    angles = np.arange(length, dtype=np.float32)[:, None] * np.tile(inverse, LANES // half)[None, :]
    angles = angles.astype(np.float32).astype(np.float64)
    sign = np.where(np.arange(LANES) % HDIM < half, -1.0, 1.0)
    return np.cos(angles).astype(np.float32), (np.sin(angles) * sign).astype(np.float32)


def extend_kernel(cotangent_ref, routes_ref, out_ref):
    rows, top_count = routes_ref.shape
    width = cotangent_ref.shape[1]
    lane = lax.broadcasted_iota(jnp.int32, (rows, LANES), 1)
    chosen = jnp.zeros((rows, LANES), F32)
    for k in range(top_count):
        chosen = chosen + jnp.where(routes_ref[:, k : k + 1] == lane, 1.0, 0.0)
    first = lax.broadcasted_iota(jnp.int32, (rows, rows), 0)
    second = lax.broadcasted_iota(jnp.int32, (rows, rows), 1)
    earlier = jnp.where(second < first, 1.0, 0.0).astype(BF16)
    rank = dot(earlier, chosen.astype(BF16))
    out_ref[:, :width] = cotangent_ref[...]
    out_ref[:, width:] = jnp.where(chosen > 0.5, rank, -1.0).astype(BF16)


def front_kernel(tokens_ref, gain_ref, key_ref, value_ref, cos_ref, sin_ref, segments_ref, normed_ref, factor_ref, kv_ref):
    hidden = tokens_ref[...].astype(F32)
    factor = lax.rsqrt(jnp.mean(hidden * hidden, axis=-1, keepdims=True) + NORM_EPSILON)
    normed = (hidden * factor * gain_ref[...]).astype(BF16)
    normed_ref[...] = normed
    factor_ref[...] = factor
    keys = dot(normed, key_ref[...])
    values = dot(normed, value_ref[...])
    cosine, sine = cos_ref[...], sin_ref[...]
    rows = hidden.shape[0]
    low = low_lanes(rows)
    for i in range(keys.shape[1] // LANES):
        slab = keys[:, i * LANES : (i + 1) * LANES]
        slab = slab * cosine + partner_lanes(slab) * sine
        value_slab = values[:, i * LANES : (i + 1) * LANES]
        even, odd = 2 * i * rows, (2 * i + 1) * rows
        kv_ref[even : even + rows, :] = jnp.where(low, slab, pltpu.roll(value_slab, HDIM, 1)).astype(BF16)
        kv_ref[odd : odd + rows, :] = jnp.where(low, pltpu.roll(slab, HDIM, 1), value_slab).astype(BF16)
    kv_ref[keys.shape[1] // HDIM * rows :, :] = segments_ref[...]


def query_kernel(normed_ref, query_ref, cos_ref, sin_ref, out_ref):
    raw = dot(normed_ref[...], query_ref[...])
    cosine, sine = cos_ref[...], sin_ref[...]
    for i in range(raw.shape[1] // LANES):
        slab = raw[:, i * LANES : (i + 1) * LANES]
        slab = slab * cosine + partner_lanes(slab) * sine
        out_ref[:, i * LANES : (i + 1) * LANES] = (slab.astype(BF16).astype(F32) * ATTENTION_SCALE).astype(BF16)


def fill_bias(bias_ref, need_ref, place_ref, seg_row, seg_columns):
    slots, keys, rows = bias_ref.shape
    for k in range(slots):
        allowed = seg_columns[k] == seg_row
        if k == 0:
            allowed = allowed & (
                lax.broadcasted_iota(jnp.int32, (keys, rows), 0) <= lax.broadcasted_iota(jnp.int32, (keys, rows), 1)
            )
        bias_ref[k] = jnp.where(allowed, 0.0, MASKED_SCORE)
    first = jnp.min(seg_row)
    need = jnp.int32(1)
    for k in range(1, slots):
        need = jnp.where((jnp.max(seg_columns[k]) >= first) & (k <= place_ref[0]), k + 1, need)
    need_ref[0] = need


def prepare_bias(bias_ref, need_ref, place_ref, seg_refs):
    slots, keys, _ = bias_ref.shape
    halves = keys // LANES
    seg_rows = [
        jnp.concatenate([ref[j : j + 1, :].astype(F32) for j in range(halves)], axis=1) for ref in seg_refs
    ]
    seg_columns = [jnp.broadcast_to(row, (LANES, keys)).T[:, :1] for row in seg_rows]
    fill_bias(bias_ref, need_ref, place_ref, seg_rows[0], seg_columns)


def head_slab(block, head, upper):
    slab = block[:, (head // 2) * LANES : (head // 2 + 1) * LANES].astype(F32)
    low = low_lanes(slab.shape[0])
    if (head % 2 == 1) != upper:
        slab = pltpu.roll(slab, HDIM, 1)
    return jnp.where(low != upper, slab, 0.0)


def add_bias(scores, bias, ratio):
    rows = bias.shape[1]
    return jnp.concatenate([scores[:, r * rows : (r + 1) * rows] + bias for r in range(ratio)], axis=1)


def attend_kernel(slots, ratio, place_ref, query_ref, *refs):
    kv_refs, seg_refs = refs[:slots], refs[slots : 2 * slots]
    attended_ref, lse_ref, top_ref, bias_ref, stacked_ref, scores_ref, acc_ref, max_ref, need_ref = refs[2 * slots :]
    rows = query_ref.shape[0]
    low = low_lanes(rows)

    @pl.when(pl.program_id(0) == 0)
    def _():
        prepare_bias(bias_ref, need_ref, place_ref, seg_refs)

    need = need_ref[0]
    outs = []
    for group in range(2):
        for r in range(ratio):
            stacked_ref[r * rows : (r + 1) * rows, :] = head_slab(
                query_ref, group * ratio + r, False
            ).astype(BF16)
        for k in range(slots):

            def score(k=k):
                kv = kv_refs[k][group * rows : (group + 1) * rows, :]
                scores = add_bias(dot(kv, stacked_ref[...], NT), bias_ref[k], ratio)
                scores_ref[k] = scores
                top = jnp.max(scores, axis=0, keepdims=True)
                max_ref[...] = top if k == 0 else jnp.maximum(max_ref[...], top)

            if k == 0:
                score()
            else:
                pl.when(k < need)(score)
        for k in range(slots):

            def mix(k=k):
                kv = kv_refs[k][group * rows : (group + 1) * rows, :]
                kv = jnp.where(low, jnp.ones_like(kv), kv)
                weights = jnp.exp(scores_ref[k] - max_ref[...]).astype(BF16)
                part = dot(kv, weights, TN)
                acc_ref[...] = part if k == 0 else acc_ref[...] + part

            if k == 0:
                mix()
            else:
                pl.when(k < need)(mix)
        total = acc_ref[:1, :]
        lse_ref[0, group : group + 1, :] = max_ref[...] + jnp.log(total)
        top_ref[0, group : group + 1, :] = max_ref[...]
        mixed = acc_ref[HDIM:, :] / total
        for r in range(ratio):
            outs.append(mixed[:, r * rows : (r + 1) * rows])
    for i in range(len(outs) // 2):
        slab = jnp.concatenate([outs[2 * i], outs[2 * i + 1]], axis=0)
        attended_ref[:, i * LANES : (i + 1) * LANES] = slab.T.astype(BF16)


def kv_specs(slots, groups, rows):
    return [pl.BlockSpec((2 * rows, LANES), lambda s: (s, 0))] * slots + [
        pl.BlockSpec((16, LANES), lambda s: (groups * rows // 16, 0))
    ] * slots


def attend(queries, kv_slots, place, groups):
    slots = len(kv_slots)
    rows, width = queries.shape
    ratio = width // HDIM // groups
    steps = groups // 2
    block = 2 * ratio * HDIM
    stats = pl.BlockSpec((1, 2, ratio * rows), lambda s: (s, 0, 0))
    return pl.pallas_call(
        functools.partial(attend_kernel, slots, ratio),
        out_shape=(jax.ShapeDtypeStruct((rows, width), BF16),)
        + (jax.ShapeDtypeStruct((steps, 2, ratio * rows), F32),) * 2,
        grid=(steps,),
        in_specs=[
            pl.BlockSpec(memory_space=pltpu.SMEM),
            pl.BlockSpec((rows, block), lambda s: (0, s)),
        ]
        + kv_specs(slots, groups, rows),
        out_specs=(pl.BlockSpec((rows, block), lambda s: (0, s)), stats, stats),
        scratch_shapes=[
            pltpu.VMEM((slots, rows, rows), F32),
            pltpu.VMEM((ratio * rows, LANES), BF16),
            pltpu.VMEM((slots, rows, ratio * rows), F32),
            pltpu.VMEM((LANES, ratio * rows), F32),
            pltpu.VMEM((1, ratio * rows), F32),
            pltpu.SMEM((1,), jnp.int32),
        ],
        compiler_params=params(),
        cost_estimate=cost(20),
        name="attend",
    )(place, queries, *kv_slots, *kv_slots)


def attend_back_kernel(slots, ratio, place_ref, query_ref, attended_ref, grad_ref, lse_ref, cos_ref, sin_ref, *refs):
    kv_refs, seg_refs = refs[:slots], refs[slots : 2 * slots]
    refs = refs[2 * slots :]
    back_ref, dkv_refs = refs[0], refs[1 : slots + 1]
    bias_ref, query_s, grad_s, acc_ref, delta_s, need_ref = refs[slots + 1 :]
    rows = query_ref.shape[0]

    @pl.when(pl.program_id(0) == 0)
    def _():
        prepare_bias(bias_ref, need_ref, place_ref, seg_refs)

    need = need_ref[0]
    outs = []
    for group in range(2):
        for r in range(ratio):
            head = group * ratio + r
            part = slice(r * rows, (r + 1) * rows)
            query_s[part, :] = head_slab(query_ref, head, False).astype(BF16)
            grad = head_slab(grad_ref, head, True)
            grad_s[part, :] = grad.astype(BF16)
            product = (grad * head_slab(attended_ref, head, True)).T
            delta_s[:, part] = jnp.sum(product, axis=0, keepdims=True)
        for k in range(slots):

            def step(k=k):
                kv = kv_refs[k][group * rows : (group + 1) * rows, :]
                scores = add_bias(dot(kv, query_s[...], NT), bias_ref[k], ratio)
                weights = jnp.exp(scores - lse_ref[0, group : group + 1, :])
                weight_grad = dot(kv, grad_s[...], NT)
                score_grad = (weights * (weight_grad - delta_s[...])).astype(BF16)
                part = dot(kv, score_grad, TN)
                acc_ref[...] = part if k == 0 else acc_ref[...] + part
                dkv_refs[k][group * rows : (group + 1) * rows, :] = (
                    dot(score_grad, query_s[...]) + dot(weights.astype(BF16), grad_s[...])
                ).astype(BF16)

            if k == 0:
                step()
            else:
                pl.when(k < need)(step)

                @pl.when(k >= need)
                def _(k=k):
                    dkv_refs[k][group * rows : (group + 1) * rows, :] = jnp.zeros((rows, LANES), BF16)

        for r in range(ratio):
            outs.append(acc_ref[:HDIM, r * rows : (r + 1) * rows] * ATTENTION_SCALE)
    cosine, sine = cos_ref[...], sin_ref[...]
    for i in range(len(outs) // 2):
        slab = jnp.concatenate([outs[2 * i], outs[2 * i + 1]], axis=0).T
        slab = slab * cosine - partner_lanes(slab) * sine
        back_ref[:, i * LANES : (i + 1) * LANES] = slab.astype(BF16)


def attend_back(queries, attended, grad, lse, tables, kv_slots, place, groups):
    slots = len(kv_slots)
    rows, width = queries.shape
    ratio = width // HDIM // groups
    steps = groups // 2
    block = 2 * ratio * HDIM
    whole = pl.BlockSpec((rows, LANES), lambda s: (0, 0))
    wide = pl.BlockSpec((rows, block), lambda s: (0, s))
    out = pl.pallas_call(
        functools.partial(attend_back_kernel, slots, ratio),
        out_shape=(jax.ShapeDtypeStruct((rows, width), BF16),)
        + (jax.ShapeDtypeStruct((groups * rows, LANES), BF16),) * slots,
        grid=(steps,),
        in_specs=[
            pl.BlockSpec(memory_space=pltpu.SMEM),
            wide,
            wide,
            wide,
            pl.BlockSpec((1, 2, ratio * rows), lambda s: (s, 0, 0)),
            whole,
            whole,
        ]
        + kv_specs(slots, groups, rows),
        out_specs=(wide,) + (pl.BlockSpec((2 * rows, LANES), lambda s: (s, 0)),) * slots,
        scratch_shapes=[
            pltpu.VMEM((slots, rows, rows), F32),
            pltpu.VMEM((ratio * rows, LANES), BF16),
            pltpu.VMEM((ratio * rows, LANES), BF16),
            pltpu.VMEM((LANES, ratio * rows), F32),
            pltpu.VMEM((1, ratio * rows), F32),
            pltpu.SMEM((1,), jnp.int32),
        ],
        compiler_params=params(),
        cost_estimate=cost(2),
        name="attend_back",
    )(place, queries, attended, grad, lse, *tables, *kv_slots, *kv_slots)
    return out[0], out[1:]


def unpack_kernel(own_ref, above_ref, cos_ref, sin_ref, key_ref, value_ref):
    rows = cos_ref.shape[0]
    low = low_lanes(rows)
    cosine, sine = cos_ref[...], sin_ref[...]
    for i in range(key_ref.shape[1] // LANES):
        even, odd = (
            own_ref[g * rows : (g + 1) * rows, :].astype(F32) + above_ref[g * rows : (g + 1) * rows, :].astype(F32)
            for g in (2 * i, 2 * i + 1)
        )
        slab = jnp.where(low, even, pltpu.roll(odd, HDIM, 1))
        slab = slab * cosine - partner_lanes(slab) * sine
        key_ref[:, i * LANES : (i + 1) * LANES] = slab.astype(BF16)
        value_ref[:, i * LANES : (i + 1) * LANES] = jnp.where(
            low, pltpu.roll(even, HDIM, 1), odd
        ).astype(BF16)


def expert_kernel(blocks, slot_rows, local_experts, place_ref, router_ref, gate_ref, up_ref, down_ref, *refs):
    sources = 2 * blocks - 1
    normed_in, cot_in = refs[:sources], refs[sources : 2 * sources]
    xs_out, cs_out, hs_ref, gate_grad_ref, up_grad_ref, hits, grad_out, router_grad_ref = refs[2 * sources : 2 * sources + 8]
    x_all, c_all, info, gates, back, xs_all, cs_all, gate_slots, slot_grads, sems, save_sem, out_sem = refs[2 * sources + 8 :]
    step = pl.program_id(0)
    rows, width = x_all.shape[1:]
    expert_pad = router_ref.shape[0]
    first_expert = place_ref[0]
    mine = pl.ds(first_expert + step, 1)

    def source_copies(i, s):
        return (
            pltpu.make_async_copy(normed_in[s], x_all.at[i], sems.at[0, i]),
            pltpu.make_async_copy(cot_in[s], c_all.at[i], sems.at[1, i]),
        )

    def save_copies():
        return (
            pltpu.make_async_copy(xs_all, xs_out, save_sem.at[0]),
            pltpu.make_async_copy(cs_all, cs_out, save_sem.at[1]),
        )

    @pl.when(step == 0)
    def _():
        for i in range(blocks):
            for s in range(sources):

                @pl.when(place_ref[1 + i] == s)
                def _(i=i, s=s):
                    for copy in source_copies(i, s):
                        copy.start()

        same = jnp.where(
            lax.broadcasted_iota(jnp.int32, (rows, rows), 0) == lax.broadcasted_iota(jnp.int32, (rows, rows), 1),
            1.0,
            0.0,
        ).astype(BF16)
        slot_ids = lax.broadcasted_iota(jnp.int32, (slot_rows, rows), 0).astype(F32)
        back[...] = jnp.zeros_like(back)
        for i in range(blocks):
            for copy in source_copies(i, 0):
                copy.wait()
            info[i] = dot(c_all[i, :, width:], same, TN)
            logits = dot(router_ref[...], x_all[i], NT)
            logits = jnp.where(info[i, :expert_pad, :] >= 0, logits, MASKED_SCORE)
            weights = jnp.exp(logits - jnp.max(logits, axis=0, keepdims=True))
            gates[i] = weights / jnp.sum(weights, axis=0, keepdims=True)
            for e in range(local_experts):
                own = pl.ds(first_expert + e, 1)
                hit = slot_ids == info[i, own, :]
                gate_slots[e, i * slot_rows : (i + 1) * slot_rows, :] = RESIDUAL_SCALE * jnp.sum(
                    jnp.where(hit, gates[i, own, :], 0.0), axis=-1, keepdims=True
                )
                hits[i, e * slot_rows : (e + 1) * slot_rows, :] = jnp.where(hit, 1.0, 0.0).astype(BF16)
            for source, target in ((x_all, xs_all), (c_all, cs_all)):
                for c in range(width // COLUMNS):
                    columns = slice(c * COLUMNS, (c + 1) * COLUMNS)
                    picked = dot(hits[i], source[i, :, columns]).astype(BF16)
                    for e in range(local_experts):
                        target[e, i * slot_rows : (i + 1) * slot_rows, columns] = picked[
                            e * slot_rows : (e + 1) * slot_rows
                        ]
        for copy in save_copies():
            copy.start()

    gate_slot = gate_slots[step]
    gate_pre = dot(xs_all[step], gate_ref[0])
    up_pre = dot(xs_all[step], up_ref[0])
    raw_grad = dot(cs_all[step], down_ref[0])
    sigmoid = 1.0 / (1.0 + jnp.exp(-gate_pre))
    active = gate_pre * sigmoid
    expert_hidden = (active * up_pre).astype(BF16).astype(F32)
    hs_ref[0] = (expert_hidden * gate_slot).astype(BF16)
    back_slot = jnp.sum(expert_hidden * raw_grad, axis=-1, keepdims=True) * RESIDUAL_SCALE
    hidden_grad = raw_grad * gate_slot
    gate_grad_ref[0] = (hidden_grad * up_pre * sigmoid * (1.0 + gate_pre * (1.0 - sigmoid))).astype(BF16)
    up_grad_ref[0] = (hidden_grad * active).astype(BF16)
    spot = pl.ds(pl.multiple_of(step * slot_rows, slot_rows), slot_rows)
    for c in range(width // COLUMNS):
        columns = slice(c * COLUMNS, (c + 1) * COLUMNS)
        slot_grad = (
            dot(gate_grad_ref[0], gate_ref[0, columns, :], NT) + dot(up_grad_ref[0], up_ref[0, columns, :], NT)
        ).astype(BF16)
        for i in range(blocks):
            slot_grads[i, spot, columns] = slot_grad[i * slot_rows : (i + 1) * slot_rows]
    for i in range(blocks):
        part = slice(i * slot_rows, (i + 1) * slot_rows)
        back_row = jnp.sum(hits[i, spot, :].astype(F32) * back_slot[part], axis=0, keepdims=True)
        back[i, mine, :] = back_row * gates[i, mine, :]

    @pl.when(step == local_experts - 1)
    def _():
        def copy(i):
            return pltpu.make_async_copy(
                c_all.at[i, :, pl.ds(0, width)], grad_out.at[place_ref[1 + blocks + i]], out_sem.at[i]
            )

        router_sum = None
        for i in range(blocks):
            share = back[i]
            logit_grad = (share - gates[i] * jnp.sum(share, axis=0, keepdims=True)).astype(BF16)
            turned = hits[i].T
            for c in range(width // COLUMNS):
                columns = slice(c * COLUMNS, (c + 1) * COLUMNS)
                c_all[i, :, columns] = (
                    dot(turned, slot_grads[i, :, columns]) + dot(logit_grad, router_ref[:, columns], TN)
                ).astype(BF16)
            copy(i).start()
            part = dot(logit_grad, x_all[i])
            router_sum = part if router_sum is None else router_sum + part
        router_grad_ref[...] = router_sum
        for i in range(blocks):
            copy(i).wait()
        for saved in save_copies():
            saved.wait()


def run_experts(place, router_t, gate_weight, up_weight, down_weight, normed, cots, slot_rows):
    local_experts, width, hidden = gate_weight.shape
    sources = len(normed)
    blocks = (sources + 1) // 2
    rows = normed[0].shape[0]
    expert_pad = router_t.shape[0]
    slots = blocks * slot_rows
    stacked = local_experts * slot_rows
    anywhere = pl.BlockSpec(memory_space=pl.ANY)
    weight_spec = pl.BlockSpec((1, width, hidden), lambda e, place: (e, 0, 0))
    narrow = pl.BlockSpec((1, slots, hidden), lambda e, place: (e, 0, 0))
    wide_shape = jax.ShapeDtypeStruct((local_experts, slots, width), BF16)
    narrow_shape = jax.ShapeDtypeStruct((local_experts, slots, hidden), BF16)
    out = pl.pallas_call(
        functools.partial(expert_kernel, blocks, slot_rows, local_experts),
        out_shape=(
            wide_shape,
            wide_shape,
            narrow_shape,
            narrow_shape,
            narrow_shape,
            jax.ShapeDtypeStruct((blocks, stacked, rows), BF16),
            jax.ShapeDtypeStruct((blocks, rows, width), BF16),
            jax.ShapeDtypeStruct((expert_pad, width), F32),
        ),
        grid_spec=pltpu.PrefetchScalarGridSpec(
            num_scalar_prefetch=1,
            grid=(local_experts,),
            in_specs=[pl.BlockSpec((expert_pad, width), lambda e, place: (0, 0))]
            + [weight_spec] * 3
            + [anywhere] * (2 * sources),
            out_specs=(
                anywhere,
                anywhere,
                narrow,
                narrow,
                narrow,
                pl.BlockSpec((blocks, stacked, rows), lambda e, place: (0, 0, 0)),
                anywhere,
                pl.BlockSpec((expert_pad, width), lambda e, place: (0, 0)),
            ),
            scratch_shapes=[
                pltpu.VMEM((blocks, rows, width), BF16),
                pltpu.VMEM((blocks, rows, width + LANES), BF16),
                pltpu.VMEM((blocks, LANES, rows), F32),
                pltpu.VMEM((blocks, expert_pad, rows), F32),
                pltpu.VMEM((blocks, expert_pad, rows), F32),
                pltpu.VMEM((local_experts, slots, width), BF16),
                pltpu.VMEM((local_experts, slots, width), BF16),
                pltpu.VMEM((local_experts, slots, 1), F32),
                pltpu.VMEM((blocks, stacked, width), BF16),
                pltpu.SemaphoreType.DMA((2, blocks)),
                pltpu.SemaphoreType.DMA((2,)),
                pltpu.SemaphoreType.DMA((blocks,)),
            ],
        ),
        compiler_params=params(),
        cost_estimate=cost(45),
        name="experts",
    )(place, router_t, gate_weight, up_weight, down_weight, *normed, *cots)
    return out[:6], out[6], out[7]


def mixture_kernel(blocks, slot_rows, local_experts, order_ref, down_ref, hs_ref, hits_ref, mix_one, mix_two, slot_outs, mix_low, out_sem):
    step = pl.program_id(0)
    width = down_ref.shape[1]
    spot = pl.ds(pl.multiple_of(step * slot_rows, slot_rows), slot_rows)
    for c in range(width // COLUMNS):
        columns = slice(c * COLUMNS, (c + 1) * COLUMNS)
        slot_out = dot(hs_ref[0], down_ref[0, columns, :], NT).astype(BF16)
        for i in range(blocks):
            slot_outs[i, spot, columns] = slot_out[i * slot_rows : (i + 1) * slot_rows]

    @pl.when(step == local_experts - 1)
    def _():
        def copy(i, h):
            columns = pl.ds(h * (width // 2), width // 2)
            return pltpu.make_async_copy(
                mix_low.at[i, :, columns], (mix_one, mix_two)[h].at[order_ref[i]], out_sem.at[i, h]
            )

        for i in range(blocks):
            turned = hits_ref[i].T
            for c in range(width // COLUMNS):
                columns = slice(c * COLUMNS, (c + 1) * COLUMNS)
                mix_low[i, :, columns] = dot(turned, slot_outs[i, :, columns]).astype(BF16)
            for h in range(2):
                copy(i, h).start()
        for i in range(blocks):
            for h in range(2):
                copy(i, h).wait()


def run_mixture(order, down_weight, saved, slot_rows):
    hs, hits = saved[2], saved[5]
    local_experts, width, hidden = down_weight.shape
    blocks, stacked, rows = hits.shape
    return pl.pallas_call(
        functools.partial(mixture_kernel, blocks, slot_rows, local_experts),
        out_shape=(jax.ShapeDtypeStruct((blocks, rows, width // 2), BF16),) * 2,
        grid_spec=pltpu.PrefetchScalarGridSpec(
            num_scalar_prefetch=1,
            grid=(local_experts,),
            in_specs=[
                pl.BlockSpec((1, width, hidden), lambda e, order: (e, 0, 0)),
                pl.BlockSpec((1, hs.shape[1], hidden), lambda e, order: (e, 0, 0)),
                pl.BlockSpec((blocks, stacked, rows), lambda e, order: (0, 0, 0)),
            ],
            out_specs=(pl.BlockSpec(memory_space=pl.ANY),) * 2,
            scratch_shapes=[
                pltpu.VMEM((blocks, stacked, width), BF16),
                pltpu.VMEM((blocks, rows, width), BF16),
                pltpu.SemaphoreType.DMA((blocks, 2)),
            ],
        ),
        compiler_params=params(),
        cost_estimate=cost(10),
        name="mixture",
    )(order, down_weight, hs, hits)


def turn_rows(block, sides_ref, owned):
    width = block.shape[1]
    chunk = int(np.lcm(2 * owned, LANES))
    for c in range(width // chunk):
        turned = block[:, c * chunk : (c + 1) * chunk].T
        for o in range(chunk // owned):
            owner = c * (chunk // owned) + o
            spot = owner // 2 * owned
            sides_ref[owner % 2, spot : spot + owned, :] = turned[o * owned : (o + 1) * owned]


def grad_products(side, xs_ref, cs_ref, hs_ref, gate_grad_ref, up_grad_ref, sides, owned):
    for left_ref, rights in ((xs_ref, ((0, gate_grad_ref), (1, up_grad_ref))), (cs_ref, ((2, hs_ref),))):
        turn_rows(left_ref[0], sides, owned)
        for w, right_ref in rights:
            yield w, dot(sides[side], right_ref[0])


def expert_send_kernel(place_ref, xs_ref, cs_ref, hs_ref, gate_grad_ref, up_grad_ref, *refs):
    send_refs, sides = refs[:-1], refs[-1]
    owned = send_refs[0].shape[2]
    side = 1 - place_ref[0] % 2
    for w, grad in grad_products(side, xs_ref, cs_ref, hs_ref, gate_grad_ref, up_grad_ref, sides, owned):
        for q, send_ref in enumerate(send_refs):
            send_ref[w, 0] = grad[q * owned : (q + 1) * owned].astype(BF16)


def expert_keep_kernel(bits, place_ref, xs_ref, cs_ref, hs_ref, gate_grad_ref, up_grad_ref, *refs):
    count = 1 << (bits - 1)
    received_refs, outs, sides = refs[:count], refs[count : count + 4], refs[-1]
    owned = received_refs[0].shape[2]
    hidden = hs_ref.shape[2] // 2
    side = place_ref[0] % 2
    for w, grad in grad_products(side, xs_ref, cs_ref, hs_ref, gate_grad_ref, up_grad_ref, sides, owned):
        for q in range(count):
            piece = (grad[q * owned : (q + 1) * owned] + received_refs[q][w, 0].astype(F32)).astype(BF16)
            for route, bit in enumerate((1, bits - 1)):
                part = piece[:, route * hidden : (route + 1) * hidden]
                own = (place_ref[0] >> bit) & 1
                spot = (q >> bit << (bit - 1)) | (q & ((1 << (bit - 1)) - 1))
                here = q >> (bit - 1) & 1

                @pl.when(own == here)
                def _(route=route, part=part, spot=spot, w=w):
                    outs[2 * route][spot, w, 0] = part

                @pl.when(own != here)
                def _(route=route, part=part, spot=spot, w=w):
                    outs[2 * route + 1][spot, w, 0] = part


def run_expert_grads(dp_word, saved, owners, received=()):
    xs, cs, hs, gate_grad, up_grad, _ = saved
    local_experts, slots, width = xs.shape
    hidden = hs.shape[2]
    owned = width // owners
    wide = pl.BlockSpec((1, slots, width), lambda e, place: (e, 0, 0))
    narrow = pl.BlockSpec((1, slots, hidden), lambda e, place: (e, 0, 0))
    pass_spec = pl.BlockSpec((3, 1, owned, hidden), lambda e, place: (0, e, 0, 0))
    pass_shape = jax.ShapeDtypeStruct((3, local_experts, owned, hidden), BF16)
    part_spec = pl.BlockSpec((owners // 4, 3, 1, owned, hidden // 2), lambda e, place: (0, 0, e, 0, 0))
    part_shape = jax.ShapeDtypeStruct((owners // 4, 3, local_experts, owned, hidden // 2), BF16)
    return pl.pallas_call(
        functools.partial(expert_keep_kernel, owners.bit_length() - 1) if received else expert_send_kernel,
        out_shape=(part_shape,) * 4 if received else (pass_shape,) * (owners // 2),
        grid_spec=pltpu.PrefetchScalarGridSpec(
            num_scalar_prefetch=1,
            grid=(local_experts,),
            in_specs=[wide, wide, narrow, narrow, narrow] + [pass_spec] * len(received),
            out_specs=(part_spec,) * 4 if received else (pass_spec,) * (owners // 2),
            scratch_shapes=[pltpu.VMEM((2, width // 2, slots), BF16)],
        ),
        compiler_params=params(),
        cost_estimate=cost(15),
        name="expert_keep" if received else "expert_send",
    )(dp_word, xs, cs, hs, gate_grad, up_grad, *received)


def dense_grad_kernel(pairs, place_ref, *refs):
    lefts, rights = refs[:pairs], refs[pairs : 2 * pairs]
    smalls = refs[2 * pairs : -3]
    keep_ref, send_ref, sides = refs[-3:]
    owned = keep_ref.shape[1]
    bit = place_ref[0] % 2
    column = 0
    for i in range(pairs):
        if i == 0 or lefts[i] is not lefts[i - 1]:
            turn_rows(lefts[i][...], sides, owned)
        columns = rights[i].shape[1]
        for out_ref, side in ((send_ref, 1 - bit), (keep_ref, bit)):
            grad = dot(sides[side], rights[i][...]).astype(BF16)
            for q in range(keep_ref.shape[0]):
                out_ref[q, :, column : column + columns] = grad[q * owned : (q + 1) * owned]
        column += columns
    if smalls:
        rows = jnp.concatenate([ref[...] for ref in smalls], axis=0)
        rows = jnp.concatenate([rows, jnp.zeros((LANES - rows.shape[0], rows.shape[1]), F32)], axis=0)
        turned = rows.T.astype(BF16)
        for owner in range(2 * keep_ref.shape[0]):
            piece = turned[owner * owned : (owner + 1) * owned]

            @pl.when(bit == owner % 2)
            def _(owner=owner, piece=piece):
                keep_ref[owner // 2, :, column:] = piece

            @pl.when(bit != owner % 2)
            def _(owner=owner, piece=piece):
                send_ref[owner // 2, :, column:] = piece


def dense_grads(dp_word, pairs, owners, smalls=()):
    rows, width = pairs[0][0].shape
    columns = sum(right.shape[1] for _, right in pairs) + (LANES if smalls else 0)
    return pl.pallas_call(
        functools.partial(dense_grad_kernel, len(pairs)),
        out_shape=(jax.ShapeDtypeStruct((owners // 2, width // owners, columns), BF16),) * 2,
        in_specs=[pl.BlockSpec(memory_space=pltpu.SMEM)] + [vmem()] * (2 * len(pairs) + len(smalls)),
        out_specs=(vmem(),) * 2,
        scratch_shapes=[pltpu.VMEM((2, width // 2, rows), BF16)],
        compiler_params=params(),
        cost_estimate=cost(4),
        name="dense_grads",
    )(dp_word, *(left for left, _ in pairs), *(right for _, right in pairs), *smalls)


def line_up(value, size):
    return lax.ppermute(value, "expert", [(i, i + 1) for i in range(size - 1)])


def line_down(value, size):
    return lax.ppermute(value, "expert", [(i + 1, i) for i in range(size - 1)])


def line_gather(value, size):
    below, above = [], []
    up, down = value, value
    for _ in range(size - 1):
        up = line_up(up, size)
        down = line_down(down, size)
        below.append(up)
        above.append(down)
    return [value] + below + above


def add_low(*terms):
    total = terms[0].astype(F32)
    for term in terms[1:]:
        total = total + term.astype(F32)
    return total.astype(BF16)


def flip(value, bit, size):
    return lax.ppermute(value, "dp", [(i, i ^ bit) for i in range(size)])


def halve(terms, bit, left, dp_place):
    axis = left.index(bit)
    own = (dp_place >> bit) & 1
    return tuple(
        add_low(*(lax.dynamic_index_in_dim(t, side, axis, keepdims=False) for t in terms)) for side in (own, 1 - own)
    )


def start_spread(routes):
    return [
        tuple(t.reshape((2,) * (t.shape[0].bit_length() - 1) + t.shape[1:]) for t in terms) for terms in routes
    ]


def step_spread(routes, stage, dp_size, dp_place):
    bits = list(range(1, dp_size.bit_length() - 1))
    kept, sent = [], []
    for terms, order in zip(routes, (bits, bits[::-1])):
        left = [bit for bit in bits[::-1] if bit not in order[:stage]]
        keep, send = halve(terms, order[stage], left, dp_place)
        kept.append(keep)
        sent.append(flip(send, 1 << order[stage], dp_size))
    sent = lax.optimization_barrier(tuple(sent))
    return list(zip(kept, sent))


def start_dense(terms):
    half = terms[0].shape[2] // 2 // LANES * LANES
    return start_spread([tuple(t[..., :half] for t in terms), tuple(t[..., half:] for t in terms)])


def finish_dense(routes, place, size):
    block = jnp.concatenate([add_low(*terms) for terms in routes], axis=-1)
    parts = block.reshape(size, -1, block.shape[-1])
    total = lax.dynamic_index_in_dim(parts, place, 0, keepdims=False).astype(F32)
    passed = []
    for k in range(1, size):
        part = lax.dynamic_index_in_dim(parts, (place + k) % size, 0, keepdims=False)
        passed.append(lax.ppermute(part, "expert", [(i, (i + k) % size) for i in range(size)]))
    for part in lax.optimization_barrier(tuple(passed)):
        total = total + part.astype(F32)
    return total


def reduce_top(top, dp_size, size):
    for bit in range(dp_size.bit_length() - 1):
        top = jnp.maximum(top, flip(top, 1 << bit, dp_size))
    for bit in range(size.bit_length() - 1):
        top = jnp.maximum(top, lax.ppermute(top, "expert", [(i, i ^ (1 << bit)) for i in range(size)]))
    return top


def arrival_order(size):
    sources, places = np.zeros((size, size), np.int32), np.zeros((size, size), np.int32)
    for place in range(size):
        spots = [(0, place)]
        for k in range(1, size):
            if place - k >= 0:
                spots.append((k, place - k))
            if place + k < size:
                spots.append((size - 1 + k, place + k))
        sources[place], places[place] = zip(*spots)
    return sources, places


def norm_backward(hidden, factor, gain_vec, grad_in):
    scaled = grad_in * gain_vec
    hidden_grad = factor * scaled - hidden * factor**3 * jnp.mean(
        scaled * hidden, axis=-1, keepdims=True
    )
    return hidden_grad, jnp.sum(grad_in * hidden * factor, axis=0)


def local(
    tokens,
    first_gain,
    query_weight,
    key_weight,
    value_weight,
    output_weight,
    second_gain,
    router_weight,
    gate_weight,
    up_weight,
    down_weight,
    cotangent,
    routes,
    segments,
    threshold,
):
    rows, width = tokens.shape
    query_width, kv_width = query_weight.shape[1], key_weight.shape[1]
    heads, groups = query_width // HDIM, kv_width // HDIM
    ratio = heads // groups
    local_experts = gate_weight.shape[0]
    size, dp_size = lax.axis_size("expert"), lax.axis_size("dp")
    place, dp_place = lax.axis_index("expert"), lax.axis_index("dp")
    experts = local_experts * size
    expert_pad = round_up(experts, 16)
    capacity = rows * routes.shape[1] * 9 // (experts * 8)
    slot_rows = round_up(capacity, 64)

    tables = tuple(
        lax.dynamic_slice_in_dim(jnp.asarray(table), place * rows, rows, 0) for table in rotary_tables(rows * size)
    )
    seg_block = jnp.pad(segments.reshape(rows // LANES, LANES).astype(BF16), ((0, 16 - rows // LANES), (0, 0)))

    normed, first_factor, kv_own = pl.pallas_call(
        front_kernel,
        out_shape=(
            jax.ShapeDtypeStruct((rows, width), BF16),
            jax.ShapeDtypeStruct((rows, 1), F32),
            jax.ShapeDtypeStruct((groups * rows + 16, LANES), BF16),
        ),
        in_specs=[vmem()] * 7,
        out_specs=(vmem(),) * 3,
        compiler_params=params(),
        cost_estimate=cost(4),
        name="front",
    )(tokens, first_gain.reshape(1, width), key_weight, value_weight, *tables, seg_block)
    kv_slots = [kv_own]
    for _ in range(size - 1):
        kv_slots.append(line_up(kv_slots[-1], size))

    cot_own = pl.pallas_call(
        extend_kernel,
        out_shape=jax.ShapeDtypeStruct((rows, width + LANES), BF16),
        in_specs=[vmem()] * 2,
        out_specs=vmem(),
        compiler_params=params(),
        cost_estimate=cost(2),
        name="extend",
    )(cotangent, routes)
    cots = line_gather(cot_own, size)

    query_block = 512
    queries = pl.pallas_call(
        query_kernel,
        out_shape=jax.ShapeDtypeStruct((rows, query_width), BF16),
        grid=(query_width // query_block,),
        in_specs=[
            pl.BlockSpec((rows, width), lambda s: (0, 0)),
            pl.BlockSpec((width, query_block), lambda s: (0, s)),
            pl.BlockSpec((rows, LANES), lambda s: (0, 0)),
            pl.BlockSpec((rows, LANES), lambda s: (0, 0)),
        ],
        out_specs=pl.BlockSpec((rows, query_block), lambda s: (0, s)),
        compiler_params=params(),
        cost_estimate=cost(5),
        name="queries",
    )(normed, query_weight, *tables)

    place_word = place.reshape(1).astype(jnp.int32)
    attended, lse, top = attend(queries, kv_slots, place_word, groups)
    head_top = jnp.max(top.reshape(heads, rows), axis=1).reshape(1, heads)
    head_top = reduce_top(head_top, dp_size, size).reshape(heads)

    hidden_in = tokens.astype(F32)
    hidden_mid = hidden_in + RESIDUAL_SCALE * dot(attended, output_weight, NT)
    second_factor = lax.rsqrt(jnp.mean(hidden_mid * hidden_mid, axis=-1, keepdims=True) + NORM_EPSILON)
    second_normed = (hidden_mid * second_factor * second_gain).astype(BF16)
    normed_blocks = line_gather(second_normed, size)

    router_t = jnp.pad(router_weight.T, ((0, expert_pad - experts), (0, 0)))
    sources, blocks_of = (jnp.asarray(table)[place] for table in arrival_order(size))
    expert_place = jnp.concatenate([(place * local_experts).reshape(1), sources, blocks_of]).astype(jnp.int32)
    expert_place, head_top = lax.optimization_barrier((expert_place, head_top))
    saved, grad_blocks, router_part = run_experts(
        expert_place, router_t, gate_weight, up_weight, down_weight, normed_blocks, cots, slot_rows
    )
    grad_blocks = lax.all_to_all(grad_blocks, "expert", 0, 0, tiled=True)

    dp_word = dp_place.reshape(1).astype(jnp.int32)
    mixture = run_mixture(blocks_of, down_weight, saved, slot_rows)
    received = [flip(part, 1, dp_size) for part in run_expert_grads(dp_word, saved, dp_size)]
    keep_a, send_a, keep_b, send_b = run_expert_grads(dp_word, saved, dp_size, received)
    mixture, grad_blocks, send_a, send_b = lax.optimization_barrier((mixture, grad_blocks, send_a, send_b))
    normed_grad = jnp.sum(grad_blocks.astype(F32), axis=0)
    passed = (flip(send_a, 2, dp_size), flip(send_b, dp_size // 2, dp_size))
    mix_one = lax.all_to_all(mixture[0], "expert", 0, 0, tiled=True)

    out_grad = cotangent.astype(F32)
    mid_back, second_gain_part = norm_backward(hidden_mid, second_factor, second_gain, normed_grad)
    mid_grad = out_grad + mid_back
    branch_grad = (RESIDUAL_SCALE * mid_grad).astype(BF16)
    attended_grad = dot(branch_grad, output_weight).astype(BF16)
    query_back, dkv = attend_back(
        queries, attended, attended_grad, lse, tables, kv_slots, place_word, groups
    )
    keep, send = dense_grads(dp_word, [(branch_grad, attended), (normed, query_back)], dp_size)
    stages = dp_size.bit_length() - 2
    down, passed, mix_one, keep, send = lax.optimization_barrier((dkv[size - 1], passed, mix_one, keep, send))
    expert_sums = step_spread(start_spread([(keep_a, passed[0]), (keep_b, passed[1])]), 1, dp_size, dp_place)
    wide = start_dense((keep, flip(send, 1, dp_size)))
    for k in range(1, size):
        from_above = line_down(down, size)
        if k == size - 2:
            from_above, wide = lax.optimization_barrier((from_above, wide))
        if k < size - 1:
            down = add_low(from_above, dkv[size - 1 - k])
    from_above, expert_sums, mix_two = lax.optimization_barrier((from_above, expert_sums, mixture[1]))
    mix_two = lax.all_to_all(mix_two, "expert", 0, 0, tiled=True)
    for stage in range(2, stages):
        expert_sums = step_spread(expert_sums, stage, dp_size, dp_place)
    expert_sums = [
        jnp.concatenate([a[w].astype(F32) + b[w].astype(F32) for a, b in expert_sums], axis=-1) for w in range(3)
    ]
    for stage in range(stages):
        wide = step_spread(wide, stage, dp_size, dp_place)
    key_back, value_back = pl.pallas_call(
        unpack_kernel,
        out_shape=(jax.ShapeDtypeStruct((rows, kv_width), BF16),) * 2,
        in_specs=[vmem()] * 4,
        out_specs=(vmem(),) * 2,
        compiler_params=params(),
        cost_estimate=cost(2),
        name="unpack",
    )(dkv[0], from_above, *tables)

    first_grad = dot(query_back, query_weight, NT)
    first_grad = first_grad + dot(key_back, key_weight, NT)
    first_grad = first_grad + dot(value_back, value_weight, NT)
    input_back, first_gain_part = norm_backward(hidden_in, first_factor, first_gain, first_grad)
    input_grad = mid_grad + input_back
    keep, send = dense_grads(
        dp_word,
        [(normed, key_back), (normed, value_back)],
        dp_size,
        (router_part, second_gain_part[None], first_gain_part[None]),
    )
    keep, send, wide = lax.optimization_barrier((keep, send, wide))
    rest = start_dense((keep, flip(send, 1, dp_size)))
    for stage in range(stages):
        rest = step_spread(rest, stage, dp_size, dp_place)
    wide_grad, rest_grad = finish_dense(wide, place, size), finish_dense(rest, place, size)
    mixture = jnp.concatenate([jnp.sum(part.astype(F32), axis=0) for part in (mix_one, mix_two)], axis=1)
    block_out = (hidden_mid + mixture).astype(BF16)
    projection_grad, query_grad = wide_grad[:, :query_width], wide_grad[:, query_width:]
    key_grad = rest_grad[:, :kv_width]
    value_grad = rest_grad[:, kv_width : 2 * kv_width]
    small_grad = rest_grad[:, 2 * kv_width :]

    head_scale = threshold / jnp.maximum(head_top, threshold)
    group_scale = jnp.min(head_scale.reshape(groups, ratio), axis=1)
    row_count = width // (dp_size * size)
    row_start = (dp_place * size + place) * row_count
    query_rows = lax.dynamic_slice_in_dim(query_weight, row_start, row_count, 0).astype(F32)
    key_rows = lax.dynamic_slice_in_dim(key_weight, row_start, row_count, 0).astype(F32)
    query_clipped = (query_rows * jnp.repeat(jnp.sqrt(head_scale), HDIM)[None, :]).astype(BF16)
    key_clipped = (key_rows * jnp.repeat(jnp.sqrt(group_scale), HDIM)[None, :]).astype(BF16)
    return (
        block_out,
        input_grad,
        small_grad[:, expert_pad + 1],
        query_grad,
        key_grad,
        value_grad,
        projection_grad,
        small_grad[:, expert_pad],
        small_grad[:, :experts],
        expert_sums[0],
        expert_sums[1],
        expert_sums[2],
        head_scale,
        query_clipped,
        key_clipped,
    )


def solution(mesh):
    row = P(("dp", "expert"), None)
    vector = P(("dp", "expert"))
    expert_in = P("expert", None, None)
    expert_out = P("expert", "dp", None)
    return jax.shard_map(
        local,
        mesh=mesh,
        in_specs=(row,) + (P(),) * 7 + (expert_in,) * 3 + (row, row, vector, P()),
        out_specs=(row, row, vector)
        + (row,) * 4
        + (vector, row)
        + (expert_out,) * 3
        + (P(), row, row),
        check_vma=False,
    )
```

```python
import functools

import jax
import jax.numpy as jnp
import numpy as np
from jax import lax
from jax.experimental import pallas as pl
from jax.experimental.pallas import tpu as pltpu
from jax.sharding import PartitionSpec as P

HDIM = 64
LANES = 128
ATTENTION_SCALE = 0.015625
RESIDUAL_SCALE = 0.22
NORM_EPSILON = 1e-06
ROTARY_BASE = 10000.0
MASKED_SCORE = -1e30
BF16 = jnp.bfloat16
F32 = jnp.float32
NN = (((1,), (0,)), ((), ()))
NT = (((1,), (1,)), ((), ()))
TN = (((0,), (0,)), ((), ()))
VMEM_LIMIT = 60 * 1024 * 1024
COLUMNS = 512


def dot(left, right, dims=NN):
    return lax.dot_general(left, right, dims, preferred_element_type=F32)


def round_up(count, unit):
    return (count + unit - 1) // unit * unit


def low_lanes(rows):
    return lax.broadcasted_iota(jnp.int32, (rows, LANES), 1) < HDIM


def partner_lanes(slab):
    lane = lax.broadcasted_iota(jnp.int32, slab.shape, 1) % HDIM
    half = HDIM // 2
    return jnp.where(lane < half, pltpu.roll(slab, LANES - half, 1), pltpu.roll(slab, half, 1))


def vmem():
    return pl.BlockSpec(memory_space=pltpu.VMEM)


def params(**more):
    return pltpu.CompilerParams(vmem_limit_bytes=VMEM_LIMIT, **more)


def cost(microseconds):
    return pl.CostEstimate(flops=int(microseconds * 1e6), bytes_accessed=0, transcendentals=0)


def rotary_tables(length):
    half = HDIM // 2
    inverse = np.float32(ROTARY_BASE) ** (np.float32(-2.0) * np.arange(half, dtype=np.float32) / np.float32(HDIM))
    angles = np.arange(length, dtype=np.float32)[:, None] * np.tile(inverse, LANES // half)[None, :]
    angles = angles.astype(np.float32).astype(np.float64)
    sign = np.where(np.arange(LANES) % HDIM < half, -1.0, 1.0)
    return np.cos(angles).astype(np.float32), (np.sin(angles) * sign).astype(np.float32)


def extend_kernel(cotangent_ref, routes_ref, out_ref):
    rows, top_count = routes_ref.shape
    width = cotangent_ref.shape[1]
    lane = lax.broadcasted_iota(jnp.int32, (rows, LANES), 1)
    chosen = jnp.zeros((rows, LANES), F32)
    for k in range(top_count):
        chosen = chosen + jnp.where(routes_ref[:, k : k + 1] == lane, 1.0, 0.0)
    first = lax.broadcasted_iota(jnp.int32, (rows, rows), 0)
    second = lax.broadcasted_iota(jnp.int32, (rows, rows), 1)
    earlier = jnp.where(second < first, 1.0, 0.0).astype(BF16)
    rank = dot(earlier, chosen.astype(BF16))
    out_ref[:, :width] = cotangent_ref[...]
    out_ref[:, width:] = jnp.where(chosen > 0.5, rank, -1.0).astype(BF16)


def front_kernel(tokens_ref, gain_ref, key_ref, value_ref, cos_ref, sin_ref, segments_ref, normed_ref, factor_ref, kv_ref):
    hidden = tokens_ref[...].astype(F32)
    factor = lax.rsqrt(jnp.mean(hidden * hidden, axis=-1, keepdims=True) + NORM_EPSILON)
    normed = (hidden * factor * gain_ref[...]).astype(BF16)
    normed_ref[...] = normed
    factor_ref[...] = factor
    keys = dot(normed, key_ref[...])
    values = dot(normed, value_ref[...])
    cosine, sine = cos_ref[...], sin_ref[...]
    rows = hidden.shape[0]
    low = low_lanes(rows)
    for i in range(keys.shape[1] // LANES):
        slab = keys[:, i * LANES : (i + 1) * LANES]
        slab = slab * cosine + partner_lanes(slab) * sine
        value_slab = values[:, i * LANES : (i + 1) * LANES]
        even, odd = 2 * i * rows, (2 * i + 1) * rows
        kv_ref[even : even + rows, :] = jnp.where(low, slab, pltpu.roll(value_slab, HDIM, 1)).astype(BF16)
        kv_ref[odd : odd + rows, :] = jnp.where(low, pltpu.roll(slab, HDIM, 1), value_slab).astype(BF16)
    kv_ref[keys.shape[1] // HDIM * rows :, :] = segments_ref[...]


def query_kernel(normed_ref, query_ref, cos_ref, sin_ref, out_ref):
    raw = dot(normed_ref[...], query_ref[...])
    cosine, sine = cos_ref[...], sin_ref[...]
    for i in range(raw.shape[1] // LANES):
        slab = raw[:, i * LANES : (i + 1) * LANES]
        slab = slab * cosine + partner_lanes(slab) * sine
        out_ref[:, i * LANES : (i + 1) * LANES] = (slab.astype(BF16).astype(F32) * ATTENTION_SCALE).astype(BF16)


def fill_bias(bias_ref, need_ref, place_ref, seg_row, seg_columns):
    slots, keys, rows = bias_ref.shape
    for k in range(slots):
        allowed = seg_columns[k] == seg_row
        if k == 0:
            allowed = allowed & (
                lax.broadcasted_iota(jnp.int32, (keys, rows), 0) <= lax.broadcasted_iota(jnp.int32, (keys, rows), 1)
            )
        bias_ref[k] = jnp.where(allowed, 0.0, MASKED_SCORE)
    first = jnp.min(seg_row)
    need = jnp.int32(1)
    for k in range(1, slots):
        need = jnp.where((jnp.max(seg_columns[k]) >= first) & (k <= place_ref[0]), k + 1, need)
    need_ref[0] = need


def prepare_bias(bias_ref, need_ref, place_ref, seg_refs):
    slots, keys, _ = bias_ref.shape
    halves = keys // LANES
    seg_rows = [
        jnp.concatenate([ref[j : j + 1, :].astype(F32) for j in range(halves)], axis=1) for ref in seg_refs
    ]
    seg_columns = [jnp.broadcast_to(row, (LANES, keys)).T[:, :1] for row in seg_rows]
    fill_bias(bias_ref, need_ref, place_ref, seg_rows[0], seg_columns)


def head_slab(block, head, upper):
    slab = block[:, (head // 2) * LANES : (head // 2 + 1) * LANES].astype(F32)
    low = low_lanes(slab.shape[0])
    if (head % 2 == 1) != upper:
        slab = pltpu.roll(slab, HDIM, 1)
    return jnp.where(low != upper, slab, 0.0)


def add_bias(scores, bias, ratio):
    rows = bias.shape[1]
    return jnp.concatenate([scores[:, r * rows : (r + 1) * rows] + bias for r in range(ratio)], axis=1)


def attend_kernel(slots, ratio, place_ref, query_ref, *refs):
    kv_refs, seg_refs = refs[:slots], refs[slots : 2 * slots]
    attended_ref, lse_ref, top_ref, bias_ref, stacked_ref, scores_ref, acc_ref, max_ref, need_ref = refs[2 * slots :]
    rows = query_ref.shape[0]
    low = low_lanes(rows)

    @pl.when(pl.program_id(0) == 0)
    def _():
        prepare_bias(bias_ref, need_ref, place_ref, seg_refs)

    need = need_ref[0]
    outs = []
    for group in range(2):
        for r in range(ratio):
            stacked_ref[r * rows : (r + 1) * rows, :] = head_slab(
                query_ref, group * ratio + r, False
            ).astype(BF16)
        for k in range(slots):

            def score(k=k):
                kv = kv_refs[k][group * rows : (group + 1) * rows, :]
                scores = add_bias(dot(kv, stacked_ref[...], NT), bias_ref[k], ratio)
                scores_ref[k] = scores
                top = jnp.max(scores, axis=0, keepdims=True)
                max_ref[...] = top if k == 0 else jnp.maximum(max_ref[...], top)

            if k == 0:
                score()
            else:
                pl.when(k < need)(score)
        for k in range(slots):

            def mix(k=k):
                kv = kv_refs[k][group * rows : (group + 1) * rows, :]
                kv = jnp.where(low, jnp.ones_like(kv), kv)
                weights = jnp.exp(scores_ref[k] - max_ref[...]).astype(BF16)
                part = dot(kv, weights, TN)
                acc_ref[...] = part if k == 0 else acc_ref[...] + part

            if k == 0:
                mix()
            else:
                pl.when(k < need)(mix)
        total = acc_ref[:1, :]
        lse_ref[0, group : group + 1, :] = max_ref[...] + jnp.log(total)
        top_ref[0, group : group + 1, :] = max_ref[...]
        mixed = acc_ref[HDIM:, :] / total
        for r in range(ratio):
            outs.append(mixed[:, r * rows : (r + 1) * rows])
    for i in range(len(outs) // 2):
        slab = jnp.concatenate([outs[2 * i], outs[2 * i + 1]], axis=0)
        attended_ref[:, i * LANES : (i + 1) * LANES] = slab.T.astype(BF16)


def kv_specs(slots, groups, rows):
    return [pl.BlockSpec((2 * rows, LANES), lambda s: (s, 0))] * slots + [
        pl.BlockSpec((16, LANES), lambda s: (groups * rows // 16, 0))
    ] * slots


def attend(queries, kv_slots, place, groups):
    slots = len(kv_slots)
    rows, width = queries.shape
    ratio = width // HDIM // groups
    steps = groups // 2
    block = 2 * ratio * HDIM
    stats = pl.BlockSpec((1, 2, ratio * rows), lambda s: (s, 0, 0))
    return pl.pallas_call(
        functools.partial(attend_kernel, slots, ratio),
        out_shape=(jax.ShapeDtypeStruct((rows, width), BF16),)
        + (jax.ShapeDtypeStruct((steps, 2, ratio * rows), F32),) * 2,
        grid=(steps,),
        in_specs=[
            pl.BlockSpec(memory_space=pltpu.SMEM),
            pl.BlockSpec((rows, block), lambda s: (0, s)),
        ]
        + kv_specs(slots, groups, rows),
        out_specs=(pl.BlockSpec((rows, block), lambda s: (0, s)), stats, stats),
        scratch_shapes=[
            pltpu.VMEM((slots, rows, rows), F32),
            pltpu.VMEM((ratio * rows, LANES), BF16),
            pltpu.VMEM((slots, rows, ratio * rows), F32),
            pltpu.VMEM((LANES, ratio * rows), F32),
            pltpu.VMEM((1, ratio * rows), F32),
            pltpu.SMEM((1,), jnp.int32),
        ],
        compiler_params=params(),
        cost_estimate=cost(20),
        name="attend",
    )(place, queries, *kv_slots, *kv_slots)


def attend_back_kernel(slots, ratio, place_ref, query_ref, attended_ref, grad_ref, lse_ref, cos_ref, sin_ref, *refs):
    kv_refs, seg_refs = refs[:slots], refs[slots : 2 * slots]
    refs = refs[2 * slots :]
    back_ref, dkv_refs = refs[0], refs[1 : slots + 1]
    bias_ref, query_s, grad_s, acc_ref, delta_s, need_ref = refs[slots + 1 :]
    rows = query_ref.shape[0]

    @pl.when(pl.program_id(0) == 0)
    def _():
        prepare_bias(bias_ref, need_ref, place_ref, seg_refs)

    need = need_ref[0]
    outs = []
    for group in range(2):
        for r in range(ratio):
            head = group * ratio + r
            part = slice(r * rows, (r + 1) * rows)
            query_s[part, :] = head_slab(query_ref, head, False).astype(BF16)
            grad = head_slab(grad_ref, head, True)
            grad_s[part, :] = grad.astype(BF16)
            product = (grad * head_slab(attended_ref, head, True)).T
            delta_s[:, part] = jnp.sum(product, axis=0, keepdims=True)
        for k in range(slots):

            def step(k=k):
                kv = kv_refs[k][group * rows : (group + 1) * rows, :]
                scores = add_bias(dot(kv, query_s[...], NT), bias_ref[k], ratio)
                weights = jnp.exp(scores - lse_ref[0, group : group + 1, :])
                weight_grad = dot(kv, grad_s[...], NT)
                score_grad = (weights * (weight_grad - delta_s[...])).astype(BF16)
                part = dot(kv, score_grad, TN)
                acc_ref[...] = part if k == 0 else acc_ref[...] + part
                dkv_refs[k][group * rows : (group + 1) * rows, :] = (
                    dot(score_grad, query_s[...]) + dot(weights.astype(BF16), grad_s[...])
                ).astype(BF16)

            if k == 0:
                step()
            else:
                pl.when(k < need)(step)

                @pl.when(k >= need)
                def _(k=k):
                    dkv_refs[k][group * rows : (group + 1) * rows, :] = jnp.zeros((rows, LANES), BF16)

        for r in range(ratio):
            outs.append(acc_ref[:HDIM, r * rows : (r + 1) * rows] * ATTENTION_SCALE)
    cosine, sine = cos_ref[...], sin_ref[...]
    for i in range(len(outs) // 2):
        slab = jnp.concatenate([outs[2 * i], outs[2 * i + 1]], axis=0).T
        slab = slab * cosine - partner_lanes(slab) * sine
        back_ref[:, i * LANES : (i + 1) * LANES] = slab.astype(BF16)


def attend_back(queries, attended, grad, lse, tables, kv_slots, place, groups):
    slots = len(kv_slots)
    rows, width = queries.shape
    ratio = width // HDIM // groups
    steps = groups // 2
    block = 2 * ratio * HDIM
    whole = pl.BlockSpec((rows, LANES), lambda s: (0, 0))
    wide = pl.BlockSpec((rows, block), lambda s: (0, s))
    out = pl.pallas_call(
        functools.partial(attend_back_kernel, slots, ratio),
        out_shape=(jax.ShapeDtypeStruct((rows, width), BF16),)
        + (jax.ShapeDtypeStruct((groups * rows, LANES), BF16),) * slots,
        grid=(steps,),
        in_specs=[
            pl.BlockSpec(memory_space=pltpu.SMEM),
            wide,
            wide,
            wide,
            pl.BlockSpec((1, 2, ratio * rows), lambda s: (s, 0, 0)),
            whole,
            whole,
        ]
        + kv_specs(slots, groups, rows),
        out_specs=(wide,) + (pl.BlockSpec((2 * rows, LANES), lambda s: (s, 0)),) * slots,
        scratch_shapes=[
            pltpu.VMEM((slots, rows, rows), F32),
            pltpu.VMEM((ratio * rows, LANES), BF16),
            pltpu.VMEM((ratio * rows, LANES), BF16),
            pltpu.VMEM((LANES, ratio * rows), F32),
            pltpu.VMEM((1, ratio * rows), F32),
            pltpu.SMEM((1,), jnp.int32),
        ],
        compiler_params=params(),
        cost_estimate=cost(2),
        name="attend_back",
    )(place, queries, attended, grad, lse, *tables, *kv_slots, *kv_slots)
    return out[0], out[1:]


def unpack_kernel(own_ref, above_ref, cos_ref, sin_ref, key_ref, value_ref):
    rows = cos_ref.shape[0]
    low = low_lanes(rows)
    cosine, sine = cos_ref[...], sin_ref[...]
    for i in range(key_ref.shape[1] // LANES):
        even, odd = (
            own_ref[g * rows : (g + 1) * rows, :].astype(F32) + above_ref[g * rows : (g + 1) * rows, :].astype(F32)
            for g in (2 * i, 2 * i + 1)
        )
        slab = jnp.where(low, even, pltpu.roll(odd, HDIM, 1))
        slab = slab * cosine - partner_lanes(slab) * sine
        key_ref[:, i * LANES : (i + 1) * LANES] = slab.astype(BF16)
        value_ref[:, i * LANES : (i + 1) * LANES] = jnp.where(
            low, pltpu.roll(even, HDIM, 1), odd
        ).astype(BF16)


def expert_kernel(blocks, slot_rows, local_experts, place_ref, router_ref, gate_ref, up_ref, down_ref, *refs):
    sources = 2 * blocks - 1
    normed_in, cot_in = refs[:sources], refs[sources : 2 * sources]
    xs_out, cs_out, hs_ref, gate_grad_ref, up_grad_ref, hits, grad_out, router_grad_ref = refs[2 * sources : 2 * sources + 8]
    x_all, c_all, info, gates, back, xs_all, cs_all, gate_slots, slot_grads, sems, save_sem, out_sem = refs[2 * sources + 8 :]
    step = pl.program_id(0)
    rows, width = x_all.shape[1:]
    expert_pad = router_ref.shape[0]
    first_expert = place_ref[0]
    mine = pl.ds(first_expert + step, 1)

    def source_copies(i, s):
        return (
            pltpu.make_async_copy(normed_in[s], x_all.at[i], sems.at[0, i]),
            pltpu.make_async_copy(cot_in[s], c_all.at[i], sems.at[1, i]),
        )

    def save_copies():
        return (
            pltpu.make_async_copy(xs_all, xs_out, save_sem.at[0]),
            pltpu.make_async_copy(cs_all, cs_out, save_sem.at[1]),
        )

    @pl.when(step == 0)
    def _():
        for i in range(blocks):
            for s in range(sources):

                @pl.when(place_ref[1 + i] == s)
                def _(i=i, s=s):
                    for copy in source_copies(i, s):
                        copy.start()

        same = jnp.where(
            lax.broadcasted_iota(jnp.int32, (rows, rows), 0) == lax.broadcasted_iota(jnp.int32, (rows, rows), 1),
            1.0,
            0.0,
        ).astype(BF16)
        slot_ids = lax.broadcasted_iota(jnp.int32, (slot_rows, rows), 0).astype(F32)
        back[...] = jnp.zeros_like(back)
        for i in range(blocks):
            for copy in source_copies(i, 0):
                copy.wait()
            info[i] = dot(c_all[i, :, width:], same, TN)
            logits = dot(router_ref[...], x_all[i], NT)
            logits = jnp.where(info[i, :expert_pad, :] >= 0, logits, MASKED_SCORE)
            weights = jnp.exp(logits - jnp.max(logits, axis=0, keepdims=True))
            gates[i] = weights / jnp.sum(weights, axis=0, keepdims=True)
            for e in range(local_experts):
                own = pl.ds(first_expert + e, 1)
                hit = slot_ids == info[i, own, :]
                gate_slots[e, i * slot_rows : (i + 1) * slot_rows, :] = RESIDUAL_SCALE * jnp.sum(
                    jnp.where(hit, gates[i, own, :], 0.0), axis=-1, keepdims=True
                )
                hits[i, e * slot_rows : (e + 1) * slot_rows, :] = jnp.where(hit, 1.0, 0.0).astype(BF16)
            for source, target in ((x_all, xs_all), (c_all, cs_all)):
                for c in range(width // COLUMNS):
                    columns = slice(c * COLUMNS, (c + 1) * COLUMNS)
                    picked = dot(hits[i], source[i, :, columns]).astype(BF16)
                    for e in range(local_experts):
                        target[e, i * slot_rows : (i + 1) * slot_rows, columns] = picked[
                            e * slot_rows : (e + 1) * slot_rows
                        ]
        for copy in save_copies():
            copy.start()

    gate_slot = gate_slots[step]
    gate_pre = dot(xs_all[step], gate_ref[0])
    up_pre = dot(xs_all[step], up_ref[0])
    raw_grad = dot(cs_all[step], down_ref[0])
    sigmoid = 1.0 / (1.0 + jnp.exp(-gate_pre))
    active = gate_pre * sigmoid
    expert_hidden = (active * up_pre).astype(BF16).astype(F32)
    hs_ref[0] = (expert_hidden * gate_slot).astype(BF16)
    back_slot = jnp.sum(expert_hidden * raw_grad, axis=-1, keepdims=True) * RESIDUAL_SCALE
    hidden_grad = raw_grad * gate_slot
    gate_grad_ref[0] = (hidden_grad * up_pre * sigmoid * (1.0 + gate_pre * (1.0 - sigmoid))).astype(BF16)
    up_grad_ref[0] = (hidden_grad * active).astype(BF16)
    spot = pl.ds(pl.multiple_of(step * slot_rows, slot_rows), slot_rows)
    for c in range(width // COLUMNS):
        columns = slice(c * COLUMNS, (c + 1) * COLUMNS)
        slot_grad = (
            dot(gate_grad_ref[0], gate_ref[0, columns, :], NT) + dot(up_grad_ref[0], up_ref[0, columns, :], NT)
        ).astype(BF16)
        for i in range(blocks):
            slot_grads[i, spot, columns] = slot_grad[i * slot_rows : (i + 1) * slot_rows]
    for i in range(blocks):
        part = slice(i * slot_rows, (i + 1) * slot_rows)
        back_row = jnp.sum(hits[i, spot, :].astype(F32) * back_slot[part], axis=0, keepdims=True)
        back[i, mine, :] = back_row * gates[i, mine, :]

    @pl.when(step == local_experts - 1)
    def _():
        def copy(i):
            return pltpu.make_async_copy(
                c_all.at[i, :, pl.ds(0, width)], grad_out.at[place_ref[1 + blocks + i]], out_sem.at[i]
            )

        router_sum = None
        for i in range(blocks):
            share = back[i]
            logit_grad = (share - gates[i] * jnp.sum(share, axis=0, keepdims=True)).astype(BF16)
            turned = hits[i].T
            for c in range(width // COLUMNS):
                columns = slice(c * COLUMNS, (c + 1) * COLUMNS)
                c_all[i, :, columns] = (
                    dot(turned, slot_grads[i, :, columns]) + dot(logit_grad, router_ref[:, columns], TN)
                ).astype(BF16)
            copy(i).start()
            part = dot(logit_grad, x_all[i])
            router_sum = part if router_sum is None else router_sum + part
        router_grad_ref[...] = router_sum
        for i in range(blocks):
            copy(i).wait()
        for saved in save_copies():
            saved.wait()


def run_experts(place, router_t, gate_weight, up_weight, down_weight, normed, cots, slot_rows):
    local_experts, width, hidden = gate_weight.shape
    sources = len(normed)
    blocks = (sources + 1) // 2
    rows = normed[0].shape[0]
    expert_pad = router_t.shape[0]
    slots = blocks * slot_rows
    stacked = local_experts * slot_rows
    anywhere = pl.BlockSpec(memory_space=pl.ANY)
    weight_spec = pl.BlockSpec((1, width, hidden), lambda e, place: (e, 0, 0))
    narrow = pl.BlockSpec((1, slots, hidden), lambda e, place: (e, 0, 0))
    wide_shape = jax.ShapeDtypeStruct((local_experts, slots, width), BF16)
    narrow_shape = jax.ShapeDtypeStruct((local_experts, slots, hidden), BF16)
    out = pl.pallas_call(
        functools.partial(expert_kernel, blocks, slot_rows, local_experts),
        out_shape=(
            wide_shape,
            wide_shape,
            narrow_shape,
            narrow_shape,
            narrow_shape,
            jax.ShapeDtypeStruct((blocks, stacked, rows), BF16),
            jax.ShapeDtypeStruct((blocks, rows, width), BF16),
            jax.ShapeDtypeStruct((expert_pad, width), F32),
        ),
        grid_spec=pltpu.PrefetchScalarGridSpec(
            num_scalar_prefetch=1,
            grid=(local_experts,),
            in_specs=[pl.BlockSpec((expert_pad, width), lambda e, place: (0, 0))]
            + [weight_spec] * 3
            + [anywhere] * (2 * sources),
            out_specs=(
                anywhere,
                anywhere,
                narrow,
                narrow,
                narrow,
                pl.BlockSpec((blocks, stacked, rows), lambda e, place: (0, 0, 0)),
                anywhere,
                pl.BlockSpec((expert_pad, width), lambda e, place: (0, 0)),
            ),
            scratch_shapes=[
                pltpu.VMEM((blocks, rows, width), BF16),
                pltpu.VMEM((blocks, rows, width + LANES), BF16),
                pltpu.VMEM((blocks, LANES, rows), F32),
                pltpu.VMEM((blocks, expert_pad, rows), F32),
                pltpu.VMEM((blocks, expert_pad, rows), F32),
                pltpu.VMEM((local_experts, slots, width), BF16),
                pltpu.VMEM((local_experts, slots, width), BF16),
                pltpu.VMEM((local_experts, slots, 1), F32),
                pltpu.VMEM((blocks, stacked, width), BF16),
                pltpu.SemaphoreType.DMA((2, blocks)),
                pltpu.SemaphoreType.DMA((2,)),
                pltpu.SemaphoreType.DMA((blocks,)),
            ],
        ),
        compiler_params=params(),
        cost_estimate=cost(45),
        name="experts",
    )(place, router_t, gate_weight, up_weight, down_weight, *normed, *cots)
    return out[:6], out[6], out[7]


def mixture_kernel(blocks, slot_rows, local_experts, order_ref, down_ref, hs_ref, hits_ref, mix_one, mix_two, slot_outs, mix_low, out_sem):
    step = pl.program_id(0)
    width = down_ref.shape[1]
    spot = pl.ds(pl.multiple_of(step * slot_rows, slot_rows), slot_rows)
    for c in range(width // COLUMNS):
        columns = slice(c * COLUMNS, (c + 1) * COLUMNS)
        slot_out = dot(hs_ref[0], down_ref[0, columns, :], NT).astype(BF16)
        for i in range(blocks):
            slot_outs[i, spot, columns] = slot_out[i * slot_rows : (i + 1) * slot_rows]

    @pl.when(step == local_experts - 1)
    def _():
        def copy(i, h):
            columns = pl.ds(h * (width // 2), width // 2)
            return pltpu.make_async_copy(
                mix_low.at[i, :, columns], (mix_one, mix_two)[h].at[order_ref[i]], out_sem.at[i, h]
            )

        for i in range(blocks):
            turned = hits_ref[i].T
            for c in range(width // COLUMNS):
                columns = slice(c * COLUMNS, (c + 1) * COLUMNS)
                mix_low[i, :, columns] = dot(turned, slot_outs[i, :, columns]).astype(BF16)
            for h in range(2):
                copy(i, h).start()
        for i in range(blocks):
            for h in range(2):
                copy(i, h).wait()


def run_mixture(order, down_weight, saved, slot_rows):
    hs, hits = saved[2], saved[5]
    local_experts, width, hidden = down_weight.shape
    blocks, stacked, rows = hits.shape
    return pl.pallas_call(
        functools.partial(mixture_kernel, blocks, slot_rows, local_experts),
        out_shape=(jax.ShapeDtypeStruct((blocks, rows, width // 2), BF16),) * 2,
        grid_spec=pltpu.PrefetchScalarGridSpec(
            num_scalar_prefetch=1,
            grid=(local_experts,),
            in_specs=[
                pl.BlockSpec((1, width, hidden), lambda e, order: (e, 0, 0)),
                pl.BlockSpec((1, hs.shape[1], hidden), lambda e, order: (e, 0, 0)),
                pl.BlockSpec((blocks, stacked, rows), lambda e, order: (0, 0, 0)),
            ],
            out_specs=(pl.BlockSpec(memory_space=pl.ANY),) * 2,
            scratch_shapes=[
                pltpu.VMEM((blocks, stacked, width), BF16),
                pltpu.VMEM((blocks, rows, width), BF16),
                pltpu.SemaphoreType.DMA((blocks, 2)),
            ],
        ),
        compiler_params=params(),
        cost_estimate=cost(10),
        name="mixture",
    )(order, down_weight, hs, hits)


def turn_rows(block, sides_ref, owned):
    width = block.shape[1]
    chunk = int(np.lcm(2 * owned, LANES))
    for c in range(width // chunk):
        turned = block[:, c * chunk : (c + 1) * chunk].T
        for o in range(chunk // owned):
            owner = c * (chunk // owned) + o
            spot = owner // 2 * owned
            sides_ref[owner % 2, spot : spot + owned, :] = turned[o * owned : (o + 1) * owned]


def grad_products(side, xs_ref, cs_ref, hs_ref, gate_grad_ref, up_grad_ref, sides, owned):
    for left_ref, rights in ((xs_ref, ((0, gate_grad_ref), (1, up_grad_ref))), (cs_ref, ((2, hs_ref),))):
        turn_rows(left_ref[0], sides, owned)
        for w, right_ref in rights:
            yield w, dot(sides[side], right_ref[0])


def expert_send_kernel(place_ref, xs_ref, cs_ref, hs_ref, gate_grad_ref, up_grad_ref, *refs):
    send_refs, sides = refs[:-1], refs[-1]
    owned = send_refs[0].shape[2]
    side = 1 - place_ref[0] % 2
    for w, grad in grad_products(side, xs_ref, cs_ref, hs_ref, gate_grad_ref, up_grad_ref, sides, owned):
        for q, send_ref in enumerate(send_refs):
            send_ref[w, 0] = grad[q * owned : (q + 1) * owned].astype(BF16)


def expert_keep_kernel(bits, place_ref, xs_ref, cs_ref, hs_ref, gate_grad_ref, up_grad_ref, *refs):
    count = 1 << (bits - 1)
    received_refs, outs, sides = refs[:count], refs[count : count + 4], refs[-1]
    owned = received_refs[0].shape[2]
    hidden = hs_ref.shape[2] // 2
    side = place_ref[0] % 2
    for w, grad in grad_products(side, xs_ref, cs_ref, hs_ref, gate_grad_ref, up_grad_ref, sides, owned):
        for q in range(count):
            piece = (grad[q * owned : (q + 1) * owned] + received_refs[q][w, 0].astype(F32)).astype(BF16)
            for route, bit in enumerate((1, bits - 1)):
                part = piece[:, route * hidden : (route + 1) * hidden]
                own = (place_ref[0] >> bit) & 1
                spot = (q >> bit << (bit - 1)) | (q & ((1 << (bit - 1)) - 1))
                here = q >> (bit - 1) & 1

                @pl.when(own == here)
                def _(route=route, part=part, spot=spot, w=w):
                    outs[2 * route][spot, w, 0] = part

                @pl.when(own != here)
                def _(route=route, part=part, spot=spot, w=w):
                    outs[2 * route + 1][spot, w, 0] = part


def run_expert_grads(dp_word, saved, owners, received=()):
    xs, cs, hs, gate_grad, up_grad, _ = saved
    local_experts, slots, width = xs.shape
    hidden = hs.shape[2]
    owned = width // owners
    wide = pl.BlockSpec((1, slots, width), lambda e, place: (e, 0, 0))
    narrow = pl.BlockSpec((1, slots, hidden), lambda e, place: (e, 0, 0))
    pass_spec = pl.BlockSpec((3, 1, owned, hidden), lambda e, place: (0, e, 0, 0))
    pass_shape = jax.ShapeDtypeStruct((3, local_experts, owned, hidden), BF16)
    part_spec = pl.BlockSpec((owners // 4, 3, 1, owned, hidden // 2), lambda e, place: (0, 0, e, 0, 0))
    part_shape = jax.ShapeDtypeStruct((owners // 4, 3, local_experts, owned, hidden // 2), BF16)
    return pl.pallas_call(
        functools.partial(expert_keep_kernel, owners.bit_length() - 1) if received else expert_send_kernel,
        out_shape=(part_shape,) * 4 if received else (pass_shape,) * (owners // 2),
        grid_spec=pltpu.PrefetchScalarGridSpec(
            num_scalar_prefetch=1,
            grid=(local_experts,),
            in_specs=[wide, wide, narrow, narrow, narrow] + [pass_spec] * len(received),
            out_specs=(part_spec,) * 4 if received else (pass_spec,) * (owners // 2),
            scratch_shapes=[pltpu.VMEM((2, width // 2, slots), BF16)],
        ),
        compiler_params=params(),
        cost_estimate=cost(15),
        name="expert_keep" if received else "expert_send",
    )(dp_word, xs, cs, hs, gate_grad, up_grad, *received)


def dense_grad_kernel(pairs, place_ref, *refs):
    lefts, rights = refs[:pairs], refs[pairs : 2 * pairs]
    smalls = refs[2 * pairs : -3]
    keep_ref, send_ref, sides = refs[-3:]
    owned = keep_ref.shape[1]
    bit = place_ref[0] % 2
    column = 0
    for i in range(pairs):
        if i == 0 or lefts[i] is not lefts[i - 1]:
            turn_rows(lefts[i][...], sides, owned)
        columns = rights[i].shape[1]
        for out_ref, side in ((send_ref, 1 - bit), (keep_ref, bit)):
            grad = dot(sides[side], rights[i][...]).astype(BF16)
            for q in range(keep_ref.shape[0]):
                out_ref[q, :, column : column + columns] = grad[q * owned : (q + 1) * owned]
        column += columns
    if smalls:
        rows = jnp.concatenate([ref[...] for ref in smalls], axis=0)
        rows = jnp.concatenate([rows, jnp.zeros((LANES - rows.shape[0], rows.shape[1]), F32)], axis=0)
        turned = rows.T.astype(BF16)
        for owner in range(2 * keep_ref.shape[0]):
            piece = turned[owner * owned : (owner + 1) * owned]

            @pl.when(bit == owner % 2)
            def _(owner=owner, piece=piece):
                keep_ref[owner // 2, :, column:] = piece

            @pl.when(bit != owner % 2)
            def _(owner=owner, piece=piece):
                send_ref[owner // 2, :, column:] = piece


def dense_grads(dp_word, pairs, owners, smalls=()):
    rows, width = pairs[0][0].shape
    columns = sum(right.shape[1] for _, right in pairs) + (LANES if smalls else 0)
    return pl.pallas_call(
        functools.partial(dense_grad_kernel, len(pairs)),
        out_shape=(jax.ShapeDtypeStruct((owners // 2, width // owners, columns), BF16),) * 2,
        in_specs=[pl.BlockSpec(memory_space=pltpu.SMEM)] + [vmem()] * (2 * len(pairs) + len(smalls)),
        out_specs=(vmem(),) * 2,
        scratch_shapes=[pltpu.VMEM((2, width // 2, rows), BF16)],
        compiler_params=params(),
        cost_estimate=cost(4),
        name="dense_grads",
    )(dp_word, *(left for left, _ in pairs), *(right for _, right in pairs), *smalls)


def line_up(value, size):
    return lax.ppermute(value, "expert", [(i, i + 1) for i in range(size - 1)])


def line_down(value, size):
    return lax.ppermute(value, "expert", [(i + 1, i) for i in range(size - 1)])


def line_gather(value, size):
    below, above = [], []
    up, down = value, value
    for _ in range(size - 1):
        up = line_up(up, size)
        down = line_down(down, size)
        below.append(up)
        above.append(down)
    return [value] + below + above


def add_low(*terms):
    total = terms[0].astype(F32)
    for term in terms[1:]:
        total = total + term.astype(F32)
    return total.astype(BF16)


def flip(value, bit, size):
    return lax.ppermute(value, "dp", [(i, i ^ bit) for i in range(size)])


def halve(terms, bit, left, dp_place):
    axis = left.index(bit)
    own = (dp_place >> bit) & 1
    return tuple(
        add_low(*(lax.dynamic_index_in_dim(t, side, axis, keepdims=False) for t in terms)) for side in (own, 1 - own)
    )


def start_spread(routes):
    return [
        tuple(t.reshape((2,) * (t.shape[0].bit_length() - 1) + t.shape[1:]) for t in terms) for terms in routes
    ]


def step_spread(routes, stage, dp_size, dp_place):
    bits = list(range(1, dp_size.bit_length() - 1))
    kept, sent = [], []
    for terms, order in zip(routes, (bits, bits[::-1])):
        left = [bit for bit in bits[::-1] if bit not in order[:stage]]
        keep, send = halve(terms, order[stage], left, dp_place)
        kept.append(keep)
        sent.append(flip(send, 1 << order[stage], dp_size))
    sent = lax.optimization_barrier(tuple(sent))
    return list(zip(kept, sent))


def start_dense(terms):
    half = terms[0].shape[2] // 2 // LANES * LANES
    return start_spread([tuple(t[..., :half] for t in terms), tuple(t[..., half:] for t in terms)])


def pass_line(routes, place, size):
    block = jnp.concatenate([add_low(*terms) for terms in routes], axis=-1)
    parts = block.reshape(size, -1, block.shape[-1])
    passed = [lax.dynamic_index_in_dim(parts, place, 0, keepdims=False)]
    for k in range(1, size):
        part = lax.dynamic_index_in_dim(parts, (place + k) % size, 0, keepdims=False)
        passed.append(lax.ppermute(part, "expert", [(i, (i + k) % size) for i in range(size)]))
    return passed


def total_of(parts):
    total = parts[0].astype(F32)
    for part in parts[1:]:
        total = total + part.astype(F32)
    return total


def swap_top(top, axis, size):
    for bit in range(size.bit_length() - 1):
        top = jnp.maximum(top, lax.ppermute(top, axis, [(i, i ^ (1 << bit)) for i in range(size)]))
    return top


def gather_and_top(value, top, dp_size, size):
    below, above = [], []
    up, down = value, value
    for k in range(1, size):
        up, down = line_up(up, size), line_down(down, size)
        if k == 1:
            up, down, top = lax.optimization_barrier((up, down, swap_top(top, "dp", dp_size)))
        below.append(up)
        above.append(down)
    return [value] + below + above, top


def arrival_order(size):
    sources, places = np.zeros((size, size), np.int32), np.zeros((size, size), np.int32)
    for place in range(size):
        spots = [(0, place)]
        for k in range(1, size):
            if place - k >= 0:
                spots.append((k, place - k))
            if place + k < size:
                spots.append((size - 1 + k, place + k))
        sources[place], places[place] = zip(*spots)
    return sources, places


def norm_backward(hidden, factor, gain_vec, grad_in):
    scaled = grad_in * gain_vec
    hidden_grad = factor * scaled - hidden * factor**3 * jnp.mean(
        scaled * hidden, axis=-1, keepdims=True
    )
    return hidden_grad, jnp.sum(grad_in * hidden * factor, axis=0)


def local(
    tokens,
    first_gain,
    query_weight,
    key_weight,
    value_weight,
    output_weight,
    second_gain,
    router_weight,
    gate_weight,
    up_weight,
    down_weight,
    cotangent,
    routes,
    segments,
    threshold,
):
    rows, width = tokens.shape
    query_width, kv_width = query_weight.shape[1], key_weight.shape[1]
    heads, groups = query_width // HDIM, kv_width // HDIM
    ratio = heads // groups
    local_experts = gate_weight.shape[0]
    size, dp_size = lax.axis_size("expert"), lax.axis_size("dp")
    place, dp_place = lax.axis_index("expert"), lax.axis_index("dp")
    experts = local_experts * size
    expert_pad = round_up(experts, 16)
    capacity = rows * routes.shape[1] * 9 // (experts * 8)
    slot_rows = round_up(capacity, 64)

    tables = tuple(
        lax.dynamic_slice_in_dim(jnp.asarray(table), place * rows, rows, 0) for table in rotary_tables(rows * size)
    )
    seg_block = jnp.pad(segments.reshape(rows // LANES, LANES).astype(BF16), ((0, 16 - rows // LANES), (0, 0)))

    normed, first_factor, kv_own = pl.pallas_call(
        front_kernel,
        out_shape=(
            jax.ShapeDtypeStruct((rows, width), BF16),
            jax.ShapeDtypeStruct((rows, 1), F32),
            jax.ShapeDtypeStruct((groups * rows + 16, LANES), BF16),
        ),
        in_specs=[vmem()] * 7,
        out_specs=(vmem(),) * 3,
        compiler_params=params(),
        cost_estimate=cost(4),
        name="front",
    )(tokens, first_gain.reshape(1, width), key_weight, value_weight, *tables, seg_block)
    kv_slots = [kv_own]
    for _ in range(size - 1):
        kv_slots.append(line_up(kv_slots[-1], size))

    cot_own = pl.pallas_call(
        extend_kernel,
        out_shape=jax.ShapeDtypeStruct((rows, width + LANES), BF16),
        in_specs=[vmem()] * 2,
        out_specs=vmem(),
        compiler_params=params(),
        cost_estimate=cost(2),
        name="extend",
    )(cotangent, routes)
    cots = line_gather(cot_own, size)

    query_block = 512
    queries = pl.pallas_call(
        query_kernel,
        out_shape=jax.ShapeDtypeStruct((rows, query_width), BF16),
        grid=(query_width // query_block,),
        in_specs=[
            pl.BlockSpec((rows, width), lambda s: (0, 0)),
            pl.BlockSpec((width, query_block), lambda s: (0, s)),
            pl.BlockSpec((rows, LANES), lambda s: (0, 0)),
            pl.BlockSpec((rows, LANES), lambda s: (0, 0)),
        ],
        out_specs=pl.BlockSpec((rows, query_block), lambda s: (0, s)),
        compiler_params=params(),
        cost_estimate=cost(5),
        name="queries",
    )(normed, query_weight, *tables)

    place_word = place.reshape(1).astype(jnp.int32)
    attended, lse, top = attend(queries, kv_slots, place_word, groups)
    head_top = jnp.max(top.reshape(heads, rows), axis=1).reshape(1, heads)

    hidden_in = tokens.astype(F32)
    hidden_mid = hidden_in + RESIDUAL_SCALE * dot(attended, output_weight, NT)
    second_factor = lax.rsqrt(jnp.mean(hidden_mid * hidden_mid, axis=-1, keepdims=True) + NORM_EPSILON)
    second_normed = (hidden_mid * second_factor * second_gain).astype(BF16)
    normed_blocks, head_top = gather_and_top(second_normed, head_top, dp_size, size)

    router_t = jnp.pad(router_weight.T, ((0, expert_pad - experts), (0, 0)))
    sources, blocks_of = (jnp.asarray(table)[place] for table in arrival_order(size))
    expert_place = jnp.concatenate([(place * local_experts).reshape(1), sources, blocks_of]).astype(jnp.int32)
    saved, grad_blocks, router_part = run_experts(
        expert_place, router_t, gate_weight, up_weight, down_weight, normed_blocks, cots, slot_rows
    )
    grad_blocks = lax.all_to_all(grad_blocks, "expert", 0, 0, tiled=True)

    dp_word = dp_place.reshape(1).astype(jnp.int32)
    mixture = run_mixture(blocks_of, down_weight, saved, slot_rows)
    received = [flip(part, 1, dp_size) for part in run_expert_grads(dp_word, saved, dp_size)]
    keep_a, send_a, keep_b, send_b = run_expert_grads(dp_word, saved, dp_size, received)
    mixture, grad_blocks, send_a, send_b = lax.optimization_barrier((mixture, grad_blocks, send_a, send_b))
    normed_grad = jnp.sum(grad_blocks.astype(F32), axis=0)
    passed = (flip(send_a, 2, dp_size), flip(send_b, dp_size // 2, dp_size))
    mix_one = lax.all_to_all(mixture[0], "expert", 0, 0, tiled=True)

    out_grad = cotangent.astype(F32)
    mid_back, second_gain_part = norm_backward(hidden_mid, second_factor, second_gain, normed_grad)
    mid_grad = out_grad + mid_back
    branch_grad = (RESIDUAL_SCALE * mid_grad).astype(BF16)
    attended_grad = dot(branch_grad, output_weight).astype(BF16)
    query_back, dkv = attend_back(
        queries, attended, attended_grad, lse, tables, kv_slots, place_word, groups
    )
    keep, send = dense_grads(dp_word, [(branch_grad, attended), (normed, query_back)], dp_size)
    stages = dp_size.bit_length() - 2
    from_above = line_down(dkv[size - 1], size)
    from_above, passed, mix_one, keep, send = lax.optimization_barrier((from_above, passed, mix_one, keep, send))
    wide = start_dense((keep, flip(send, 1, dp_size)))
    for k in range(1, size):
        if k > 1:
            from_above = line_down(down, size)
        if k == size - 2:
            from_above, wide = lax.optimization_barrier((from_above, wide))
        if k < size - 1:
            down = add_low(from_above, dkv[size - 1 - k])
    from_above, passed, head_top = lax.optimization_barrier((from_above, passed, head_top))
    head_top = swap_top(head_top, "expert", size)
    mix_two, head_top = lax.optimization_barrier((mixture[1], head_top))
    head_top = head_top.reshape(heads)
    expert_sums = step_spread(start_spread([(keep_a, passed[0]), (keep_b, passed[1])]), 1, dp_size, dp_place)
    mix_two = lax.all_to_all(mix_two, "expert", 0, 0, tiled=True)
    for stage in range(stages):
        wide = step_spread(wide, stage, dp_size, dp_place)
    key_back, value_back = pl.pallas_call(
        unpack_kernel,
        out_shape=(jax.ShapeDtypeStruct((rows, kv_width), BF16),) * 2,
        in_specs=[vmem()] * 4,
        out_specs=(vmem(),) * 2,
        compiler_params=params(),
        cost_estimate=cost(2),
        name="unpack",
    )(dkv[0], from_above, *tables)

    first_grad = dot(query_back, query_weight, NT)
    first_grad = first_grad + dot(key_back, key_weight, NT)
    first_grad = first_grad + dot(value_back, value_weight, NT)
    input_back, first_gain_part = norm_backward(hidden_in, first_factor, first_gain, first_grad)
    input_grad = mid_grad + input_back
    keep, send = dense_grads(
        dp_word,
        [(normed, key_back), (normed, value_back)],
        dp_size,
        (router_part, second_gain_part[None], first_gain_part[None]),
    )
    keep, send, wide, expert_sums = lax.optimization_barrier((keep, send, wide, expert_sums))
    rest = start_dense((keep, flip(send, 1, dp_size)))
    rest = step_spread(rest, 0, dp_size, dp_place)
    wide_parts, rest, expert_sums, mix_two = lax.optimization_barrier(
        (pass_line(wide, place, size), rest, expert_sums, mix_two)
    )
    for stage in range(2, stages):
        expert_sums = step_spread(expert_sums, stage, dp_size, dp_place)
    expert_sums = [
        jnp.concatenate([a[w].astype(F32) + b[w].astype(F32) for a, b in expert_sums], axis=-1) for w in range(3)
    ]
    for stage in range(1, stages):
        rest = step_spread(rest, stage, dp_size, dp_place)
    rest_parts = lax.optimization_barrier(pass_line(rest, place, size))
    wide_grad, rest_grad = total_of(wide_parts), total_of(rest_parts)
    mixture = jnp.concatenate([jnp.sum(part.astype(F32), axis=0) for part in (mix_one, mix_two)], axis=1)
    block_out = (hidden_mid + mixture).astype(BF16)
    projection_grad, query_grad = wide_grad[:, :query_width], wide_grad[:, query_width:]
    key_grad = rest_grad[:, :kv_width]
    value_grad = rest_grad[:, kv_width : 2 * kv_width]
    small_grad = rest_grad[:, 2 * kv_width :]

    head_scale = threshold / jnp.maximum(head_top, threshold)
    group_scale = jnp.min(head_scale.reshape(groups, ratio), axis=1)
    row_count = width // (dp_size * size)
    row_start = (dp_place * size + place) * row_count
    query_rows = lax.dynamic_slice_in_dim(query_weight, row_start, row_count, 0).astype(F32)
    key_rows = lax.dynamic_slice_in_dim(key_weight, row_start, row_count, 0).astype(F32)
    query_clipped = (query_rows * jnp.repeat(jnp.sqrt(head_scale), HDIM)[None, :]).astype(BF16)
    key_clipped = (key_rows * jnp.repeat(jnp.sqrt(group_scale), HDIM)[None, :]).astype(BF16)
    return (
        block_out,
        input_grad,
        small_grad[:, expert_pad + 1],
        query_grad,
        key_grad,
        value_grad,
        projection_grad,
        small_grad[:, expert_pad],
        small_grad[:, :experts],
        expert_sums[0],
        expert_sums[1],
        expert_sums[2],
        head_scale,
        query_clipped,
        key_clipped,
    )


def solution(mesh):
    row = P(("dp", "expert"), None)
    vector = P(("dp", "expert"))
    expert_in = P("expert", None, None)
    expert_out = P("expert", "dp", None)
    return jax.shard_map(
        local,
        mesh=mesh,
        in_specs=(row,) + (P(),) * 7 + (expert_in,) * 3 + (row, row, vector, P()),
        out_specs=(row, row, vector)
        + (row,) * 4
        + (vector, row)
        + (expert_out,) * 3
        + (P(), row, row),
        check_vma=False,
    )
```

```python
import functools

import jax
import jax.numpy as jnp
import numpy as np
from jax import lax
from jax.experimental import pallas as pl
from jax.experimental.pallas import tpu as pltpu
from jax.sharding import PartitionSpec as P

HDIM = 64
LANES = 128
ATTENTION_SCALE = 0.015625
RESIDUAL_SCALE = 0.22
NORM_EPSILON = 1e-06
ROTARY_BASE = 10000.0
MASKED_SCORE = -1e30
BF16 = jnp.bfloat16
F32 = jnp.float32
NN = (((1,), (0,)), ((), ()))
NT = (((1,), (1,)), ((), ()))
TN = (((0,), (0,)), ((), ()))
VMEM_LIMIT = 60 * 1024 * 1024
COLUMNS = 512


def dot(left, right, dims=NN):
    return lax.dot_general(left, right, dims, preferred_element_type=F32)


def round_up(count, unit):
    return (count + unit - 1) // unit * unit


def low_lanes(rows):
    return lax.broadcasted_iota(jnp.int32, (rows, LANES), 1) < HDIM


def partner_lanes(slab):
    lane = lax.broadcasted_iota(jnp.int32, slab.shape, 1) % HDIM
    half = HDIM // 2
    return jnp.where(lane < half, pltpu.roll(slab, LANES - half, 1), pltpu.roll(slab, half, 1))


def vmem():
    return pl.BlockSpec(memory_space=pltpu.VMEM)


def params(**more):
    return pltpu.CompilerParams(vmem_limit_bytes=VMEM_LIMIT, **more)


def cost(microseconds):
    return pl.CostEstimate(flops=int(microseconds * 1e6), bytes_accessed=0, transcendentals=0)


def rotary_tables(length):
    half = HDIM // 2
    inverse = np.float32(ROTARY_BASE) ** (np.float32(-2.0) * np.arange(half, dtype=np.float32) / np.float32(HDIM))
    angles = np.arange(length, dtype=np.float32)[:, None] * np.tile(inverse, LANES // half)[None, :]
    angles = angles.astype(np.float32).astype(np.float64)
    sign = np.where(np.arange(LANES) % HDIM < half, -1.0, 1.0)
    return np.cos(angles).astype(np.float32), (np.sin(angles) * sign).astype(np.float32)


def extend_kernel(cotangent_ref, routes_ref, out_ref):
    rows, top_count = routes_ref.shape
    width = cotangent_ref.shape[1]
    lane = lax.broadcasted_iota(jnp.int32, (rows, LANES), 1)
    chosen = jnp.zeros((rows, LANES), F32)
    for k in range(top_count):
        chosen = chosen + jnp.where(routes_ref[:, k : k + 1] == lane, 1.0, 0.0)
    first = lax.broadcasted_iota(jnp.int32, (rows, rows), 0)
    second = lax.broadcasted_iota(jnp.int32, (rows, rows), 1)
    earlier = jnp.where(second < first, 1.0, 0.0).astype(BF16)
    rank = dot(earlier, chosen.astype(BF16))
    out_ref[:, :width] = cotangent_ref[...]
    out_ref[:, width:] = jnp.where(chosen > 0.5, rank, -1.0).astype(BF16)


def front_kernel(tokens_ref, gain_ref, key_ref, value_ref, cos_ref, sin_ref, segments_ref, normed_ref, factor_ref, kv_ref):
    hidden = tokens_ref[...].astype(F32)
    factor = lax.rsqrt(jnp.mean(hidden * hidden, axis=-1, keepdims=True) + NORM_EPSILON)
    normed = (hidden * factor * gain_ref[...]).astype(BF16)
    normed_ref[...] = normed
    factor_ref[...] = factor
    keys = dot(normed, key_ref[...])
    values = dot(normed, value_ref[...])
    cosine, sine = cos_ref[...], sin_ref[...]
    rows = hidden.shape[0]
    low = low_lanes(rows)
    for i in range(keys.shape[1] // LANES):
        slab = keys[:, i * LANES : (i + 1) * LANES]
        slab = slab * cosine + partner_lanes(slab) * sine
        value_slab = values[:, i * LANES : (i + 1) * LANES]
        even, odd = 2 * i * rows, (2 * i + 1) * rows
        kv_ref[even : even + rows, :] = jnp.where(low, slab, pltpu.roll(value_slab, HDIM, 1)).astype(BF16)
        kv_ref[odd : odd + rows, :] = jnp.where(low, pltpu.roll(slab, HDIM, 1), value_slab).astype(BF16)
    kv_ref[keys.shape[1] // HDIM * rows :, :] = segments_ref[...]


def query_kernel(normed_ref, query_ref, cos_ref, sin_ref, out_ref):
    raw = dot(normed_ref[...], query_ref[...])
    cosine, sine = cos_ref[...], sin_ref[...]
    for i in range(raw.shape[1] // LANES):
        slab = raw[:, i * LANES : (i + 1) * LANES]
        slab = slab * cosine + partner_lanes(slab) * sine
        out_ref[:, i * LANES : (i + 1) * LANES] = (slab.astype(BF16).astype(F32) * ATTENTION_SCALE).astype(BF16)


def fill_bias(bias_ref, need_ref, place_ref, seg_row, seg_columns):
    slots, keys, rows = bias_ref.shape
    for k in range(slots):
        allowed = seg_columns[k] == seg_row
        if k == 0:
            allowed = allowed & (
                lax.broadcasted_iota(jnp.int32, (keys, rows), 0) <= lax.broadcasted_iota(jnp.int32, (keys, rows), 1)
            )
        bias_ref[k] = jnp.where(allowed, 0.0, MASKED_SCORE)
    first = jnp.min(seg_row)
    need = jnp.int32(1)
    for k in range(1, slots):
        need = jnp.where((jnp.max(seg_columns[k]) >= first) & (k <= place_ref[0]), k + 1, need)
    need_ref[0] = need


def prepare_bias(bias_ref, need_ref, place_ref, seg_refs):
    slots, keys, _ = bias_ref.shape
    halves = keys // LANES
    seg_rows = [
        jnp.concatenate([ref[j : j + 1, :].astype(F32) for j in range(halves)], axis=1) for ref in seg_refs
    ]
    seg_columns = [jnp.broadcast_to(row, (LANES, keys)).T[:, :1] for row in seg_rows]
    fill_bias(bias_ref, need_ref, place_ref, seg_rows[0], seg_columns)


def head_slab(block, head, upper):
    slab = block[:, (head // 2) * LANES : (head // 2 + 1) * LANES].astype(F32)
    low = low_lanes(slab.shape[0])
    if (head % 2 == 1) != upper:
        slab = pltpu.roll(slab, HDIM, 1)
    return jnp.where(low != upper, slab, 0.0)


def add_bias(scores, bias, ratio):
    rows = bias.shape[1]
    return jnp.concatenate([scores[:, r * rows : (r + 1) * rows] + bias for r in range(ratio)], axis=1)


def attend_kernel(slots, ratio, place_ref, query_ref, *refs):
    kv_refs, seg_refs = refs[:slots], refs[slots : 2 * slots]
    attended_ref, lse_ref, top_ref, bias_ref, stacked_ref, scores_ref, acc_ref, max_ref, need_ref = refs[2 * slots :]
    rows = query_ref.shape[0]
    low = low_lanes(rows)

    @pl.when(pl.program_id(0) == 0)
    def _():
        prepare_bias(bias_ref, need_ref, place_ref, seg_refs)

    need = need_ref[0]
    outs = []
    for group in range(2):
        for r in range(ratio):
            stacked_ref[r * rows : (r + 1) * rows, :] = head_slab(
                query_ref, group * ratio + r, False
            ).astype(BF16)
        for k in range(slots):

            def score(k=k):
                kv = kv_refs[k][group * rows : (group + 1) * rows, :]
                scores = add_bias(dot(kv, stacked_ref[...], NT), bias_ref[k], ratio)
                scores_ref[k] = scores
                top = jnp.max(scores, axis=0, keepdims=True)
                max_ref[...] = top if k == 0 else jnp.maximum(max_ref[...], top)

            if k == 0:
                score()
            else:
                pl.when(k < need)(score)
        for k in range(slots):

            def mix(k=k):
                kv = kv_refs[k][group * rows : (group + 1) * rows, :]
                kv = jnp.where(low, jnp.ones_like(kv), kv)
                weights = jnp.exp(scores_ref[k] - max_ref[...]).astype(BF16)
                part = dot(kv, weights, TN)
                acc_ref[...] = part if k == 0 else acc_ref[...] + part

            if k == 0:
                mix()
            else:
                pl.when(k < need)(mix)
        total = acc_ref[:1, :]
        lse_ref[0, group : group + 1, :] = max_ref[...] + jnp.log(total)
        top_ref[0, group : group + 1, :] = max_ref[...]
        mixed = acc_ref[HDIM:, :] / total
        for r in range(ratio):
            outs.append(mixed[:, r * rows : (r + 1) * rows])
    for i in range(len(outs) // 2):
        slab = jnp.concatenate([outs[2 * i], outs[2 * i + 1]], axis=0)
        attended_ref[:, i * LANES : (i + 1) * LANES] = slab.T.astype(BF16)


def kv_specs(slots, groups, rows):
    return [pl.BlockSpec((2 * rows, LANES), lambda s: (s, 0))] * slots + [
        pl.BlockSpec((16, LANES), lambda s: (groups * rows // 16, 0))
    ] * slots


def attend(queries, kv_slots, place, groups):
    slots = len(kv_slots)
    rows, width = queries.shape
    ratio = width // HDIM // groups
    steps = groups // 2
    block = 2 * ratio * HDIM
    stats = pl.BlockSpec((1, 2, ratio * rows), lambda s: (s, 0, 0))
    return pl.pallas_call(
        functools.partial(attend_kernel, slots, ratio),
        out_shape=(jax.ShapeDtypeStruct((rows, width), BF16),)
        + (jax.ShapeDtypeStruct((steps, 2, ratio * rows), F32),) * 2,
        grid=(steps,),
        in_specs=[
            pl.BlockSpec(memory_space=pltpu.SMEM),
            pl.BlockSpec((rows, block), lambda s: (0, s)),
        ]
        + kv_specs(slots, groups, rows),
        out_specs=(pl.BlockSpec((rows, block), lambda s: (0, s)), stats, stats),
        scratch_shapes=[
            pltpu.VMEM((slots, rows, rows), F32),
            pltpu.VMEM((ratio * rows, LANES), BF16),
            pltpu.VMEM((slots, rows, ratio * rows), F32),
            pltpu.VMEM((LANES, ratio * rows), F32),
            pltpu.VMEM((1, ratio * rows), F32),
            pltpu.SMEM((1,), jnp.int32),
        ],
        compiler_params=params(),
        cost_estimate=cost(20),
        name="attend",
    )(place, queries, *kv_slots, *kv_slots)


def attend_back_kernel(slots, ratio, place_ref, query_ref, attended_ref, grad_ref, lse_ref, cos_ref, sin_ref, *refs):
    kv_refs, seg_refs = refs[:slots], refs[slots : 2 * slots]
    refs = refs[2 * slots :]
    back_ref, dkv_refs = refs[0], refs[1 : slots + 1]
    bias_ref, query_s, grad_s, acc_ref, delta_s, need_ref = refs[slots + 1 :]
    rows = query_ref.shape[0]

    @pl.when(pl.program_id(0) == 0)
    def _():
        prepare_bias(bias_ref, need_ref, place_ref, seg_refs)

    need = need_ref[0]
    outs = []
    for group in range(2):
        for r in range(ratio):
            head = group * ratio + r
            part = slice(r * rows, (r + 1) * rows)
            query_s[part, :] = head_slab(query_ref, head, False).astype(BF16)
            grad = head_slab(grad_ref, head, True)
            grad_s[part, :] = grad.astype(BF16)
            product = (grad * head_slab(attended_ref, head, True)).T
            delta_s[:, part] = jnp.sum(product, axis=0, keepdims=True)
        for k in range(slots):

            def step(k=k):
                kv = kv_refs[k][group * rows : (group + 1) * rows, :]
                scores = add_bias(dot(kv, query_s[...], NT), bias_ref[k], ratio)
                weights = jnp.exp(scores - lse_ref[0, group : group + 1, :])
                weight_grad = dot(kv, grad_s[...], NT)
                score_grad = (weights * (weight_grad - delta_s[...])).astype(BF16)
                part = dot(kv, score_grad, TN)
                acc_ref[...] = part if k == 0 else acc_ref[...] + part
                dkv_refs[k][group * rows : (group + 1) * rows, :] = (
                    dot(score_grad, query_s[...]) + dot(weights.astype(BF16), grad_s[...])
                ).astype(BF16)

            if k == 0:
                step()
            else:
                pl.when(k < need)(step)

                @pl.when(k >= need)
                def _(k=k):
                    dkv_refs[k][group * rows : (group + 1) * rows, :] = jnp.zeros((rows, LANES), BF16)

        for r in range(ratio):
            outs.append(acc_ref[:HDIM, r * rows : (r + 1) * rows] * ATTENTION_SCALE)
    cosine, sine = cos_ref[...], sin_ref[...]
    for i in range(len(outs) // 2):
        slab = jnp.concatenate([outs[2 * i], outs[2 * i + 1]], axis=0).T
        slab = slab * cosine - partner_lanes(slab) * sine
        back_ref[:, i * LANES : (i + 1) * LANES] = slab.astype(BF16)


def attend_back(queries, attended, grad, lse, tables, kv_slots, place, groups):
    slots = len(kv_slots)
    rows, width = queries.shape
    ratio = width // HDIM // groups
    steps = groups // 2
    block = 2 * ratio * HDIM
    whole = pl.BlockSpec((rows, LANES), lambda s: (0, 0))
    wide = pl.BlockSpec((rows, block), lambda s: (0, s))
    out = pl.pallas_call(
        functools.partial(attend_back_kernel, slots, ratio),
        out_shape=(jax.ShapeDtypeStruct((rows, width), BF16),)
        + (jax.ShapeDtypeStruct((groups * rows, LANES), BF16),) * slots,
        grid=(steps,),
        in_specs=[
            pl.BlockSpec(memory_space=pltpu.SMEM),
            wide,
            wide,
            wide,
            pl.BlockSpec((1, 2, ratio * rows), lambda s: (s, 0, 0)),
            whole,
            whole,
        ]
        + kv_specs(slots, groups, rows),
        out_specs=(wide,) + (pl.BlockSpec((2 * rows, LANES), lambda s: (s, 0)),) * slots,
        scratch_shapes=[
            pltpu.VMEM((slots, rows, rows), F32),
            pltpu.VMEM((ratio * rows, LANES), BF16),
            pltpu.VMEM((ratio * rows, LANES), BF16),
            pltpu.VMEM((LANES, ratio * rows), F32),
            pltpu.VMEM((1, ratio * rows), F32),
            pltpu.SMEM((1,), jnp.int32),
        ],
        compiler_params=params(),
        cost_estimate=cost(2),
        name="attend_back",
    )(place, queries, attended, grad, lse, *tables, *kv_slots, *kv_slots)
    return out[0], out[1:]


def unpack_kernel(own_ref, above_ref, cos_ref, sin_ref, key_ref, value_ref):
    rows = cos_ref.shape[0]
    low = low_lanes(rows)
    cosine, sine = cos_ref[...], sin_ref[...]
    for i in range(key_ref.shape[1] // LANES):
        even, odd = (
            own_ref[g * rows : (g + 1) * rows, :].astype(F32) + above_ref[g * rows : (g + 1) * rows, :].astype(F32)
            for g in (2 * i, 2 * i + 1)
        )
        slab = jnp.where(low, even, pltpu.roll(odd, HDIM, 1))
        slab = slab * cosine - partner_lanes(slab) * sine
        key_ref[:, i * LANES : (i + 1) * LANES] = slab.astype(BF16)
        value_ref[:, i * LANES : (i + 1) * LANES] = jnp.where(
            low, pltpu.roll(even, HDIM, 1), odd
        ).astype(BF16)


def expert_kernel(blocks, slot_rows, local_experts, place_ref, router_ref, gate_ref, up_ref, down_ref, *refs):
    sources = 2 * blocks - 1
    normed_in, cot_in = refs[:sources], refs[sources : 2 * sources]
    xs_out, cs_out, hs_ref, gate_grad_ref, up_grad_ref, hits, grad_out, router_grad_ref = refs[2 * sources : 2 * sources + 8]
    x_all, c_all, info, gates, back, xs_all, cs_all, gate_slots, slot_grads, sems, save_sem, out_sem = refs[2 * sources + 8 :]
    step = pl.program_id(0)
    rows, width = x_all.shape[1:]
    expert_pad = router_ref.shape[0]
    first_expert = place_ref[0]
    mine = pl.ds(first_expert + step, 1)

    def source_copies(i, s):
        return (
            pltpu.make_async_copy(normed_in[s], x_all.at[i], sems.at[0, i]),
            pltpu.make_async_copy(cot_in[s], c_all.at[i], sems.at[1, i]),
        )

    def save_copies():
        return (
            pltpu.make_async_copy(xs_all, xs_out, save_sem.at[0]),
            pltpu.make_async_copy(cs_all, cs_out, save_sem.at[1]),
        )

    @pl.when(step == 0)
    def _():
        for i in range(blocks):
            for s in range(sources):

                @pl.when(place_ref[1 + i] == s)
                def _(i=i, s=s):
                    for copy in source_copies(i, s):
                        copy.start()

        same = jnp.where(
            lax.broadcasted_iota(jnp.int32, (rows, rows), 0) == lax.broadcasted_iota(jnp.int32, (rows, rows), 1),
            1.0,
            0.0,
        ).astype(BF16)
        slot_ids = lax.broadcasted_iota(jnp.int32, (slot_rows, rows), 0).astype(F32)
        back[...] = jnp.zeros_like(back)
        for i in range(blocks):
            for copy in source_copies(i, 0):
                copy.wait()
            info[i] = dot(c_all[i, :, width:], same, TN)
            logits = dot(router_ref[...], x_all[i], NT)
            logits = jnp.where(info[i, :expert_pad, :] >= 0, logits, MASKED_SCORE)
            weights = jnp.exp(logits - jnp.max(logits, axis=0, keepdims=True))
            gates[i] = weights / jnp.sum(weights, axis=0, keepdims=True)
            for e in range(local_experts):
                own = pl.ds(first_expert + e, 1)
                hit = slot_ids == info[i, own, :]
                gate_slots[e, i * slot_rows : (i + 1) * slot_rows, :] = RESIDUAL_SCALE * jnp.sum(
                    jnp.where(hit, gates[i, own, :], 0.0), axis=-1, keepdims=True
                )
                hits[i, e * slot_rows : (e + 1) * slot_rows, :] = jnp.where(hit, 1.0, 0.0).astype(BF16)
            for source, target in ((x_all, xs_all), (c_all, cs_all)):
                for c in range(width // COLUMNS):
                    columns = slice(c * COLUMNS, (c + 1) * COLUMNS)
                    picked = dot(hits[i], source[i, :, columns]).astype(BF16)
                    for e in range(local_experts):
                        target[e, i * slot_rows : (i + 1) * slot_rows, columns] = picked[
                            e * slot_rows : (e + 1) * slot_rows
                        ]
        for copy in save_copies():
            copy.start()

    gate_slot = gate_slots[step]
    gate_pre = dot(xs_all[step], gate_ref[0])
    up_pre = dot(xs_all[step], up_ref[0])
    raw_grad = dot(cs_all[step], down_ref[0])
    sigmoid = 1.0 / (1.0 + jnp.exp(-gate_pre))
    active = gate_pre * sigmoid
    expert_hidden = (active * up_pre).astype(BF16).astype(F32)
    hs_ref[0] = (expert_hidden * gate_slot).astype(BF16)
    back_slot = jnp.sum(expert_hidden * raw_grad, axis=-1, keepdims=True) * RESIDUAL_SCALE
    hidden_grad = raw_grad * gate_slot
    gate_grad_ref[0] = (hidden_grad * up_pre * sigmoid * (1.0 + gate_pre * (1.0 - sigmoid))).astype(BF16)
    up_grad_ref[0] = (hidden_grad * active).astype(BF16)
    spot = pl.ds(pl.multiple_of(step * slot_rows, slot_rows), slot_rows)
    for c in range(width // COLUMNS):
        columns = slice(c * COLUMNS, (c + 1) * COLUMNS)
        slot_grad = (
            dot(gate_grad_ref[0], gate_ref[0, columns, :], NT) + dot(up_grad_ref[0], up_ref[0, columns, :], NT)
        ).astype(BF16)
        for i in range(blocks):
            slot_grads[i, spot, columns] = slot_grad[i * slot_rows : (i + 1) * slot_rows]
    for i in range(blocks):
        part = slice(i * slot_rows, (i + 1) * slot_rows)
        back_row = jnp.sum(hits[i, spot, :].astype(F32) * back_slot[part], axis=0, keepdims=True)
        back[i, mine, :] = back_row * gates[i, mine, :]

    @pl.when(step == local_experts - 1)
    def _():
        def copy(i):
            return pltpu.make_async_copy(
                c_all.at[i, :, pl.ds(0, width)], grad_out.at[place_ref[1 + blocks + i]], out_sem.at[i]
            )

        router_sum = None
        for i in range(blocks):
            share = back[i]
            logit_grad = (share - gates[i] * jnp.sum(share, axis=0, keepdims=True)).astype(BF16)
            turned = hits[i].T
            for c in range(width // COLUMNS):
                columns = slice(c * COLUMNS, (c + 1) * COLUMNS)
                c_all[i, :, columns] = (
                    dot(turned, slot_grads[i, :, columns]) + dot(logit_grad, router_ref[:, columns], TN)
                ).astype(BF16)
            copy(i).start()
            part = dot(logit_grad, x_all[i])
            router_sum = part if router_sum is None else router_sum + part
        router_grad_ref[...] = router_sum
        for i in range(blocks):
            copy(i).wait()
        for saved in save_copies():
            saved.wait()


def run_experts(place, router_t, gate_weight, up_weight, down_weight, normed, cots, slot_rows):
    local_experts, width, hidden = gate_weight.shape
    sources = len(normed)
    blocks = (sources + 1) // 2
    rows = normed[0].shape[0]
    expert_pad = router_t.shape[0]
    slots = blocks * slot_rows
    stacked = local_experts * slot_rows
    anywhere = pl.BlockSpec(memory_space=pl.ANY)
    weight_spec = pl.BlockSpec((1, width, hidden), lambda e, place: (e, 0, 0))
    narrow = pl.BlockSpec((1, slots, hidden), lambda e, place: (e, 0, 0))
    wide_shape = jax.ShapeDtypeStruct((local_experts, slots, width), BF16)
    narrow_shape = jax.ShapeDtypeStruct((local_experts, slots, hidden), BF16)
    out = pl.pallas_call(
        functools.partial(expert_kernel, blocks, slot_rows, local_experts),
        out_shape=(
            wide_shape,
            wide_shape,
            narrow_shape,
            narrow_shape,
            narrow_shape,
            jax.ShapeDtypeStruct((blocks, stacked, rows), BF16),
            jax.ShapeDtypeStruct((blocks, rows, width), BF16),
            jax.ShapeDtypeStruct((expert_pad, width), F32),
        ),
        grid_spec=pltpu.PrefetchScalarGridSpec(
            num_scalar_prefetch=1,
            grid=(local_experts,),
            in_specs=[pl.BlockSpec((expert_pad, width), lambda e, place: (0, 0))]
            + [weight_spec] * 3
            + [anywhere] * (2 * sources),
            out_specs=(
                anywhere,
                anywhere,
                narrow,
                narrow,
                narrow,
                pl.BlockSpec((blocks, stacked, rows), lambda e, place: (0, 0, 0)),
                anywhere,
                pl.BlockSpec((expert_pad, width), lambda e, place: (0, 0)),
            ),
            scratch_shapes=[
                pltpu.VMEM((blocks, rows, width), BF16),
                pltpu.VMEM((blocks, rows, width + LANES), BF16),
                pltpu.VMEM((blocks, LANES, rows), F32),
                pltpu.VMEM((blocks, expert_pad, rows), F32),
                pltpu.VMEM((blocks, expert_pad, rows), F32),
                pltpu.VMEM((local_experts, slots, width), BF16),
                pltpu.VMEM((local_experts, slots, width), BF16),
                pltpu.VMEM((local_experts, slots, 1), F32),
                pltpu.VMEM((blocks, stacked, width), BF16),
                pltpu.SemaphoreType.DMA((2, blocks)),
                pltpu.SemaphoreType.DMA((2,)),
                pltpu.SemaphoreType.DMA((blocks,)),
            ],
        ),
        compiler_params=params(),
        cost_estimate=cost(45),
        name="experts",
    )(place, router_t, gate_weight, up_weight, down_weight, *normed, *cots)
    return out[:6], out[6], out[7]


def mixture_kernel(blocks, slot_rows, local_experts, order_ref, down_ref, hs_ref, hits_ref, mix_one, mix_two, slot_outs, mix_low, out_sem):
    step = pl.program_id(0)
    width = down_ref.shape[1]
    spot = pl.ds(pl.multiple_of(step * slot_rows, slot_rows), slot_rows)
    for c in range(width // COLUMNS):
        columns = slice(c * COLUMNS, (c + 1) * COLUMNS)
        slot_out = dot(hs_ref[0], down_ref[0, columns, :], NT).astype(BF16)
        for i in range(blocks):
            slot_outs[i, spot, columns] = slot_out[i * slot_rows : (i + 1) * slot_rows]

    @pl.when(step == local_experts - 1)
    def _():
        def copy(i, h):
            columns = pl.ds(h * (width // 2), width // 2)
            return pltpu.make_async_copy(
                mix_low.at[i, :, columns], (mix_one, mix_two)[h].at[order_ref[i]], out_sem.at[i, h]
            )

        for i in range(blocks):
            turned = hits_ref[i].T
            for c in range(width // COLUMNS):
                columns = slice(c * COLUMNS, (c + 1) * COLUMNS)
                mix_low[i, :, columns] = dot(turned, slot_outs[i, :, columns]).astype(BF16)
            for h in range(2):
                copy(i, h).start()
        for i in range(blocks):
            for h in range(2):
                copy(i, h).wait()


def run_mixture(order, down_weight, saved, slot_rows):
    hs, hits = saved[2], saved[5]
    local_experts, width, hidden = down_weight.shape
    blocks, stacked, rows = hits.shape
    return pl.pallas_call(
        functools.partial(mixture_kernel, blocks, slot_rows, local_experts),
        out_shape=(jax.ShapeDtypeStruct((blocks, rows, width // 2), BF16),) * 2,
        grid_spec=pltpu.PrefetchScalarGridSpec(
            num_scalar_prefetch=1,
            grid=(local_experts,),
            in_specs=[
                pl.BlockSpec((1, width, hidden), lambda e, order: (e, 0, 0)),
                pl.BlockSpec((1, hs.shape[1], hidden), lambda e, order: (e, 0, 0)),
                pl.BlockSpec((blocks, stacked, rows), lambda e, order: (0, 0, 0)),
            ],
            out_specs=(pl.BlockSpec(memory_space=pl.ANY),) * 2,
            scratch_shapes=[
                pltpu.VMEM((blocks, stacked, width), BF16),
                pltpu.VMEM((blocks, rows, width), BF16),
                pltpu.SemaphoreType.DMA((blocks, 2)),
            ],
        ),
        compiler_params=params(),
        cost_estimate=cost(10),
        name="mixture",
    )(order, down_weight, hs, hits)


def turn_rows(block, sides_ref, owned):
    width = block.shape[1]
    chunk = int(np.lcm(2 * owned, LANES))
    for c in range(width // chunk):
        turned = block[:, c * chunk : (c + 1) * chunk].T
        for o in range(chunk // owned):
            owner = c * (chunk // owned) + o
            spot = owner // 2 * owned
            sides_ref[owner % 2, spot : spot + owned, :] = turned[o * owned : (o + 1) * owned]


def grad_products(side, xs_ref, cs_ref, hs_ref, gate_grad_ref, up_grad_ref, sides, owned):
    for left_ref, rights in ((xs_ref, ((0, gate_grad_ref), (1, up_grad_ref))), (cs_ref, ((2, hs_ref),))):
        turn_rows(left_ref[0], sides, owned)
        for w, right_ref in rights:
            yield w, dot(sides[side], right_ref[0])


def expert_send_kernel(place_ref, xs_ref, cs_ref, hs_ref, gate_grad_ref, up_grad_ref, *refs):
    send_refs, sides = refs[:-1], refs[-1]
    owned = send_refs[0].shape[2]
    side = 1 - place_ref[0] % 2
    for w, grad in grad_products(side, xs_ref, cs_ref, hs_ref, gate_grad_ref, up_grad_ref, sides, owned):
        for q, send_ref in enumerate(send_refs):
            send_ref[w, 0] = grad[q * owned : (q + 1) * owned].astype(BF16)


def expert_keep_kernel(bits, place_ref, xs_ref, cs_ref, hs_ref, gate_grad_ref, up_grad_ref, *refs):
    count = 1 << (bits - 1)
    received_refs, outs, sides = refs[:count], refs[count : count + 4], refs[-1]
    owned = received_refs[0].shape[2]
    hidden = hs_ref.shape[2] // 2
    side = place_ref[0] % 2
    for w, grad in grad_products(side, xs_ref, cs_ref, hs_ref, gate_grad_ref, up_grad_ref, sides, owned):
        for q in range(count):
            piece = (grad[q * owned : (q + 1) * owned] + received_refs[q][w, 0].astype(F32)).astype(BF16)
            for route, bit in enumerate((1, bits - 1)):
                part = piece[:, route * hidden : (route + 1) * hidden]
                own = (place_ref[0] >> bit) & 1
                spot = (q >> bit << (bit - 1)) | (q & ((1 << (bit - 1)) - 1))
                here = q >> (bit - 1) & 1

                @pl.when(own == here)
                def _(route=route, part=part, spot=spot, w=w):
                    outs[2 * route][spot, w, 0] = part

                @pl.when(own != here)
                def _(route=route, part=part, spot=spot, w=w):
                    outs[2 * route + 1][spot, w, 0] = part


def run_expert_grads(dp_word, saved, owners, received=()):
    xs, cs, hs, gate_grad, up_grad, _ = saved
    local_experts, slots, width = xs.shape
    hidden = hs.shape[2]
    owned = width // owners
    wide = pl.BlockSpec((1, slots, width), lambda e, place: (e, 0, 0))
    narrow = pl.BlockSpec((1, slots, hidden), lambda e, place: (e, 0, 0))
    pass_spec = pl.BlockSpec((3, 1, owned, hidden), lambda e, place: (0, e, 0, 0))
    pass_shape = jax.ShapeDtypeStruct((3, local_experts, owned, hidden), BF16)
    part_spec = pl.BlockSpec((owners // 4, 3, 1, owned, hidden // 2), lambda e, place: (0, 0, e, 0, 0))
    part_shape = jax.ShapeDtypeStruct((owners // 4, 3, local_experts, owned, hidden // 2), BF16)
    return pl.pallas_call(
        functools.partial(expert_keep_kernel, owners.bit_length() - 1) if received else expert_send_kernel,
        out_shape=(part_shape,) * 4 if received else (pass_shape,) * (owners // 2),
        grid_spec=pltpu.PrefetchScalarGridSpec(
            num_scalar_prefetch=1,
            grid=(local_experts,),
            in_specs=[wide, wide, narrow, narrow, narrow] + [pass_spec] * len(received),
            out_specs=(part_spec,) * 4 if received else (pass_spec,) * (owners // 2),
            scratch_shapes=[pltpu.VMEM((2, width // 2, slots), BF16)],
        ),
        compiler_params=params(),
        cost_estimate=cost(15),
        name="expert_keep" if received else "expert_send",
    )(dp_word, xs, cs, hs, gate_grad, up_grad, *received)


def dense_grad_kernel(pairs, place_ref, *refs):
    lefts, rights = refs[:pairs], refs[pairs : 2 * pairs]
    smalls = refs[2 * pairs : -3]
    keep_ref, send_ref, sides = refs[-3:]
    owned = keep_ref.shape[1]
    bit = place_ref[0] % 2
    column = 0
    for i in range(pairs):
        if i == 0 or lefts[i] is not lefts[i - 1]:
            turn_rows(lefts[i][...], sides, owned)
        columns = rights[i].shape[1]
        for out_ref, side in ((send_ref, 1 - bit), (keep_ref, bit)):
            grad = dot(sides[side], rights[i][...]).astype(BF16)
            for q in range(keep_ref.shape[0]):
                out_ref[q, :, column : column + columns] = grad[q * owned : (q + 1) * owned]
        column += columns
    if smalls:
        rows = jnp.concatenate([ref[...] for ref in smalls], axis=0)
        rows = jnp.concatenate([rows, jnp.zeros((LANES - rows.shape[0], rows.shape[1]), F32)], axis=0)
        turned = rows.T.astype(BF16)
        for owner in range(2 * keep_ref.shape[0]):
            piece = turned[owner * owned : (owner + 1) * owned]

            @pl.when(bit == owner % 2)
            def _(owner=owner, piece=piece):
                keep_ref[owner // 2, :, column:] = piece

            @pl.when(bit != owner % 2)
            def _(owner=owner, piece=piece):
                send_ref[owner // 2, :, column:] = piece


def dense_grads(dp_word, pairs, owners, smalls=()):
    rows, width = pairs[0][0].shape
    columns = sum(right.shape[1] for _, right in pairs) + (LANES if smalls else 0)
    return pl.pallas_call(
        functools.partial(dense_grad_kernel, len(pairs)),
        out_shape=(jax.ShapeDtypeStruct((owners // 2, width // owners, columns), BF16),) * 2,
        in_specs=[pl.BlockSpec(memory_space=pltpu.SMEM)] + [vmem()] * (2 * len(pairs) + len(smalls)),
        out_specs=(vmem(),) * 2,
        scratch_shapes=[pltpu.VMEM((2, width // 2, rows), BF16)],
        compiler_params=params(),
        cost_estimate=cost(4),
        name="dense_grads",
    )(dp_word, *(left for left, _ in pairs), *(right for _, right in pairs), *smalls)


def line_up(value, size):
    return lax.ppermute(value, "expert", [(i, i + 1) for i in range(size - 1)])


def line_down(value, size):
    return lax.ppermute(value, "expert", [(i + 1, i) for i in range(size - 1)])


def line_gather(value, size):
    below, above = [], []
    up, down = value, value
    for _ in range(size - 1):
        up = line_up(up, size)
        down = line_down(down, size)
        below.append(up)
        above.append(down)
    return [value] + below + above


def add_low(*terms):
    total = terms[0].astype(F32)
    for term in terms[1:]:
        total = total + term.astype(F32)
    return total.astype(BF16)


def flip(value, bit, size):
    return lax.ppermute(value, "dp", [(i, i ^ bit) for i in range(size)])


def halve(terms, bit, left, dp_place):
    axis = left.index(bit)
    own = (dp_place >> bit) & 1
    return tuple(
        add_low(*(lax.dynamic_index_in_dim(t, side, axis, keepdims=False) for t in terms)) for side in (own, 1 - own)
    )


def start_spread(routes):
    return [
        tuple(t.reshape((2,) * (t.shape[0].bit_length() - 1) + t.shape[1:]) for t in terms) for terms in routes
    ]


def step_spread(routes, stage, dp_size, dp_place):
    bits = list(range(1, dp_size.bit_length() - 1))
    kept, sent = [], []
    for terms, order in zip(routes, (bits, bits[::-1])):
        left = [bit for bit in bits[::-1] if bit not in order[:stage]]
        keep, send = halve(terms, order[stage], left, dp_place)
        kept.append(keep)
        sent.append(flip(send, 1 << order[stage], dp_size))
    sent = lax.optimization_barrier(tuple(sent))
    return list(zip(kept, sent))


def start_dense(terms):
    half = terms[0].shape[2] // 2 // LANES * LANES
    return start_spread([tuple(t[..., :half] for t in terms), tuple(t[..., half:] for t in terms)])


def pass_line(routes, place, size):
    block = jnp.concatenate([add_low(*terms) for terms in routes], axis=-1)
    parts = block.reshape(size, -1, block.shape[-1])
    passed = [lax.dynamic_index_in_dim(parts, place, 0, keepdims=False)]
    for k in range(1, size):
        part = lax.dynamic_index_in_dim(parts, (place + k) % size, 0, keepdims=False)
        passed.append(lax.ppermute(part, "expert", [(i, (i + k) % size) for i in range(size)]))
    return passed


def total_of(parts):
    total = parts[0].astype(F32)
    for part in parts[1:]:
        total = total + part.astype(F32)
    return total


def swap_top(top, axis, size):
    for bit in range(size.bit_length() - 1):
        top = jnp.maximum(top, lax.ppermute(top, axis, [(i, i ^ (1 << bit)) for i in range(size)]))
    return top


def gather_and_top(value, top, dp_size, size):
    below, above = [], []
    up, down = value, value
    for k in range(1, size):
        up, down = line_up(up, size), line_down(down, size)
        if k == 1:
            up, down, top = lax.optimization_barrier((up, down, swap_top(top, "dp", dp_size)))
        below.append(up)
        above.append(down)
    return [value] + below + above, top


def arrival_order(size):
    sources, places = np.zeros((size, size), np.int32), np.zeros((size, size), np.int32)
    for place in range(size):
        spots = [(0, place)]
        for k in range(1, size):
            if place - k >= 0:
                spots.append((k, place - k))
            if place + k < size:
                spots.append((size - 1 + k, place + k))
        sources[place], places[place] = zip(*spots)
    return sources, places


def norm_backward(hidden, factor, gain_vec, grad_in):
    scaled = grad_in * gain_vec
    hidden_grad = factor * scaled - hidden * factor**3 * jnp.mean(
        scaled * hidden, axis=-1, keepdims=True
    )
    return hidden_grad, jnp.sum(grad_in * hidden * factor, axis=0)


def local(
    tokens,
    first_gain,
    query_weight,
    key_weight,
    value_weight,
    output_weight,
    second_gain,
    router_weight,
    gate_weight,
    up_weight,
    down_weight,
    cotangent,
    routes,
    segments,
    threshold,
):
    rows, width = tokens.shape
    query_width, kv_width = query_weight.shape[1], key_weight.shape[1]
    heads, groups = query_width // HDIM, kv_width // HDIM
    ratio = heads // groups
    local_experts = gate_weight.shape[0]
    size, dp_size = lax.axis_size("expert"), lax.axis_size("dp")
    place, dp_place = lax.axis_index("expert"), lax.axis_index("dp")
    experts = local_experts * size
    expert_pad = round_up(experts, 16)
    capacity = rows * routes.shape[1] * 9 // (experts * 8)
    slot_rows = round_up(capacity, 64)

    tables = tuple(
        lax.dynamic_slice_in_dim(jnp.asarray(table), place * rows, rows, 0) for table in rotary_tables(rows * size)
    )
    seg_block = jnp.pad(segments.reshape(rows // LANES, LANES).astype(BF16), ((0, 16 - rows // LANES), (0, 0)))

    normed, first_factor, kv_own = pl.pallas_call(
        front_kernel,
        out_shape=(
            jax.ShapeDtypeStruct((rows, width), BF16),
            jax.ShapeDtypeStruct((rows, 1), F32),
            jax.ShapeDtypeStruct((groups * rows + 16, LANES), BF16),
        ),
        in_specs=[vmem()] * 7,
        out_specs=(vmem(),) * 3,
        compiler_params=params(),
        cost_estimate=cost(4),
        name="front",
    )(tokens, first_gain.reshape(1, width), key_weight, value_weight, *tables, seg_block)
    kv_slots = [kv_own]
    for _ in range(size - 1):
        kv_slots.append(line_up(kv_slots[-1], size))

    cot_own = pl.pallas_call(
        extend_kernel,
        out_shape=jax.ShapeDtypeStruct((rows, width + LANES), BF16),
        in_specs=[vmem()] * 2,
        out_specs=vmem(),
        compiler_params=params(),
        cost_estimate=cost(2),
        name="extend",
    )(cotangent, routes)
    cots = line_gather(cot_own, size)

    query_block = 512
    queries = pl.pallas_call(
        query_kernel,
        out_shape=jax.ShapeDtypeStruct((rows, query_width), BF16),
        grid=(query_width // query_block,),
        in_specs=[
            pl.BlockSpec((rows, width), lambda s: (0, 0)),
            pl.BlockSpec((width, query_block), lambda s: (0, s)),
            pl.BlockSpec((rows, LANES), lambda s: (0, 0)),
            pl.BlockSpec((rows, LANES), lambda s: (0, 0)),
        ],
        out_specs=pl.BlockSpec((rows, query_block), lambda s: (0, s)),
        compiler_params=params(),
        cost_estimate=cost(5),
        name="queries",
    )(normed, query_weight, *tables)

    place_word = place.reshape(1).astype(jnp.int32)
    attended, lse, top = attend(queries, kv_slots, place_word, groups)
    head_top = jnp.max(top.reshape(heads, rows), axis=1).reshape(1, heads)

    hidden_in = tokens.astype(F32)
    hidden_mid = hidden_in + RESIDUAL_SCALE * dot(attended, output_weight, NT)
    second_factor = lax.rsqrt(jnp.mean(hidden_mid * hidden_mid, axis=-1, keepdims=True) + NORM_EPSILON)
    second_normed = (hidden_mid * second_factor * second_gain).astype(BF16)
    normed_blocks, head_top = gather_and_top(second_normed, head_top, dp_size, size)

    router_t = jnp.pad(router_weight.T, ((0, expert_pad - experts), (0, 0)))
    sources, blocks_of = (jnp.asarray(table)[place] for table in arrival_order(size))
    expert_place = jnp.concatenate([(place * local_experts).reshape(1), sources, blocks_of]).astype(jnp.int32)
    saved, grad_blocks, router_part = run_experts(
        expert_place, router_t, gate_weight, up_weight, down_weight, normed_blocks, cots, slot_rows
    )
    grad_blocks = lax.all_to_all(grad_blocks, "expert", 0, 0, tiled=True)

    dp_word = dp_place.reshape(1).astype(jnp.int32)
    mixture = run_mixture(blocks_of, down_weight, saved, slot_rows)
    received = [flip(part, 1, dp_size) for part in run_expert_grads(dp_word, saved, dp_size)]
    keep_a, send_a, keep_b, send_b = run_expert_grads(dp_word, saved, dp_size, received)
    mixture, grad_blocks, send_a, send_b = lax.optimization_barrier((mixture, grad_blocks, send_a, send_b))
    normed_grad = jnp.sum(grad_blocks.astype(F32), axis=0)
    passed = (flip(send_a, 2, dp_size), flip(send_b, dp_size // 2, dp_size))
    mix_one = lax.all_to_all(mixture[0], "expert", 0, 0, tiled=True)

    out_grad = cotangent.astype(F32)
    mid_back, second_gain_part = norm_backward(hidden_mid, second_factor, second_gain, normed_grad)
    mid_grad = out_grad + mid_back
    branch_grad = (RESIDUAL_SCALE * mid_grad).astype(BF16)
    attended_grad = dot(branch_grad, output_weight).astype(BF16)
    query_back, dkv = attend_back(
        queries, attended, attended_grad, lse, tables, kv_slots, place_word, groups
    )
    keep, send = dense_grads(dp_word, [(branch_grad, attended), (normed, query_back)], dp_size)
    stages = dp_size.bit_length() - 2
    from_above = line_down(dkv[size - 1], size)
    from_above, passed, mix_one, keep, send = lax.optimization_barrier((from_above, passed, mix_one, keep, send))
    wide = start_dense((keep, flip(send, 1, dp_size)))
    for k in range(1, size):
        if k > 1:
            from_above = line_down(down, size)
        if k == size - 2:
            from_above, wide = lax.optimization_barrier((from_above, wide))
        if k < size - 1:
            down = add_low(from_above, dkv[size - 1 - k])
    from_above, passed, head_top = lax.optimization_barrier((from_above, passed, head_top))
    head_top = swap_top(head_top, "expert", size)
    mix_two, head_top = lax.optimization_barrier((mixture[1], head_top))
    head_top = head_top.reshape(heads)
    expert_sums = step_spread(start_spread([(keep_a, passed[0]), (keep_b, passed[1])]), 1, dp_size, dp_place)
    mix_two = lax.all_to_all(mix_two, "expert", 0, 0, tiled=True)
    for stage in range(stages):
        wide = step_spread(wide, stage, dp_size, dp_place)
    key_back, value_back = pl.pallas_call(
        unpack_kernel,
        out_shape=(jax.ShapeDtypeStruct((rows, kv_width), BF16),) * 2,
        in_specs=[vmem()] * 4,
        out_specs=(vmem(),) * 2,
        compiler_params=params(),
        cost_estimate=cost(2),
        name="unpack",
    )(dkv[0], from_above, *tables)

    first_grad = dot(query_back, query_weight, NT)
    first_grad = first_grad + dot(key_back, key_weight, NT)
    first_grad = first_grad + dot(value_back, value_weight, NT)
    input_back, first_gain_part = norm_backward(hidden_in, first_factor, first_gain, first_grad)
    input_grad = mid_grad + input_back
    keep, send = dense_grads(
        dp_word,
        [(normed, key_back), (normed, value_back)],
        dp_size,
        (router_part, second_gain_part[None], first_gain_part[None]),
    )
    keep, send, wide, expert_sums = lax.optimization_barrier((keep, send, wide, expert_sums))
    rest = start_dense((keep, flip(send, 1, dp_size)))
    rest = step_spread(rest, 0, dp_size, dp_place)
    rest, expert_sums, mix_two = lax.optimization_barrier((rest, expert_sums, mix_two))
    for stage in range(1, stages):
        rest = step_spread(rest, stage, dp_size, dp_place)
    wide_parts, rest, expert_sums, mix_two = lax.optimization_barrier(
        (pass_line(wide, place, size), rest, expert_sums, mix_two)
    )
    for stage in range(2, stages):
        expert_sums = step_spread(expert_sums, stage, dp_size, dp_place)
    expert_sums = [
        jnp.concatenate([a[w].astype(F32) + b[w].astype(F32) for a, b in expert_sums], axis=-1) for w in range(3)
    ]
    rest_parts = lax.optimization_barrier(pass_line(rest, place, size))
    wide_grad, rest_grad = total_of(wide_parts), total_of(rest_parts)
    mixture = jnp.concatenate([jnp.sum(part.astype(F32), axis=0) for part in (mix_one, mix_two)], axis=1)
    block_out = (hidden_mid + mixture).astype(BF16)
    projection_grad, query_grad = wide_grad[:, :query_width], wide_grad[:, query_width:]
    key_grad = rest_grad[:, :kv_width]
    value_grad = rest_grad[:, kv_width : 2 * kv_width]
    small_grad = rest_grad[:, 2 * kv_width :]

    head_scale = threshold / jnp.maximum(head_top, threshold)
    group_scale = jnp.min(head_scale.reshape(groups, ratio), axis=1)
    row_count = width // (dp_size * size)
    row_start = (dp_place * size + place) * row_count
    query_rows = lax.dynamic_slice_in_dim(query_weight, row_start, row_count, 0).astype(F32)
    key_rows = lax.dynamic_slice_in_dim(key_weight, row_start, row_count, 0).astype(F32)
    query_clipped = (query_rows * jnp.repeat(jnp.sqrt(head_scale), HDIM)[None, :]).astype(BF16)
    key_clipped = (key_rows * jnp.repeat(jnp.sqrt(group_scale), HDIM)[None, :]).astype(BF16)
    return (
        block_out,
        input_grad,
        small_grad[:, expert_pad + 1],
        query_grad,
        key_grad,
        value_grad,
        projection_grad,
        small_grad[:, expert_pad],
        small_grad[:, :experts],
        expert_sums[0],
        expert_sums[1],
        expert_sums[2],
        head_scale,
        query_clipped,
        key_clipped,
    )


def solution(mesh):
    row = P(("dp", "expert"), None)
    vector = P(("dp", "expert"))
    expert_in = P("expert", None, None)
    expert_out = P("expert", "dp", None)
    return jax.shard_map(
        local,
        mesh=mesh,
        in_specs=(row,) + (P(),) * 7 + (expert_in,) * 3 + (row, row, vector, P()),
        out_specs=(row, row, vector)
        + (row,) * 4
        + (vector, row)
        + (expert_out,) * 3
        + (P(), row, row),
        check_vma=False,
    )
```

```python
import functools

import jax
import jax.numpy as jnp
import numpy as np
from jax import lax
from jax.experimental import pallas as pl
from jax.experimental.pallas import tpu as pltpu
from jax.sharding import PartitionSpec as P

HDIM = 64
LANES = 128
ATTENTION_SCALE = 0.015625
RESIDUAL_SCALE = 0.22
NORM_EPSILON = 1e-06
ROTARY_BASE = 10000.0
MASKED_SCORE = -1e30
BF16 = jnp.bfloat16
F32 = jnp.float32
NN = (((1,), (0,)), ((), ()))
NT = (((1,), (1,)), ((), ()))
TN = (((0,), (0,)), ((), ()))
VMEM_LIMIT = 60 * 1024 * 1024
COLUMNS = 512


def dot(left, right, dims=NN):
    return lax.dot_general(left, right, dims, preferred_element_type=F32)


def round_up(count, unit):
    return (count + unit - 1) // unit * unit


def low_lanes(rows):
    return lax.broadcasted_iota(jnp.int32, (rows, LANES), 1) < HDIM


def partner_lanes(slab):
    lane = lax.broadcasted_iota(jnp.int32, slab.shape, 1) % HDIM
    half = HDIM // 2
    return jnp.where(lane < half, pltpu.roll(slab, LANES - half, 1), pltpu.roll(slab, half, 1))


def vmem():
    return pl.BlockSpec(memory_space=pltpu.VMEM)


def params(**more):
    return pltpu.CompilerParams(vmem_limit_bytes=VMEM_LIMIT, **more)


def cost(microseconds):
    return pl.CostEstimate(flops=int(microseconds * 1e6), bytes_accessed=0, transcendentals=0)


def rotary_tables(length):
    half = HDIM // 2
    inverse = np.float32(ROTARY_BASE) ** (np.float32(-2.0) * np.arange(half, dtype=np.float32) / np.float32(HDIM))
    angles = np.arange(length, dtype=np.float32)[:, None] * np.tile(inverse, LANES // half)[None, :]
    angles = angles.astype(np.float32).astype(np.float64)
    sign = np.where(np.arange(LANES) % HDIM < half, -1.0, 1.0)
    return np.cos(angles).astype(np.float32), (np.sin(angles) * sign).astype(np.float32)


def extend_kernel(cotangent_ref, routes_ref, out_ref):
    rows, top_count = routes_ref.shape
    width = cotangent_ref.shape[1]
    lane = lax.broadcasted_iota(jnp.int32, (rows, LANES), 1)
    chosen = jnp.zeros((rows, LANES), F32)
    for k in range(top_count):
        chosen = chosen + jnp.where(routes_ref[:, k : k + 1] == lane, 1.0, 0.0)
    first = lax.broadcasted_iota(jnp.int32, (rows, rows), 0)
    second = lax.broadcasted_iota(jnp.int32, (rows, rows), 1)
    earlier = jnp.where(second < first, 1.0, 0.0).astype(BF16)
    rank = dot(earlier, chosen.astype(BF16))
    out_ref[:, :width] = cotangent_ref[...]
    out_ref[:, width:] = jnp.where(chosen > 0.5, rank, -1.0).astype(BF16)


def front_kernel(tokens_ref, gain_ref, key_ref, value_ref, cos_ref, sin_ref, segments_ref, normed_ref, factor_ref, kv_ref):
    hidden = tokens_ref[...].astype(F32)
    factor = lax.rsqrt(jnp.mean(hidden * hidden, axis=-1, keepdims=True) + NORM_EPSILON)
    normed = (hidden * factor * gain_ref[...]).astype(BF16)
    normed_ref[...] = normed
    factor_ref[...] = factor
    keys = dot(normed, key_ref[...])
    values = dot(normed, value_ref[...])
    cosine, sine = cos_ref[...], sin_ref[...]
    rows = hidden.shape[0]
    low = low_lanes(rows)
    for i in range(keys.shape[1] // LANES):
        slab = keys[:, i * LANES : (i + 1) * LANES]
        slab = slab * cosine + partner_lanes(slab) * sine
        value_slab = values[:, i * LANES : (i + 1) * LANES]
        even, odd = 2 * i * rows, (2 * i + 1) * rows
        kv_ref[even : even + rows, :] = jnp.where(low, slab, pltpu.roll(value_slab, HDIM, 1)).astype(BF16)
        kv_ref[odd : odd + rows, :] = jnp.where(low, pltpu.roll(slab, HDIM, 1), value_slab).astype(BF16)
    kv_ref[keys.shape[1] // HDIM * rows :, :] = segments_ref[...]


def query_kernel(normed_ref, query_ref, cos_ref, sin_ref, out_ref):
    raw = dot(normed_ref[...], query_ref[...])
    cosine, sine = cos_ref[...], sin_ref[...]
    for i in range(raw.shape[1] // LANES):
        slab = raw[:, i * LANES : (i + 1) * LANES]
        slab = slab * cosine + partner_lanes(slab) * sine
        out_ref[:, i * LANES : (i + 1) * LANES] = (slab.astype(BF16).astype(F32) * ATTENTION_SCALE).astype(BF16)


def fill_bias(bias_ref, need_ref, place_ref, seg_row, seg_columns):
    slots, keys, rows = bias_ref.shape
    for k in range(slots):
        allowed = seg_columns[k] == seg_row
        if k == 0:
            allowed = allowed & (
                lax.broadcasted_iota(jnp.int32, (keys, rows), 0) <= lax.broadcasted_iota(jnp.int32, (keys, rows), 1)
            )
        bias_ref[k] = jnp.where(allowed, 0.0, MASKED_SCORE)
    first = jnp.min(seg_row)
    need = jnp.int32(1)
    for k in range(1, slots):
        need = jnp.where((jnp.max(seg_columns[k]) >= first) & (k <= place_ref[0]), k + 1, need)
    need_ref[0] = need


def prepare_bias(bias_ref, need_ref, place_ref, seg_refs):
    slots, keys, _ = bias_ref.shape
    halves = keys // LANES
    seg_rows = [
        jnp.concatenate([ref[j : j + 1, :].astype(F32) for j in range(halves)], axis=1) for ref in seg_refs
    ]
    seg_columns = [jnp.broadcast_to(row, (LANES, keys)).T[:, :1] for row in seg_rows]
    fill_bias(bias_ref, need_ref, place_ref, seg_rows[0], seg_columns)


def head_slab(block, head, upper):
    slab = block[:, (head // 2) * LANES : (head // 2 + 1) * LANES].astype(F32)
    low = low_lanes(slab.shape[0])
    if (head % 2 == 1) != upper:
        slab = pltpu.roll(slab, HDIM, 1)
    return jnp.where(low != upper, slab, 0.0)


def add_bias(scores, bias, ratio):
    rows = bias.shape[1]
    return jnp.concatenate([scores[:, r * rows : (r + 1) * rows] + bias for r in range(ratio)], axis=1)


def attend_kernel(slots, ratio, place_ref, query_ref, *refs):
    kv_refs, seg_refs = refs[:slots], refs[slots : 2 * slots]
    attended_ref, lse_ref, top_ref, bias_ref, stacked_ref, scores_ref, acc_ref, max_ref, need_ref = refs[2 * slots :]
    rows = query_ref.shape[0]
    low = low_lanes(rows)

    @pl.when(pl.program_id(0) == 0)
    def _():
        prepare_bias(bias_ref, need_ref, place_ref, seg_refs)

    need = need_ref[0]
    outs = []
    for group in range(2):
        for r in range(ratio):
            stacked_ref[r * rows : (r + 1) * rows, :] = head_slab(
                query_ref, group * ratio + r, False
            ).astype(BF16)
        for k in range(slots):

            def score(k=k):
                kv = kv_refs[k][group * rows : (group + 1) * rows, :]
                scores = add_bias(dot(kv, stacked_ref[...], NT), bias_ref[k], ratio)
                scores_ref[k] = scores
                top = jnp.max(scores, axis=0, keepdims=True)
                max_ref[...] = top if k == 0 else jnp.maximum(max_ref[...], top)

            if k == 0:
                score()
            else:
                pl.when(k < need)(score)
        for k in range(slots):

            def mix(k=k):
                kv = kv_refs[k][group * rows : (group + 1) * rows, :]
                kv = jnp.where(low, jnp.ones_like(kv), kv)
                weights = jnp.exp(scores_ref[k] - max_ref[...]).astype(BF16)
                part = dot(kv, weights, TN)
                acc_ref[...] = part if k == 0 else acc_ref[...] + part

            if k == 0:
                mix()
            else:
                pl.when(k < need)(mix)
        total = acc_ref[:1, :]
        lse_ref[0, group : group + 1, :] = max_ref[...] + jnp.log(total)
        top_ref[0, group : group + 1, :] = max_ref[...]
        mixed = acc_ref[HDIM:, :] / total
        for r in range(ratio):
            outs.append(mixed[:, r * rows : (r + 1) * rows])
    for i in range(len(outs) // 2):
        slab = jnp.concatenate([outs[2 * i], outs[2 * i + 1]], axis=0)
        attended_ref[:, i * LANES : (i + 1) * LANES] = slab.T.astype(BF16)


def kv_specs(slots, groups, rows):
    return [pl.BlockSpec((2 * rows, LANES), lambda s: (s, 0))] * slots + [
        pl.BlockSpec((16, LANES), lambda s: (groups * rows // 16, 0))
    ] * slots


def attend(queries, kv_slots, place, groups):
    slots = len(kv_slots)
    rows, width = queries.shape
    ratio = width // HDIM // groups
    steps = groups // 2
    block = 2 * ratio * HDIM
    stats = pl.BlockSpec((1, 2, ratio * rows), lambda s: (s, 0, 0))
    return pl.pallas_call(
        functools.partial(attend_kernel, slots, ratio),
        out_shape=(jax.ShapeDtypeStruct((rows, width), BF16),)
        + (jax.ShapeDtypeStruct((steps, 2, ratio * rows), F32),) * 2,
        grid=(steps,),
        in_specs=[
            pl.BlockSpec(memory_space=pltpu.SMEM),
            pl.BlockSpec((rows, block), lambda s: (0, s)),
        ]
        + kv_specs(slots, groups, rows),
        out_specs=(pl.BlockSpec((rows, block), lambda s: (0, s)), stats, stats),
        scratch_shapes=[
            pltpu.VMEM((slots, rows, rows), F32),
            pltpu.VMEM((ratio * rows, LANES), BF16),
            pltpu.VMEM((slots, rows, ratio * rows), F32),
            pltpu.VMEM((LANES, ratio * rows), F32),
            pltpu.VMEM((1, ratio * rows), F32),
            pltpu.SMEM((1,), jnp.int32),
        ],
        compiler_params=params(),
        cost_estimate=cost(20),
        name="attend",
    )(place, queries, *kv_slots, *kv_slots)


def attend_back_kernel(slots, ratio, place_ref, query_ref, attended_ref, grad_ref, lse_ref, cos_ref, sin_ref, *refs):
    kv_refs, seg_refs = refs[:slots], refs[slots : 2 * slots]
    refs = refs[2 * slots :]
    back_ref, dkv_refs = refs[0], refs[1 : slots + 1]
    bias_ref, query_s, grad_s, acc_ref, delta_s, need_ref = refs[slots + 1 :]
    rows = query_ref.shape[0]

    @pl.when(pl.program_id(0) == 0)
    def _():
        prepare_bias(bias_ref, need_ref, place_ref, seg_refs)

    need = need_ref[0]
    outs = []
    for group in range(2):
        for r in range(ratio):
            head = group * ratio + r
            part = slice(r * rows, (r + 1) * rows)
            query_s[part, :] = head_slab(query_ref, head, False).astype(BF16)
            grad = head_slab(grad_ref, head, True)
            grad_s[part, :] = grad.astype(BF16)
            product = (grad * head_slab(attended_ref, head, True)).T
            delta_s[:, part] = jnp.sum(product, axis=0, keepdims=True)
        for k in range(slots):

            def step(k=k):
                kv = kv_refs[k][group * rows : (group + 1) * rows, :]
                scores = add_bias(dot(kv, query_s[...], NT), bias_ref[k], ratio)
                weights = jnp.exp(scores - lse_ref[0, group : group + 1, :])
                weight_grad = dot(kv, grad_s[...], NT)
                score_grad = (weights * (weight_grad - delta_s[...])).astype(BF16)
                part = dot(kv, score_grad, TN)
                acc_ref[...] = part if k == 0 else acc_ref[...] + part
                dkv_refs[k][group * rows : (group + 1) * rows, :] = (
                    dot(score_grad, query_s[...]) + dot(weights.astype(BF16), grad_s[...])
                ).astype(BF16)

            if k == 0:
                step()
            else:
                pl.when(k < need)(step)

                @pl.when(k >= need)
                def _(k=k):
                    dkv_refs[k][group * rows : (group + 1) * rows, :] = jnp.zeros((rows, LANES), BF16)

        for r in range(ratio):
            outs.append(acc_ref[:HDIM, r * rows : (r + 1) * rows] * ATTENTION_SCALE)
    cosine, sine = cos_ref[...], sin_ref[...]
    for i in range(len(outs) // 2):
        slab = jnp.concatenate([outs[2 * i], outs[2 * i + 1]], axis=0).T
        slab = slab * cosine - partner_lanes(slab) * sine
        back_ref[:, i * LANES : (i + 1) * LANES] = slab.astype(BF16)


def attend_back(queries, attended, grad, lse, tables, kv_slots, place, groups):
    slots = len(kv_slots)
    rows, width = queries.shape
    ratio = width // HDIM // groups
    steps = groups // 2
    block = 2 * ratio * HDIM
    whole = pl.BlockSpec((rows, LANES), lambda s: (0, 0))
    wide = pl.BlockSpec((rows, block), lambda s: (0, s))
    out = pl.pallas_call(
        functools.partial(attend_back_kernel, slots, ratio),
        out_shape=(jax.ShapeDtypeStruct((rows, width), BF16),)
        + (jax.ShapeDtypeStruct((groups * rows, LANES), BF16),) * slots,
        grid=(steps,),
        in_specs=[
            pl.BlockSpec(memory_space=pltpu.SMEM),
            wide,
            wide,
            wide,
            pl.BlockSpec((1, 2, ratio * rows), lambda s: (s, 0, 0)),
            whole,
            whole,
        ]
        + kv_specs(slots, groups, rows),
        out_specs=(wide,) + (pl.BlockSpec((2 * rows, LANES), lambda s: (s, 0)),) * slots,
        scratch_shapes=[
            pltpu.VMEM((slots, rows, rows), F32),
            pltpu.VMEM((ratio * rows, LANES), BF16),
            pltpu.VMEM((ratio * rows, LANES), BF16),
            pltpu.VMEM((LANES, ratio * rows), F32),
            pltpu.VMEM((1, ratio * rows), F32),
            pltpu.SMEM((1,), jnp.int32),
        ],
        compiler_params=params(),
        cost_estimate=cost(2),
        name="attend_back",
    )(place, queries, attended, grad, lse, *tables, *kv_slots, *kv_slots)
    return out[0], out[1:]


def unpack_kernel(own_ref, above_ref, cos_ref, sin_ref, key_ref, value_ref):
    rows = cos_ref.shape[0]
    low = low_lanes(rows)
    cosine, sine = cos_ref[...], sin_ref[...]
    for i in range(key_ref.shape[1] // LANES):
        even, odd = (
            own_ref[g * rows : (g + 1) * rows, :].astype(F32) + above_ref[g * rows : (g + 1) * rows, :].astype(F32)
            for g in (2 * i, 2 * i + 1)
        )
        slab = jnp.where(low, even, pltpu.roll(odd, HDIM, 1))
        slab = slab * cosine - partner_lanes(slab) * sine
        key_ref[:, i * LANES : (i + 1) * LANES] = slab.astype(BF16)
        value_ref[:, i * LANES : (i + 1) * LANES] = jnp.where(
            low, pltpu.roll(even, HDIM, 1), odd
        ).astype(BF16)


def expert_kernel(blocks, slot_rows, local_experts, place_ref, router_ref, gate_ref, up_ref, down_ref, *refs):
    sources = 2 * blocks - 1
    normed_in, cot_in = refs[:sources], refs[sources : 2 * sources]
    xs_out, cs_out, hs_ref, gate_grad_ref, up_grad_ref, hits, grad_out, router_grad_ref = refs[2 * sources : 2 * sources + 8]
    x_all, c_all, info, gates, back, xs_all, cs_all, gate_slots, slot_grads, sems, save_sem, out_sem = refs[2 * sources + 8 :]
    step = pl.program_id(0)
    rows, width = x_all.shape[1:]
    expert_pad = router_ref.shape[0]
    first_expert = place_ref[0]
    mine = pl.ds(first_expert + step, 1)

    def source_copies(i, s):
        return (
            pltpu.make_async_copy(normed_in[s], x_all.at[i], sems.at[0, i]),
            pltpu.make_async_copy(cot_in[s], c_all.at[i], sems.at[1, i]),
        )

    def save_copies():
        return (
            pltpu.make_async_copy(xs_all, xs_out, save_sem.at[0]),
            pltpu.make_async_copy(cs_all, cs_out, save_sem.at[1]),
        )

    @pl.when(step == 0)
    def _():
        for i in range(blocks):
            for s in range(sources):

                @pl.when(place_ref[1 + i] == s)
                def _(i=i, s=s):
                    for copy in source_copies(i, s):
                        copy.start()

        same = jnp.where(
            lax.broadcasted_iota(jnp.int32, (rows, rows), 0) == lax.broadcasted_iota(jnp.int32, (rows, rows), 1),
            1.0,
            0.0,
        ).astype(BF16)
        slot_ids = lax.broadcasted_iota(jnp.int32, (slot_rows, rows), 0).astype(F32)
        back[...] = jnp.zeros_like(back)
        for i in range(blocks):
            for copy in source_copies(i, 0):
                copy.wait()
            info[i] = dot(c_all[i, :, width:], same, TN)
            logits = dot(router_ref[...], x_all[i], NT)
            logits = jnp.where(info[i, :expert_pad, :] >= 0, logits, MASKED_SCORE)
            weights = jnp.exp(logits - jnp.max(logits, axis=0, keepdims=True))
            gates[i] = weights / jnp.sum(weights, axis=0, keepdims=True)
            for e in range(local_experts):
                own = pl.ds(first_expert + e, 1)
                hit = slot_ids == info[i, own, :]
                gate_slots[e, i * slot_rows : (i + 1) * slot_rows, :] = RESIDUAL_SCALE * jnp.sum(
                    jnp.where(hit, gates[i, own, :], 0.0), axis=-1, keepdims=True
                )
                hits[i, e * slot_rows : (e + 1) * slot_rows, :] = jnp.where(hit, 1.0, 0.0).astype(BF16)
            for source, target in ((x_all, xs_all), (c_all, cs_all)):
                for c in range(width // COLUMNS):
                    columns = slice(c * COLUMNS, (c + 1) * COLUMNS)
                    picked = dot(hits[i], source[i, :, columns]).astype(BF16)
                    for e in range(local_experts):
                        target[e, i * slot_rows : (i + 1) * slot_rows, columns] = picked[
                            e * slot_rows : (e + 1) * slot_rows
                        ]
        for copy in save_copies():
            copy.start()

    gate_slot = gate_slots[step]
    gate_pre = dot(xs_all[step], gate_ref[0])
    up_pre = dot(xs_all[step], up_ref[0])
    raw_grad = dot(cs_all[step], down_ref[0])
    sigmoid = 1.0 / (1.0 + jnp.exp(-gate_pre))
    active = gate_pre * sigmoid
    expert_hidden = (active * up_pre).astype(BF16).astype(F32)
    hs_ref[0] = (expert_hidden * gate_slot).astype(BF16)
    back_slot = jnp.sum(expert_hidden * raw_grad, axis=-1, keepdims=True) * RESIDUAL_SCALE
    hidden_grad = raw_grad * gate_slot
    gate_grad_ref[0] = (hidden_grad * up_pre * sigmoid * (1.0 + gate_pre * (1.0 - sigmoid))).astype(BF16)
    up_grad_ref[0] = (hidden_grad * active).astype(BF16)
    spot = pl.ds(pl.multiple_of(step * slot_rows, slot_rows), slot_rows)
    for c in range(width // COLUMNS):
        columns = slice(c * COLUMNS, (c + 1) * COLUMNS)
        slot_grad = (
            dot(gate_grad_ref[0], gate_ref[0, columns, :], NT) + dot(up_grad_ref[0], up_ref[0, columns, :], NT)
        ).astype(BF16)
        for i in range(blocks):
            slot_grads[i, spot, columns] = slot_grad[i * slot_rows : (i + 1) * slot_rows]
    for i in range(blocks):
        part = slice(i * slot_rows, (i + 1) * slot_rows)
        back_row = jnp.sum(hits[i, spot, :].astype(F32) * back_slot[part], axis=0, keepdims=True)
        back[i, mine, :] = back_row * gates[i, mine, :]

    @pl.when(step == local_experts - 1)
    def _():
        def copy(i):
            return pltpu.make_async_copy(
                c_all.at[i, :, pl.ds(0, width)], grad_out.at[place_ref[1 + blocks + i]], out_sem.at[i]
            )

        router_sum = None
        for i in range(blocks):
            share = back[i]
            logit_grad = (share - gates[i] * jnp.sum(share, axis=0, keepdims=True)).astype(BF16)
            turned = hits[i].T
            for c in range(width // COLUMNS):
                columns = slice(c * COLUMNS, (c + 1) * COLUMNS)
                c_all[i, :, columns] = (
                    dot(turned, slot_grads[i, :, columns]) + dot(logit_grad, router_ref[:, columns], TN)
                ).astype(BF16)
            copy(i).start()
            part = dot(logit_grad, x_all[i])
            router_sum = part if router_sum is None else router_sum + part
        router_grad_ref[...] = router_sum
        for i in range(blocks):
            copy(i).wait()
        for saved in save_copies():
            saved.wait()


def run_experts(place, router_t, gate_weight, up_weight, down_weight, normed, cots, slot_rows):
    local_experts, width, hidden = gate_weight.shape
    sources = len(normed)
    blocks = (sources + 1) // 2
    rows = normed[0].shape[0]
    expert_pad = router_t.shape[0]
    slots = blocks * slot_rows
    stacked = local_experts * slot_rows
    anywhere = pl.BlockSpec(memory_space=pl.ANY)
    weight_spec = pl.BlockSpec((1, width, hidden), lambda e, place: (e, 0, 0))
    narrow = pl.BlockSpec((1, slots, hidden), lambda e, place: (e, 0, 0))
    wide_shape = jax.ShapeDtypeStruct((local_experts, slots, width), BF16)
    narrow_shape = jax.ShapeDtypeStruct((local_experts, slots, hidden), BF16)
    out = pl.pallas_call(
        functools.partial(expert_kernel, blocks, slot_rows, local_experts),
        out_shape=(
            wide_shape,
            wide_shape,
            narrow_shape,
            narrow_shape,
            narrow_shape,
            jax.ShapeDtypeStruct((blocks, stacked, rows), BF16),
            jax.ShapeDtypeStruct((blocks, rows, width), BF16),
            jax.ShapeDtypeStruct((expert_pad, width), F32),
        ),
        grid_spec=pltpu.PrefetchScalarGridSpec(
            num_scalar_prefetch=1,
            grid=(local_experts,),
            in_specs=[pl.BlockSpec((expert_pad, width), lambda e, place: (0, 0))]
            + [weight_spec] * 3
            + [anywhere] * (2 * sources),
            out_specs=(
                anywhere,
                anywhere,
                narrow,
                narrow,
                narrow,
                pl.BlockSpec((blocks, stacked, rows), lambda e, place: (0, 0, 0)),
                anywhere,
                pl.BlockSpec((expert_pad, width), lambda e, place: (0, 0)),
            ),
            scratch_shapes=[
                pltpu.VMEM((blocks, rows, width), BF16),
                pltpu.VMEM((blocks, rows, width + LANES), BF16),
                pltpu.VMEM((blocks, LANES, rows), F32),
                pltpu.VMEM((blocks, expert_pad, rows), F32),
                pltpu.VMEM((blocks, expert_pad, rows), F32),
                pltpu.VMEM((local_experts, slots, width), BF16),
                pltpu.VMEM((local_experts, slots, width), BF16),
                pltpu.VMEM((local_experts, slots, 1), F32),
                pltpu.VMEM((blocks, stacked, width), BF16),
                pltpu.SemaphoreType.DMA((2, blocks)),
                pltpu.SemaphoreType.DMA((2,)),
                pltpu.SemaphoreType.DMA((blocks,)),
            ],
        ),
        compiler_params=params(),
        cost_estimate=cost(45),
        name="experts",
    )(place, router_t, gate_weight, up_weight, down_weight, *normed, *cots)
    return out[:6], out[6], out[7]


def mixture_kernel(blocks, slot_rows, local_experts, order_ref, down_ref, hs_ref, hits_ref, mix_one, mix_two, slot_outs, mix_low, out_sem):
    step = pl.program_id(0)
    width = down_ref.shape[1]
    spot = pl.ds(pl.multiple_of(step * slot_rows, slot_rows), slot_rows)
    for c in range(width // COLUMNS):
        columns = slice(c * COLUMNS, (c + 1) * COLUMNS)
        slot_out = dot(hs_ref[0], down_ref[0, columns, :], NT).astype(BF16)
        for i in range(blocks):
            slot_outs[i, spot, columns] = slot_out[i * slot_rows : (i + 1) * slot_rows]

    @pl.when(step == local_experts - 1)
    def _():
        def copy(i, h):
            columns = pl.ds(h * (width // 2), width // 2)
            return pltpu.make_async_copy(
                mix_low.at[i, :, columns], (mix_one, mix_two)[h].at[order_ref[i]], out_sem.at[i, h]
            )

        for i in range(blocks):
            turned = hits_ref[i].T
            for c in range(width // COLUMNS):
                columns = slice(c * COLUMNS, (c + 1) * COLUMNS)
                mix_low[i, :, columns] = dot(turned, slot_outs[i, :, columns]).astype(BF16)
            for h in range(2):
                copy(i, h).start()
        for i in range(blocks):
            for h in range(2):
                copy(i, h).wait()


def run_mixture(order, down_weight, saved, slot_rows):
    hs, hits = saved[2], saved[5]
    local_experts, width, hidden = down_weight.shape
    blocks, stacked, rows = hits.shape
    return pl.pallas_call(
        functools.partial(mixture_kernel, blocks, slot_rows, local_experts),
        out_shape=(jax.ShapeDtypeStruct((blocks, rows, width // 2), BF16),) * 2,
        grid_spec=pltpu.PrefetchScalarGridSpec(
            num_scalar_prefetch=1,
            grid=(local_experts,),
            in_specs=[
                pl.BlockSpec((1, width, hidden), lambda e, order: (e, 0, 0)),
                pl.BlockSpec((1, hs.shape[1], hidden), lambda e, order: (e, 0, 0)),
                pl.BlockSpec((blocks, stacked, rows), lambda e, order: (0, 0, 0)),
            ],
            out_specs=(pl.BlockSpec(memory_space=pl.ANY),) * 2,
            scratch_shapes=[
                pltpu.VMEM((blocks, stacked, width), BF16),
                pltpu.VMEM((blocks, rows, width), BF16),
                pltpu.SemaphoreType.DMA((blocks, 2)),
            ],
        ),
        compiler_params=params(),
        cost_estimate=cost(10),
        name="mixture",
    )(order, down_weight, hs, hits)


def turn_rows(block, sides_ref, owned):
    width = block.shape[1]
    chunk = int(np.lcm(2 * owned, LANES))
    for c in range(width // chunk):
        turned = block[:, c * chunk : (c + 1) * chunk].T
        for o in range(chunk // owned):
            owner = c * (chunk // owned) + o
            spot = owner // 2 * owned
            sides_ref[owner % 2, spot : spot + owned, :] = turned[o * owned : (o + 1) * owned]


def grad_products(side, xs_ref, cs_ref, hs_ref, gate_grad_ref, up_grad_ref, sides, owned):
    for left_ref, rights in ((xs_ref, ((0, gate_grad_ref), (1, up_grad_ref))), (cs_ref, ((2, hs_ref),))):
        turn_rows(left_ref[0], sides, owned)
        for w, right_ref in rights:
            yield w, dot(sides[side], right_ref[0])


def expert_send_kernel(place_ref, xs_ref, cs_ref, hs_ref, gate_grad_ref, up_grad_ref, *refs):
    send_refs, sides = refs[:-1], refs[-1]
    owned = send_refs[0].shape[2]
    side = 1 - place_ref[0] % 2
    for w, grad in grad_products(side, xs_ref, cs_ref, hs_ref, gate_grad_ref, up_grad_ref, sides, owned):
        for q, send_ref in enumerate(send_refs):
            send_ref[w, 0] = grad[q * owned : (q + 1) * owned].astype(BF16)


def expert_keep_kernel(bits, place_ref, xs_ref, cs_ref, hs_ref, gate_grad_ref, up_grad_ref, *refs):
    count = 1 << (bits - 1)
    received_refs, outs, sides = refs[:count], refs[count : count + 4], refs[-1]
    owned = received_refs[0].shape[2]
    hidden = hs_ref.shape[2] // 2
    side = place_ref[0] % 2
    for w, grad in grad_products(side, xs_ref, cs_ref, hs_ref, gate_grad_ref, up_grad_ref, sides, owned):
        for q in range(count):
            piece = (grad[q * owned : (q + 1) * owned] + received_refs[q][w, 0].astype(F32)).astype(BF16)
            for route, bit in enumerate((1, bits - 1)):
                part = piece[:, route * hidden : (route + 1) * hidden]
                own = (place_ref[0] >> bit) & 1
                spot = (q >> bit << (bit - 1)) | (q & ((1 << (bit - 1)) - 1))
                here = q >> (bit - 1) & 1

                @pl.when(own == here)
                def _(route=route, part=part, spot=spot, w=w):
                    outs[2 * route][spot, w, 0] = part

                @pl.when(own != here)
                def _(route=route, part=part, spot=spot, w=w):
                    outs[2 * route + 1][spot, w, 0] = part


def run_expert_grads(dp_word, saved, owners, received=()):
    xs, cs, hs, gate_grad, up_grad, _ = saved
    local_experts, slots, width = xs.shape
    hidden = hs.shape[2]
    owned = width // owners
    wide = pl.BlockSpec((1, slots, width), lambda e, place: (e, 0, 0))
    narrow = pl.BlockSpec((1, slots, hidden), lambda e, place: (e, 0, 0))
    pass_spec = pl.BlockSpec((3, 1, owned, hidden), lambda e, place: (0, e, 0, 0))
    pass_shape = jax.ShapeDtypeStruct((3, local_experts, owned, hidden), BF16)
    part_spec = pl.BlockSpec((owners // 4, 3, 1, owned, hidden // 2), lambda e, place: (0, 0, e, 0, 0))
    part_shape = jax.ShapeDtypeStruct((owners // 4, 3, local_experts, owned, hidden // 2), BF16)
    return pl.pallas_call(
        functools.partial(expert_keep_kernel, owners.bit_length() - 1) if received else expert_send_kernel,
        out_shape=(part_shape,) * 4 if received else (pass_shape,) * (owners // 2),
        grid_spec=pltpu.PrefetchScalarGridSpec(
            num_scalar_prefetch=1,
            grid=(local_experts,),
            in_specs=[wide, wide, narrow, narrow, narrow] + [pass_spec] * len(received),
            out_specs=(part_spec,) * 4 if received else (pass_spec,) * (owners // 2),
            scratch_shapes=[pltpu.VMEM((2, width // 2, slots), BF16)],
        ),
        compiler_params=params(),
        cost_estimate=cost(15),
        name="expert_keep" if received else "expert_send",
    )(dp_word, xs, cs, hs, gate_grad, up_grad, *received)


def dense_grad_kernel(pairs, place_ref, *refs):
    lefts, rights = refs[:pairs], refs[pairs : 2 * pairs]
    smalls = refs[2 * pairs : -3]
    keep_ref, send_ref, sides = refs[-3:]
    owned = keep_ref.shape[1]
    bit = place_ref[0] % 2
    column = 0
    for i in range(pairs):
        if i == 0 or lefts[i] is not lefts[i - 1]:
            turn_rows(lefts[i][...], sides, owned)
        columns = rights[i].shape[1]
        for out_ref, side in ((send_ref, 1 - bit), (keep_ref, bit)):
            grad = dot(sides[side], rights[i][...]).astype(BF16)
            for q in range(keep_ref.shape[0]):
                out_ref[q, :, column : column + columns] = grad[q * owned : (q + 1) * owned]
        column += columns
    if smalls:
        rows = jnp.concatenate([ref[...] for ref in smalls], axis=0)
        rows = jnp.concatenate([rows, jnp.zeros((LANES - rows.shape[0], rows.shape[1]), F32)], axis=0)
        turned = rows.T.astype(BF16)
        for owner in range(2 * keep_ref.shape[0]):
            piece = turned[owner * owned : (owner + 1) * owned]

            @pl.when(bit == owner % 2)
            def _(owner=owner, piece=piece):
                keep_ref[owner // 2, :, column:] = piece

            @pl.when(bit != owner % 2)
            def _(owner=owner, piece=piece):
                send_ref[owner // 2, :, column:] = piece


def dense_grads(dp_word, pairs, owners, smalls=()):
    rows, width = pairs[0][0].shape
    columns = sum(right.shape[1] for _, right in pairs) + (LANES if smalls else 0)
    return pl.pallas_call(
        functools.partial(dense_grad_kernel, len(pairs)),
        out_shape=(jax.ShapeDtypeStruct((owners // 2, width // owners, columns), BF16),) * 2,
        in_specs=[pl.BlockSpec(memory_space=pltpu.SMEM)] + [vmem()] * (2 * len(pairs) + len(smalls)),
        out_specs=(vmem(),) * 2,
        scratch_shapes=[pltpu.VMEM((2, width // 2, rows), BF16)],
        compiler_params=params(),
        cost_estimate=cost(4),
        name="dense_grads",
    )(dp_word, *(left for left, _ in pairs), *(right for _, right in pairs), *smalls)


def line_up(value, size):
    return lax.ppermute(value, "expert", [(i, i + 1) for i in range(size - 1)])


def line_down(value, size):
    return lax.ppermute(value, "expert", [(i + 1, i) for i in range(size - 1)])


def line_gather(value, size):
    below, above = [], []
    up, down = value, value
    for _ in range(size - 1):
        up = line_up(up, size)
        down = line_down(down, size)
        below.append(up)
        above.append(down)
    return [value] + below + above


def add_low(*terms):
    total = terms[0].astype(F32)
    for term in terms[1:]:
        total = total + term.astype(F32)
    return total.astype(BF16)


def flip(value, bit, size):
    return lax.ppermute(value, "dp", [(i, i ^ bit) for i in range(size)])


def halve(terms, bit, left, dp_place):
    axis = left.index(bit)
    own = (dp_place >> bit) & 1
    return tuple(
        add_low(*(lax.dynamic_index_in_dim(t, side, axis, keepdims=False) for t in terms)) for side in (own, 1 - own)
    )


def start_spread(routes):
    return [
        tuple(t.reshape((2,) * (t.shape[0].bit_length() - 1) + t.shape[1:]) for t in terms) for terms in routes
    ]


def step_spread(routes, stage, dp_size, dp_place):
    bits = list(range(1, dp_size.bit_length() - 1))
    kept, sent = [], []
    for terms, order in zip(routes, (bits, bits[::-1])):
        left = [bit for bit in bits[::-1] if bit not in order[:stage]]
        keep, send = halve(terms, order[stage], left, dp_place)
        kept.append(keep)
        sent.append(flip(send, 1 << order[stage], dp_size))
    sent = lax.optimization_barrier(tuple(sent))
    return list(zip(kept, sent))


def start_dense(terms):
    half = terms[0].shape[2] // 2 // LANES * LANES
    return start_spread([tuple(t[..., :half] for t in terms), tuple(t[..., half:] for t in terms)])


def pass_line(routes, place, size):
    block = jnp.concatenate([add_low(*terms) for terms in routes], axis=-1)
    parts = block.reshape(size, -1, block.shape[-1])
    passed = [lax.dynamic_index_in_dim(parts, place, 0, keepdims=False)]
    for k in range(1, size):
        part = lax.dynamic_index_in_dim(parts, (place + k) % size, 0, keepdims=False)
        passed.append(lax.ppermute(part, "expert", [(i, (i + k) % size) for i in range(size)]))
    return passed


def total_of(parts):
    total = parts[0].astype(F32)
    for part in parts[1:]:
        total = total + part.astype(F32)
    return total


def swap_top(top, axis, size):
    for bit in range(size.bit_length() - 1):
        top = jnp.maximum(top, lax.ppermute(top, axis, [(i, i ^ (1 << bit)) for i in range(size)]))
    return top


def gather_and_top(value, top, dp_size, size):
    below, above = [], []
    up, down = value, value
    for k in range(1, size):
        up, down = line_up(up, size), line_down(down, size)
        if k == 1:
            up, down, top = lax.optimization_barrier((up, down, swap_top(top, "dp", dp_size)))
        below.append(up)
        above.append(down)
    return [value] + below + above, top


def arrival_order(size):
    sources, places = np.zeros((size, size), np.int32), np.zeros((size, size), np.int32)
    for place in range(size):
        spots = [(0, place)]
        for k in range(1, size):
            if place - k >= 0:
                spots.append((k, place - k))
            if place + k < size:
                spots.append((size - 1 + k, place + k))
        sources[place], places[place] = zip(*spots)
    return sources, places


def norm_backward(hidden, factor, gain_vec, grad_in):
    scaled = grad_in * gain_vec
    hidden_grad = factor * scaled - hidden * factor**3 * jnp.mean(
        scaled * hidden, axis=-1, keepdims=True
    )
    return hidden_grad, jnp.sum(grad_in * hidden * factor, axis=0)


def local(
    tokens,
    first_gain,
    query_weight,
    key_weight,
    value_weight,
    output_weight,
    second_gain,
    router_weight,
    gate_weight,
    up_weight,
    down_weight,
    cotangent,
    routes,
    segments,
    threshold,
):
    rows, width = tokens.shape
    query_width, kv_width = query_weight.shape[1], key_weight.shape[1]
    heads, groups = query_width // HDIM, kv_width // HDIM
    ratio = heads // groups
    local_experts = gate_weight.shape[0]
    size, dp_size = lax.axis_size("expert"), lax.axis_size("dp")
    place, dp_place = lax.axis_index("expert"), lax.axis_index("dp")
    experts = local_experts * size
    expert_pad = round_up(experts, 16)
    capacity = rows * routes.shape[1] * 9 // (experts * 8)
    slot_rows = round_up(capacity, 64)

    tables = tuple(
        lax.dynamic_slice_in_dim(jnp.asarray(table), place * rows, rows, 0) for table in rotary_tables(rows * size)
    )
    seg_block = jnp.pad(segments.reshape(rows // LANES, LANES).astype(BF16), ((0, 16 - rows // LANES), (0, 0)))

    normed, first_factor, kv_own = pl.pallas_call(
        front_kernel,
        out_shape=(
            jax.ShapeDtypeStruct((rows, width), BF16),
            jax.ShapeDtypeStruct((rows, 1), F32),
            jax.ShapeDtypeStruct((groups * rows + 16, LANES), BF16),
        ),
        in_specs=[vmem()] * 7,
        out_specs=(vmem(),) * 3,
        compiler_params=params(),
        cost_estimate=cost(4),
        name="front",
    )(tokens, first_gain.reshape(1, width), key_weight, value_weight, *tables, seg_block)
    kv_slots = [kv_own]
    for _ in range(size - 1):
        kv_slots.append(line_up(kv_slots[-1], size))

    cot_own = pl.pallas_call(
        extend_kernel,
        out_shape=jax.ShapeDtypeStruct((rows, width + LANES), BF16),
        in_specs=[vmem()] * 2,
        out_specs=vmem(),
        compiler_params=params(),
        cost_estimate=cost(2),
        name="extend",
    )(cotangent, routes)
    cots = line_gather(cot_own, size)

    query_block = 512
    queries = pl.pallas_call(
        query_kernel,
        out_shape=jax.ShapeDtypeStruct((rows, query_width), BF16),
        grid=(query_width // query_block,),
        in_specs=[
            pl.BlockSpec((rows, width), lambda s: (0, 0)),
            pl.BlockSpec((width, query_block), lambda s: (0, s)),
            pl.BlockSpec((rows, LANES), lambda s: (0, 0)),
            pl.BlockSpec((rows, LANES), lambda s: (0, 0)),
        ],
        out_specs=pl.BlockSpec((rows, query_block), lambda s: (0, s)),
        compiler_params=params(),
        cost_estimate=cost(5),
        name="queries",
    )(normed, query_weight, *tables)

    place_word = place.reshape(1).astype(jnp.int32)
    attended, lse, top = attend(queries, kv_slots, place_word, groups)
    head_top = jnp.max(top.reshape(heads, rows), axis=1).reshape(1, heads)

    hidden_in = tokens.astype(F32)
    hidden_mid = hidden_in + RESIDUAL_SCALE * dot(attended, output_weight, NT)
    second_factor = lax.rsqrt(jnp.mean(hidden_mid * hidden_mid, axis=-1, keepdims=True) + NORM_EPSILON)
    second_normed = (hidden_mid * second_factor * second_gain).astype(BF16)
    normed_blocks, head_top = gather_and_top(second_normed, head_top, dp_size, size)

    router_t = jnp.pad(router_weight.T, ((0, expert_pad - experts), (0, 0)))
    sources, blocks_of = (jnp.asarray(table)[place] for table in arrival_order(size))
    expert_place = jnp.concatenate([(place * local_experts).reshape(1), sources, blocks_of]).astype(jnp.int32)
    saved, grad_blocks, router_part = run_experts(
        expert_place, router_t, gate_weight, up_weight, down_weight, normed_blocks, cots, slot_rows
    )
    grad_blocks = lax.all_to_all(grad_blocks, "expert", 0, 0, tiled=True)

    dp_word = dp_place.reshape(1).astype(jnp.int32)
    mixture = run_mixture(blocks_of, down_weight, saved, slot_rows)
    received = [flip(part, 1, dp_size) for part in run_expert_grads(dp_word, saved, dp_size)]
    keep_a, send_a, keep_b, send_b = run_expert_grads(dp_word, saved, dp_size, received)
    mixture, grad_blocks, send_a, send_b = lax.optimization_barrier((mixture, grad_blocks, send_a, send_b))
    normed_grad = jnp.sum(grad_blocks.astype(F32), axis=0)
    passed = (flip(send_a, 2, dp_size), flip(send_b, dp_size // 2, dp_size))
    mix_one = lax.all_to_all(mixture[0], "expert", 0, 0, tiled=True)

    out_grad = cotangent.astype(F32)
    mid_back, second_gain_part = norm_backward(hidden_mid, second_factor, second_gain, normed_grad)
    mid_grad = out_grad + mid_back
    branch_grad = (RESIDUAL_SCALE * mid_grad).astype(BF16)
    attended_grad = dot(branch_grad, output_weight).astype(BF16)
    query_back, dkv = attend_back(
        queries, attended, attended_grad, lse, tables, kv_slots, place_word, groups
    )
    keep, send = dense_grads(dp_word, [(branch_grad, attended), (normed, query_back)], dp_size)
    stages = dp_size.bit_length() - 2
    from_above = line_down(dkv[size - 1], size)
    from_above, passed, mix_one, keep, send = lax.optimization_barrier((from_above, passed, mix_one, keep, send))
    wide = start_dense((keep, flip(send, 1, dp_size)))
    for k in range(1, size):
        if k > 1:
            from_above = line_down(down, size)
        if k == size - 2:
            from_above, wide = lax.optimization_barrier((from_above, wide))
        if k < size - 1:
            down = add_low(from_above, dkv[size - 1 - k])
    from_above, passed, head_top = lax.optimization_barrier((from_above, passed, head_top))
    head_top = swap_top(head_top, "expert", size)
    mix_two, head_top = lax.optimization_barrier((mixture[1], head_top))
    head_top = head_top.reshape(heads)
    expert_sums = step_spread(start_spread([(keep_a, passed[0]), (keep_b, passed[1])]), 1, dp_size, dp_place)
    mix_two = lax.all_to_all(mix_two, "expert", 0, 0, tiled=True)
    for stage in range(stages):
        wide = step_spread(wide, stage, dp_size, dp_place)
    key_back, value_back = pl.pallas_call(
        unpack_kernel,
        out_shape=(jax.ShapeDtypeStruct((rows, kv_width), BF16),) * 2,
        in_specs=[vmem()] * 4,
        out_specs=(vmem(),) * 2,
        compiler_params=params(),
        cost_estimate=cost(2),
        name="unpack",
    )(dkv[0], from_above, *tables)

    first_grad = dot(query_back, query_weight, NT)
    first_grad = first_grad + dot(key_back, key_weight, NT)
    first_grad = first_grad + dot(value_back, value_weight, NT)
    input_back, first_gain_part = norm_backward(hidden_in, first_factor, first_gain, first_grad)
    input_grad = mid_grad + input_back
    keep, send = dense_grads(
        dp_word,
        [(normed, key_back), (normed, value_back)],
        dp_size,
        (router_part, second_gain_part[None], first_gain_part[None]),
    )
    keep, send, wide, expert_sums = lax.optimization_barrier((keep, send, wide, expert_sums))
    for stage in range(2, stages):
        expert_sums = step_spread(expert_sums, stage, dp_size, dp_place)
    expert_sums = [
        jnp.concatenate([a[w].astype(F32) + b[w].astype(F32) for a, b in expert_sums], axis=-1) for w in range(3)
    ]
    rest = start_dense((keep, flip(send, 1, dp_size)))
    rest = step_spread(rest, 0, dp_size, dp_place)
    wide_parts, rest = lax.optimization_barrier((pass_line(wide, place, size), rest))
    for stage in range(1, stages):
        rest = step_spread(rest, stage, dp_size, dp_place)
    rest_parts = lax.optimization_barrier(pass_line(rest, place, size))
    wide_grad, rest_grad = total_of(wide_parts), total_of(rest_parts)
    mixture = jnp.concatenate([jnp.sum(part.astype(F32), axis=0) for part in (mix_one, mix_two)], axis=1)
    block_out = (hidden_mid + mixture).astype(BF16)
    projection_grad, query_grad = wide_grad[:, :query_width], wide_grad[:, query_width:]
    key_grad = rest_grad[:, :kv_width]
    value_grad = rest_grad[:, kv_width : 2 * kv_width]
    small_grad = rest_grad[:, 2 * kv_width :]

    head_scale = threshold / jnp.maximum(head_top, threshold)
    group_scale = jnp.min(head_scale.reshape(groups, ratio), axis=1)
    row_count = width // (dp_size * size)
    row_start = (dp_place * size + place) * row_count
    query_rows = lax.dynamic_slice_in_dim(query_weight, row_start, row_count, 0).astype(F32)
    key_rows = lax.dynamic_slice_in_dim(key_weight, row_start, row_count, 0).astype(F32)
    query_clipped = (query_rows * jnp.repeat(jnp.sqrt(head_scale), HDIM)[None, :]).astype(BF16)
    key_clipped = (key_rows * jnp.repeat(jnp.sqrt(group_scale), HDIM)[None, :]).astype(BF16)
    return (
        block_out,
        input_grad,
        small_grad[:, expert_pad + 1],
        query_grad,
        key_grad,
        value_grad,
        projection_grad,
        small_grad[:, expert_pad],
        small_grad[:, :experts],
        expert_sums[0],
        expert_sums[1],
        expert_sums[2],
        head_scale,
        query_clipped,
        key_clipped,
    )


def solution(mesh):
    row = P(("dp", "expert"), None)
    vector = P(("dp", "expert"))
    expert_in = P("expert", None, None)
    expert_out = P("expert", "dp", None)
    return jax.shard_map(
        local,
        mesh=mesh,
        in_specs=(row,) + (P(),) * 7 + (expert_in,) * 3 + (row, row, vector, P()),
        out_specs=(row, row, vector)
        + (row,) * 4
        + (vector, row)
        + (expert_out,) * 3
        + (P(), row, row),
        check_vma=False,
    )
```

```python
import functools

import jax
import jax.numpy as jnp
import numpy as np
from jax import lax
from jax.experimental import pallas as pl
from jax.experimental.pallas import tpu as pltpu
from jax.sharding import PartitionSpec as P

HDIM = 64
LANES = 128
ATTENTION_SCALE = 0.015625
RESIDUAL_SCALE = 0.22
NORM_EPSILON = 1e-06
ROTARY_BASE = 10000.0
MASKED_SCORE = -1e30
BF16 = jnp.bfloat16
F32 = jnp.float32
NN = (((1,), (0,)), ((), ()))
NT = (((1,), (1,)), ((), ()))
TN = (((0,), (0,)), ((), ()))
VMEM_LIMIT = 60 * 1024 * 1024
COLUMNS = 512


def dot(left, right, dims=NN):
    return lax.dot_general(left, right, dims, preferred_element_type=F32)


def round_up(count, unit):
    return (count + unit - 1) // unit * unit


def low_lanes(rows):
    return lax.broadcasted_iota(jnp.int32, (rows, LANES), 1) < HDIM


def partner_lanes(slab):
    lane = lax.broadcasted_iota(jnp.int32, slab.shape, 1) % HDIM
    half = HDIM // 2
    return jnp.where(lane < half, pltpu.roll(slab, LANES - half, 1), pltpu.roll(slab, half, 1))


def vmem():
    return pl.BlockSpec(memory_space=pltpu.VMEM)


def params(**more):
    return pltpu.CompilerParams(vmem_limit_bytes=VMEM_LIMIT, **more)


def cost(microseconds):
    return pl.CostEstimate(flops=int(microseconds * 1e6), bytes_accessed=0, transcendentals=0)


def rotary_tables(length):
    half = HDIM // 2
    inverse = np.float32(ROTARY_BASE) ** (np.float32(-2.0) * np.arange(half, dtype=np.float32) / np.float32(HDIM))
    angles = np.arange(length, dtype=np.float32)[:, None] * np.tile(inverse, LANES // half)[None, :]
    angles = angles.astype(np.float32).astype(np.float64)
    sign = np.where(np.arange(LANES) % HDIM < half, -1.0, 1.0)
    return np.cos(angles).astype(np.float32), (np.sin(angles) * sign).astype(np.float32)


def extend_kernel(cotangent_ref, routes_ref, out_ref):
    rows, top_count = routes_ref.shape
    width = cotangent_ref.shape[1]
    lane = lax.broadcasted_iota(jnp.int32, (rows, LANES), 1)
    chosen = jnp.zeros((rows, LANES), F32)
    for k in range(top_count):
        chosen = chosen + jnp.where(routes_ref[:, k : k + 1] == lane, 1.0, 0.0)
    first = lax.broadcasted_iota(jnp.int32, (rows, rows), 0)
    second = lax.broadcasted_iota(jnp.int32, (rows, rows), 1)
    earlier = jnp.where(second < first, 1.0, 0.0).astype(BF16)
    rank = dot(earlier, chosen.astype(BF16))
    out_ref[:, :width] = cotangent_ref[...]
    out_ref[:, width:] = jnp.where(chosen > 0.5, rank, -1.0).astype(BF16)


def front_kernel(tokens_ref, gain_ref, key_ref, value_ref, cos_ref, sin_ref, segments_ref, normed_ref, factor_ref, kv_ref):
    hidden = tokens_ref[...].astype(F32)
    factor = lax.rsqrt(jnp.mean(hidden * hidden, axis=-1, keepdims=True) + NORM_EPSILON)
    normed = (hidden * factor * gain_ref[...]).astype(BF16)
    normed_ref[...] = normed
    factor_ref[...] = factor
    keys = dot(normed, key_ref[...])
    values = dot(normed, value_ref[...])
    cosine, sine = cos_ref[...], sin_ref[...]
    rows = hidden.shape[0]
    low = low_lanes(rows)
    for i in range(keys.shape[1] // LANES):
        slab = keys[:, i * LANES : (i + 1) * LANES]
        slab = slab * cosine + partner_lanes(slab) * sine
        value_slab = values[:, i * LANES : (i + 1) * LANES]
        even, odd = 2 * i * rows, (2 * i + 1) * rows
        kv_ref[even : even + rows, :] = jnp.where(low, slab, pltpu.roll(value_slab, HDIM, 1)).astype(BF16)
        kv_ref[odd : odd + rows, :] = jnp.where(low, pltpu.roll(slab, HDIM, 1), value_slab).astype(BF16)
    kv_ref[keys.shape[1] // HDIM * rows :, :] = segments_ref[...]


def query_kernel(normed_ref, query_ref, cos_ref, sin_ref, out_ref):
    raw = dot(normed_ref[...], query_ref[...])
    cosine, sine = cos_ref[...], sin_ref[...]
    for i in range(raw.shape[1] // LANES):
        slab = raw[:, i * LANES : (i + 1) * LANES]
        slab = slab * cosine + partner_lanes(slab) * sine
        out_ref[:, i * LANES : (i + 1) * LANES] = (slab.astype(BF16).astype(F32) * ATTENTION_SCALE).astype(BF16)


def fill_bias(bias_ref, need_ref, place_ref, seg_row, seg_columns):
    slots, keys, rows = bias_ref.shape
    for k in range(slots):
        allowed = seg_columns[k] == seg_row
        if k == 0:
            allowed = allowed & (
                lax.broadcasted_iota(jnp.int32, (keys, rows), 0) <= lax.broadcasted_iota(jnp.int32, (keys, rows), 1)
            )
        bias_ref[k] = jnp.where(allowed, 0.0, MASKED_SCORE)
    first = jnp.min(seg_row)
    need = jnp.int32(1)
    for k in range(1, slots):
        need = jnp.where((jnp.max(seg_columns[k]) >= first) & (k <= place_ref[0]), k + 1, need)
    need_ref[0] = need


def prepare_bias(bias_ref, need_ref, place_ref, seg_refs):
    slots, keys, _ = bias_ref.shape
    halves = keys // LANES
    seg_rows = [
        jnp.concatenate([ref[j : j + 1, :].astype(F32) for j in range(halves)], axis=1) for ref in seg_refs
    ]
    seg_columns = [jnp.broadcast_to(row, (LANES, keys)).T[:, :1] for row in seg_rows]
    fill_bias(bias_ref, need_ref, place_ref, seg_rows[0], seg_columns)


def head_slab(block, head, upper):
    slab = block[:, (head // 2) * LANES : (head // 2 + 1) * LANES].astype(F32)
    low = low_lanes(slab.shape[0])
    if (head % 2 == 1) != upper:
        slab = pltpu.roll(slab, HDIM, 1)
    return jnp.where(low != upper, slab, 0.0)


def add_bias(scores, bias, ratio):
    rows = bias.shape[1]
    return jnp.concatenate([scores[:, r * rows : (r + 1) * rows] + bias for r in range(ratio)], axis=1)


def attend_kernel(slots, ratio, place_ref, query_ref, *refs):
    kv_refs, seg_refs = refs[:slots], refs[slots : 2 * slots]
    attended_ref, lse_ref, top_ref, bias_ref, stacked_ref, scores_ref, acc_ref, max_ref, need_ref = refs[2 * slots :]
    rows = query_ref.shape[0]
    low = low_lanes(rows)

    @pl.when(pl.program_id(0) == 0)
    def _():
        prepare_bias(bias_ref, need_ref, place_ref, seg_refs)

    need = need_ref[0]
    outs = []
    for group in range(2):
        for r in range(ratio):
            stacked_ref[r * rows : (r + 1) * rows, :] = head_slab(
                query_ref, group * ratio + r, False
            ).astype(BF16)
        for k in range(slots):

            def score(k=k):
                kv = kv_refs[k][group * rows : (group + 1) * rows, :]
                scores = add_bias(dot(kv, stacked_ref[...], NT), bias_ref[k], ratio)
                scores_ref[k] = scores
                top = jnp.max(scores, axis=0, keepdims=True)
                max_ref[...] = top if k == 0 else jnp.maximum(max_ref[...], top)

            if k == 0:
                score()
            else:
                pl.when(k < need)(score)
        for k in range(slots):

            def mix(k=k):
                kv = kv_refs[k][group * rows : (group + 1) * rows, :]
                kv = jnp.where(low, jnp.ones_like(kv), kv)
                weights = jnp.exp(scores_ref[k] - max_ref[...]).astype(BF16)
                part = dot(kv, weights, TN)
                acc_ref[...] = part if k == 0 else acc_ref[...] + part

            if k == 0:
                mix()
            else:
                pl.when(k < need)(mix)
        total = acc_ref[:1, :]
        lse_ref[0, group : group + 1, :] = max_ref[...] + jnp.log(total)
        top_ref[0, group : group + 1, :] = max_ref[...]
        mixed = acc_ref[HDIM:, :] / total
        for r in range(ratio):
            outs.append(mixed[:, r * rows : (r + 1) * rows])
    for i in range(len(outs) // 2):
        slab = jnp.concatenate([outs[2 * i], outs[2 * i + 1]], axis=0)
        attended_ref[:, i * LANES : (i + 1) * LANES] = slab.T.astype(BF16)


def kv_specs(slots, groups, rows):
    return [pl.BlockSpec((2 * rows, LANES), lambda s: (s, 0))] * slots + [
        pl.BlockSpec((16, LANES), lambda s: (groups * rows // 16, 0))
    ] * slots


def attend(queries, kv_slots, place, groups):
    slots = len(kv_slots)
    rows, width = queries.shape
    ratio = width // HDIM // groups
    steps = groups // 2
    block = 2 * ratio * HDIM
    stats = pl.BlockSpec((1, 2, ratio * rows), lambda s: (s, 0, 0))
    return pl.pallas_call(
        functools.partial(attend_kernel, slots, ratio),
        out_shape=(jax.ShapeDtypeStruct((rows, width), BF16),)
        + (jax.ShapeDtypeStruct((steps, 2, ratio * rows), F32),) * 2,
        grid=(steps,),
        in_specs=[
            pl.BlockSpec(memory_space=pltpu.SMEM),
            pl.BlockSpec((rows, block), lambda s: (0, s)),
        ]
        + kv_specs(slots, groups, rows),
        out_specs=(pl.BlockSpec((rows, block), lambda s: (0, s)), stats, stats),
        scratch_shapes=[
            pltpu.VMEM((slots, rows, rows), F32),
            pltpu.VMEM((ratio * rows, LANES), BF16),
            pltpu.VMEM((slots, rows, ratio * rows), F32),
            pltpu.VMEM((LANES, ratio * rows), F32),
            pltpu.VMEM((1, ratio * rows), F32),
            pltpu.SMEM((1,), jnp.int32),
        ],
        compiler_params=params(),
        cost_estimate=cost(20),
        name="attend",
    )(place, queries, *kv_slots, *kv_slots)


def attend_back_kernel(slots, ratio, place_ref, query_ref, attended_ref, grad_ref, lse_ref, cos_ref, sin_ref, *refs):
    kv_refs, seg_refs = refs[:slots], refs[slots : 2 * slots]
    refs = refs[2 * slots :]
    back_ref, dkv_refs = refs[0], refs[1 : slots + 1]
    bias_ref, query_s, grad_s, acc_ref, delta_s, need_ref = refs[slots + 1 :]
    rows = query_ref.shape[0]

    @pl.when(pl.program_id(0) == 0)
    def _():
        prepare_bias(bias_ref, need_ref, place_ref, seg_refs)

    need = need_ref[0]
    outs = []
    for group in range(2):
        for r in range(ratio):
            head = group * ratio + r
            part = slice(r * rows, (r + 1) * rows)
            query_s[part, :] = head_slab(query_ref, head, False).astype(BF16)
            grad = head_slab(grad_ref, head, True)
            grad_s[part, :] = grad.astype(BF16)
            product = (grad * head_slab(attended_ref, head, True)).T
            delta_s[:, part] = jnp.sum(product, axis=0, keepdims=True)
        for k in range(slots):

            def step(k=k):
                kv = kv_refs[k][group * rows : (group + 1) * rows, :]
                scores = add_bias(dot(kv, query_s[...], NT), bias_ref[k], ratio)
                weights = jnp.exp(scores - lse_ref[0, group : group + 1, :])
                weight_grad = dot(kv, grad_s[...], NT)
                score_grad = (weights * (weight_grad - delta_s[...])).astype(BF16)
                part = dot(kv, score_grad, TN)
                acc_ref[...] = part if k == 0 else acc_ref[...] + part
                dkv_refs[k][group * rows : (group + 1) * rows, :] = (
                    dot(score_grad, query_s[...]) + dot(weights.astype(BF16), grad_s[...])
                ).astype(BF16)

            if k == 0:
                step()
            else:
                pl.when(k < need)(step)

                @pl.when(k >= need)
                def _(k=k):
                    dkv_refs[k][group * rows : (group + 1) * rows, :] = jnp.zeros((rows, LANES), BF16)

        for r in range(ratio):
            outs.append(acc_ref[:HDIM, r * rows : (r + 1) * rows] * ATTENTION_SCALE)
    cosine, sine = cos_ref[...], sin_ref[...]
    for i in range(len(outs) // 2):
        slab = jnp.concatenate([outs[2 * i], outs[2 * i + 1]], axis=0).T
        slab = slab * cosine - partner_lanes(slab) * sine
        back_ref[:, i * LANES : (i + 1) * LANES] = slab.astype(BF16)


def attend_back(queries, attended, grad, lse, tables, kv_slots, place, groups):
    slots = len(kv_slots)
    rows, width = queries.shape
    ratio = width // HDIM // groups
    steps = groups // 2
    block = 2 * ratio * HDIM
    whole = pl.BlockSpec((rows, LANES), lambda s: (0, 0))
    wide = pl.BlockSpec((rows, block), lambda s: (0, s))
    out = pl.pallas_call(
        functools.partial(attend_back_kernel, slots, ratio),
        out_shape=(jax.ShapeDtypeStruct((rows, width), BF16),)
        + (jax.ShapeDtypeStruct((groups * rows, LANES), BF16),) * slots,
        grid=(steps,),
        in_specs=[
            pl.BlockSpec(memory_space=pltpu.SMEM),
            wide,
            wide,
            wide,
            pl.BlockSpec((1, 2, ratio * rows), lambda s: (s, 0, 0)),
            whole,
            whole,
        ]
        + kv_specs(slots, groups, rows),
        out_specs=(wide,) + (pl.BlockSpec((2 * rows, LANES), lambda s: (s, 0)),) * slots,
        scratch_shapes=[
            pltpu.VMEM((slots, rows, rows), F32),
            pltpu.VMEM((ratio * rows, LANES), BF16),
            pltpu.VMEM((ratio * rows, LANES), BF16),
            pltpu.VMEM((LANES, ratio * rows), F32),
            pltpu.VMEM((1, ratio * rows), F32),
            pltpu.SMEM((1,), jnp.int32),
        ],
        compiler_params=params(),
        cost_estimate=cost(2),
        name="attend_back",
    )(place, queries, attended, grad, lse, *tables, *kv_slots, *kv_slots)
    return out[0], out[1:]


def unpack_kernel(own_ref, above_ref, cos_ref, sin_ref, key_ref, value_ref):
    rows = cos_ref.shape[0]
    low = low_lanes(rows)
    cosine, sine = cos_ref[...], sin_ref[...]
    for i in range(key_ref.shape[1] // LANES):
        even, odd = (
            own_ref[g * rows : (g + 1) * rows, :].astype(F32) + above_ref[g * rows : (g + 1) * rows, :].astype(F32)
            for g in (2 * i, 2 * i + 1)
        )
        slab = jnp.where(low, even, pltpu.roll(odd, HDIM, 1))
        slab = slab * cosine - partner_lanes(slab) * sine
        key_ref[:, i * LANES : (i + 1) * LANES] = slab.astype(BF16)
        value_ref[:, i * LANES : (i + 1) * LANES] = jnp.where(
            low, pltpu.roll(even, HDIM, 1), odd
        ).astype(BF16)


def expert_kernel(blocks, slot_rows, local_experts, place_ref, router_ref, gate_ref, up_ref, down_ref, *refs):
    sources = 2 * blocks - 1
    normed_in, cot_in = refs[:sources], refs[sources : 2 * sources]
    xs_out, cs_out, hs_ref, gate_grad_ref, up_grad_ref, hits, grad_out, router_grad_ref = refs[2 * sources : 2 * sources + 8]
    x_all, c_all, info, gates, back, xs_all, cs_all, gate_slots, slot_grads, sems, save_sem, out_sem = refs[2 * sources + 8 :]
    step = pl.program_id(0)
    rows, width = x_all.shape[1:]
    expert_pad = router_ref.shape[0]
    first_expert = place_ref[0]
    mine = pl.ds(first_expert + step, 1)

    def source_copies(i, s):
        return (
            pltpu.make_async_copy(normed_in[s], x_all.at[i], sems.at[0, i]),
            pltpu.make_async_copy(cot_in[s], c_all.at[i], sems.at[1, i]),
        )

    def save_copies():
        return (
            pltpu.make_async_copy(xs_all, xs_out, save_sem.at[0]),
            pltpu.make_async_copy(cs_all, cs_out, save_sem.at[1]),
        )

    @pl.when(step == 0)
    def _():
        for i in range(blocks):
            for s in range(sources):

                @pl.when(place_ref[1 + i] == s)
                def _(i=i, s=s):
                    for copy in source_copies(i, s):
                        copy.start()

        same = jnp.where(
            lax.broadcasted_iota(jnp.int32, (rows, rows), 0) == lax.broadcasted_iota(jnp.int32, (rows, rows), 1),
            1.0,
            0.0,
        ).astype(BF16)
        slot_ids = lax.broadcasted_iota(jnp.int32, (slot_rows, rows), 0).astype(F32)
        back[...] = jnp.zeros_like(back)
        for i in range(blocks):
            for copy in source_copies(i, 0):
                copy.wait()
            info[i] = dot(c_all[i, :, width:], same, TN)
            logits = dot(router_ref[...], x_all[i], NT)
            logits = jnp.where(info[i, :expert_pad, :] >= 0, logits, MASKED_SCORE)
            weights = jnp.exp(logits - jnp.max(logits, axis=0, keepdims=True))
            gates[i] = weights / jnp.sum(weights, axis=0, keepdims=True)
            for e in range(local_experts):
                own = pl.ds(first_expert + e, 1)
                hit = slot_ids == info[i, own, :]
                gate_slots[e, i * slot_rows : (i + 1) * slot_rows, :] = RESIDUAL_SCALE * jnp.sum(
                    jnp.where(hit, gates[i, own, :], 0.0), axis=-1, keepdims=True
                )
                hits[i, e * slot_rows : (e + 1) * slot_rows, :] = jnp.where(hit, 1.0, 0.0).astype(BF16)
            for source, target in ((x_all, xs_all), (c_all, cs_all)):
                for c in range(width // COLUMNS):
                    columns = slice(c * COLUMNS, (c + 1) * COLUMNS)
                    picked = dot(hits[i], source[i, :, columns]).astype(BF16)
                    for e in range(local_experts):
                        target[e, i * slot_rows : (i + 1) * slot_rows, columns] = picked[
                            e * slot_rows : (e + 1) * slot_rows
                        ]
        for copy in save_copies():
            copy.start()

    gate_slot = gate_slots[step]
    gate_pre = dot(xs_all[step], gate_ref[0])
    up_pre = dot(xs_all[step], up_ref[0])
    raw_grad = dot(cs_all[step], down_ref[0])
    sigmoid = 1.0 / (1.0 + jnp.exp(-gate_pre))
    active = gate_pre * sigmoid
    expert_hidden = (active * up_pre).astype(BF16).astype(F32)
    hs_ref[0] = (expert_hidden * gate_slot).astype(BF16)
    back_slot = jnp.sum(expert_hidden * raw_grad, axis=-1, keepdims=True) * RESIDUAL_SCALE
    hidden_grad = raw_grad * gate_slot
    gate_grad_ref[0] = (hidden_grad * up_pre * sigmoid * (1.0 + gate_pre * (1.0 - sigmoid))).astype(BF16)
    up_grad_ref[0] = (hidden_grad * active).astype(BF16)
    spot = pl.ds(pl.multiple_of(step * slot_rows, slot_rows), slot_rows)
    for c in range(width // COLUMNS):
        columns = slice(c * COLUMNS, (c + 1) * COLUMNS)
        slot_grad = (
            dot(gate_grad_ref[0], gate_ref[0, columns, :], NT) + dot(up_grad_ref[0], up_ref[0, columns, :], NT)
        ).astype(BF16)
        for i in range(blocks):
            slot_grads[i, spot, columns] = slot_grad[i * slot_rows : (i + 1) * slot_rows]
    for i in range(blocks):
        part = slice(i * slot_rows, (i + 1) * slot_rows)
        back_row = jnp.sum(hits[i, spot, :].astype(F32) * back_slot[part], axis=0, keepdims=True)
        back[i, mine, :] = back_row * gates[i, mine, :]

    @pl.when(step == local_experts - 1)
    def _():
        def copy(i):
            return pltpu.make_async_copy(
                c_all.at[i, :, pl.ds(0, width)], grad_out.at[place_ref[1 + blocks + i]], out_sem.at[i]
            )

        router_sum = None
        for i in range(blocks):
            share = back[i]
            logit_grad = (share - gates[i] * jnp.sum(share, axis=0, keepdims=True)).astype(BF16)
            turned = hits[i].T
            for c in range(width // COLUMNS):
                columns = slice(c * COLUMNS, (c + 1) * COLUMNS)
                c_all[i, :, columns] = (
                    dot(turned, slot_grads[i, :, columns]) + dot(logit_grad, router_ref[:, columns], TN)
                ).astype(BF16)
            copy(i).start()
            part = dot(logit_grad, x_all[i])
            router_sum = part if router_sum is None else router_sum + part
        router_grad_ref[...] = router_sum
        for i in range(blocks):
            copy(i).wait()
        for saved in save_copies():
            saved.wait()


def run_experts(place, router_t, gate_weight, up_weight, down_weight, normed, cots, slot_rows):
    local_experts, width, hidden = gate_weight.shape
    sources = len(normed)
    blocks = (sources + 1) // 2
    rows = normed[0].shape[0]
    expert_pad = router_t.shape[0]
    slots = blocks * slot_rows
    stacked = local_experts * slot_rows
    anywhere = pl.BlockSpec(memory_space=pl.ANY)
    weight_spec = pl.BlockSpec((1, width, hidden), lambda e, place: (e, 0, 0))
    narrow = pl.BlockSpec((1, slots, hidden), lambda e, place: (e, 0, 0))
    wide_shape = jax.ShapeDtypeStruct((local_experts, slots, width), BF16)
    narrow_shape = jax.ShapeDtypeStruct((local_experts, slots, hidden), BF16)
    out = pl.pallas_call(
        functools.partial(expert_kernel, blocks, slot_rows, local_experts),
        out_shape=(
            wide_shape,
            wide_shape,
            narrow_shape,
            narrow_shape,
            narrow_shape,
            jax.ShapeDtypeStruct((blocks, stacked, rows), BF16),
            jax.ShapeDtypeStruct((blocks, rows, width), BF16),
            jax.ShapeDtypeStruct((expert_pad, width), F32),
        ),
        grid_spec=pltpu.PrefetchScalarGridSpec(
            num_scalar_prefetch=1,
            grid=(local_experts,),
            in_specs=[pl.BlockSpec((expert_pad, width), lambda e, place: (0, 0))]
            + [weight_spec] * 3
            + [anywhere] * (2 * sources),
            out_specs=(
                anywhere,
                anywhere,
                narrow,
                narrow,
                narrow,
                pl.BlockSpec((blocks, stacked, rows), lambda e, place: (0, 0, 0)),
                anywhere,
                pl.BlockSpec((expert_pad, width), lambda e, place: (0, 0)),
            ),
            scratch_shapes=[
                pltpu.VMEM((blocks, rows, width), BF16),
                pltpu.VMEM((blocks, rows, width + LANES), BF16),
                pltpu.VMEM((blocks, LANES, rows), F32),
                pltpu.VMEM((blocks, expert_pad, rows), F32),
                pltpu.VMEM((blocks, expert_pad, rows), F32),
                pltpu.VMEM((local_experts, slots, width), BF16),
                pltpu.VMEM((local_experts, slots, width), BF16),
                pltpu.VMEM((local_experts, slots, 1), F32),
                pltpu.VMEM((blocks, stacked, width), BF16),
                pltpu.SemaphoreType.DMA((2, blocks)),
                pltpu.SemaphoreType.DMA((2,)),
                pltpu.SemaphoreType.DMA((blocks,)),
            ],
        ),
        compiler_params=params(),
        cost_estimate=cost(45),
        name="experts",
    )(place, router_t, gate_weight, up_weight, down_weight, *normed, *cots)
    return out[:6], out[6], out[7]


def mixture_kernel(blocks, slot_rows, local_experts, order_ref, down_ref, hs_ref, hits_ref, mix_one, mix_two, slot_outs, mix_low, out_sem):
    step = pl.program_id(0)
    width = down_ref.shape[1]
    spot = pl.ds(pl.multiple_of(step * slot_rows, slot_rows), slot_rows)
    for c in range(width // COLUMNS):
        columns = slice(c * COLUMNS, (c + 1) * COLUMNS)
        slot_out = dot(hs_ref[0], down_ref[0, columns, :], NT).astype(BF16)
        for i in range(blocks):
            slot_outs[i, spot, columns] = slot_out[i * slot_rows : (i + 1) * slot_rows]

    @pl.when(step == local_experts - 1)
    def _():
        def copy(i, h):
            columns = pl.ds(h * (width // 2), width // 2)
            return pltpu.make_async_copy(
                mix_low.at[i, :, columns], (mix_one, mix_two)[h].at[order_ref[i]], out_sem.at[i, h]
            )

        for i in range(blocks):
            turned = hits_ref[i].T
            for c in range(width // COLUMNS):
                columns = slice(c * COLUMNS, (c + 1) * COLUMNS)
                mix_low[i, :, columns] = dot(turned, slot_outs[i, :, columns]).astype(BF16)
            for h in range(2):
                copy(i, h).start()
        for i in range(blocks):
            for h in range(2):
                copy(i, h).wait()


def run_mixture(order, down_weight, saved, slot_rows):
    hs, hits = saved[2], saved[5]
    local_experts, width, hidden = down_weight.shape
    blocks, stacked, rows = hits.shape
    return pl.pallas_call(
        functools.partial(mixture_kernel, blocks, slot_rows, local_experts),
        out_shape=(jax.ShapeDtypeStruct((blocks, rows, width // 2), BF16),) * 2,
        grid_spec=pltpu.PrefetchScalarGridSpec(
            num_scalar_prefetch=1,
            grid=(local_experts,),
            in_specs=[
                pl.BlockSpec((1, width, hidden), lambda e, order: (e, 0, 0)),
                pl.BlockSpec((1, hs.shape[1], hidden), lambda e, order: (e, 0, 0)),
                pl.BlockSpec((blocks, stacked, rows), lambda e, order: (0, 0, 0)),
            ],
            out_specs=(pl.BlockSpec(memory_space=pl.ANY),) * 2,
            scratch_shapes=[
                pltpu.VMEM((blocks, stacked, width), BF16),
                pltpu.VMEM((blocks, rows, width), BF16),
                pltpu.SemaphoreType.DMA((blocks, 2)),
            ],
        ),
        compiler_params=params(),
        cost_estimate=cost(10),
        name="mixture",
    )(order, down_weight, hs, hits)


def turn_rows(block, sides_ref, owned):
    width = block.shape[1]
    chunk = int(np.lcm(2 * owned, LANES))
    for c in range(width // chunk):
        turned = block[:, c * chunk : (c + 1) * chunk].T
        for o in range(chunk // owned):
            owner = c * (chunk // owned) + o
            spot = owner // 2 * owned
            sides_ref[owner % 2, spot : spot + owned, :] = turned[o * owned : (o + 1) * owned]


def grad_products(side, xs_ref, cs_ref, hs_ref, gate_grad_ref, up_grad_ref, sides, owned):
    for left_ref, rights in ((xs_ref, ((0, gate_grad_ref), (1, up_grad_ref))), (cs_ref, ((2, hs_ref),))):
        turn_rows(left_ref[0], sides, owned)
        for w, right_ref in rights:
            yield w, dot(sides[side], right_ref[0])


def expert_send_kernel(place_ref, xs_ref, cs_ref, hs_ref, gate_grad_ref, up_grad_ref, *refs):
    send_refs, sides = refs[:-1], refs[-1]
    owned = send_refs[0].shape[2]
    side = 1 - place_ref[0] % 2
    for w, grad in grad_products(side, xs_ref, cs_ref, hs_ref, gate_grad_ref, up_grad_ref, sides, owned):
        for q, send_ref in enumerate(send_refs):
            send_ref[w, 0] = grad[q * owned : (q + 1) * owned].astype(BF16)


def expert_keep_kernel(bits, place_ref, xs_ref, cs_ref, hs_ref, gate_grad_ref, up_grad_ref, *refs):
    count = 1 << (bits - 1)
    received_refs, outs, sides = refs[:count], refs[count : count + 4], refs[-1]
    owned = received_refs[0].shape[2]
    hidden = hs_ref.shape[2] // 2
    side = place_ref[0] % 2
    for w, grad in grad_products(side, xs_ref, cs_ref, hs_ref, gate_grad_ref, up_grad_ref, sides, owned):
        for q in range(count):
            piece = (grad[q * owned : (q + 1) * owned] + received_refs[q][w, 0].astype(F32)).astype(BF16)
            for route, bit in enumerate((1, bits - 1)):
                part = piece[:, route * hidden : (route + 1) * hidden]
                own = (place_ref[0] >> bit) & 1
                spot = (q >> bit << (bit - 1)) | (q & ((1 << (bit - 1)) - 1))
                here = q >> (bit - 1) & 1

                @pl.when(own == here)
                def _(route=route, part=part, spot=spot, w=w):
                    outs[2 * route][spot, w, 0] = part

                @pl.when(own != here)
                def _(route=route, part=part, spot=spot, w=w):
                    outs[2 * route + 1][spot, w, 0] = part


def run_expert_grads(dp_word, saved, owners, received=()):
    xs, cs, hs, gate_grad, up_grad, _ = saved
    local_experts, slots, width = xs.shape
    hidden = hs.shape[2]
    owned = width // owners
    wide = pl.BlockSpec((1, slots, width), lambda e, place: (e, 0, 0))
    narrow = pl.BlockSpec((1, slots, hidden), lambda e, place: (e, 0, 0))
    pass_spec = pl.BlockSpec((3, 1, owned, hidden), lambda e, place: (0, e, 0, 0))
    pass_shape = jax.ShapeDtypeStruct((3, local_experts, owned, hidden), BF16)
    part_spec = pl.BlockSpec((owners // 4, 3, 1, owned, hidden // 2), lambda e, place: (0, 0, e, 0, 0))
    part_shape = jax.ShapeDtypeStruct((owners // 4, 3, local_experts, owned, hidden // 2), BF16)
    return pl.pallas_call(
        functools.partial(expert_keep_kernel, owners.bit_length() - 1) if received else expert_send_kernel,
        out_shape=(part_shape,) * 4 if received else (pass_shape,) * (owners // 2),
        grid_spec=pltpu.PrefetchScalarGridSpec(
            num_scalar_prefetch=1,
            grid=(local_experts,),
            in_specs=[wide, wide, narrow, narrow, narrow] + [pass_spec] * len(received),
            out_specs=(part_spec,) * 4 if received else (pass_spec,) * (owners // 2),
            scratch_shapes=[pltpu.VMEM((2, width // 2, slots), BF16)],
        ),
        compiler_params=params(),
        cost_estimate=cost(15),
        name="expert_keep" if received else "expert_send",
    )(dp_word, xs, cs, hs, gate_grad, up_grad, *received)


def dense_grad_kernel(pairs, place_ref, *refs):
    lefts, rights = refs[:pairs], refs[pairs : 2 * pairs]
    smalls = refs[2 * pairs : -3]
    keep_ref, send_ref, sides = refs[-3:]
    owned = keep_ref.shape[1]
    bit = place_ref[0] % 2
    column = 0
    for i in range(pairs):
        if i == 0 or lefts[i] is not lefts[i - 1]:
            turn_rows(lefts[i][...], sides, owned)
        columns = rights[i].shape[1]
        for out_ref, side in ((send_ref, 1 - bit), (keep_ref, bit)):
            grad = dot(sides[side], rights[i][...]).astype(BF16)
            for q in range(keep_ref.shape[0]):
                out_ref[q, :, column : column + columns] = grad[q * owned : (q + 1) * owned]
        column += columns
    if smalls:
        rows = jnp.concatenate([ref[...] for ref in smalls], axis=0)
        rows = jnp.concatenate([rows, jnp.zeros((LANES - rows.shape[0], rows.shape[1]), F32)], axis=0)
        turned = rows.T.astype(BF16)
        for owner in range(2 * keep_ref.shape[0]):
            piece = turned[owner * owned : (owner + 1) * owned]

            @pl.when(bit == owner % 2)
            def _(owner=owner, piece=piece):
                keep_ref[owner // 2, :, column:] = piece

            @pl.when(bit != owner % 2)
            def _(owner=owner, piece=piece):
                send_ref[owner // 2, :, column:] = piece


def dense_grads(dp_word, pairs, owners, smalls=()):
    rows, width = pairs[0][0].shape
    columns = sum(right.shape[1] for _, right in pairs) + (LANES if smalls else 0)
    return pl.pallas_call(
        functools.partial(dense_grad_kernel, len(pairs)),
        out_shape=(jax.ShapeDtypeStruct((owners // 2, width // owners, columns), BF16),) * 2,
        in_specs=[pl.BlockSpec(memory_space=pltpu.SMEM)] + [vmem()] * (2 * len(pairs) + len(smalls)),
        out_specs=(vmem(),) * 2,
        scratch_shapes=[pltpu.VMEM((2, width // 2, rows), BF16)],
        compiler_params=params(),
        cost_estimate=cost(4),
        name="dense_grads",
    )(dp_word, *(left for left, _ in pairs), *(right for _, right in pairs), *smalls)


def line_up(value, size):
    return lax.ppermute(value, "expert", [(i, i + 1) for i in range(size - 1)])


def line_down(value, size):
    return lax.ppermute(value, "expert", [(i + 1, i) for i in range(size - 1)])


def line_gather(value, size):
    below, above = [], []
    up, down = value, value
    for _ in range(size - 1):
        up = line_up(up, size)
        down = line_down(down, size)
        below.append(up)
        above.append(down)
    return [value] + below + above


def add_low(*terms):
    total = terms[0].astype(F32)
    for term in terms[1:]:
        total = total + term.astype(F32)
    return total.astype(BF16)


def flip(value, bit, size):
    return lax.ppermute(value, "dp", [(i, i ^ bit) for i in range(size)])


def halve(terms, bit, left, dp_place):
    axis = left.index(bit)
    own = (dp_place >> bit) & 1
    return tuple(
        add_low(*(lax.dynamic_index_in_dim(t, side, axis, keepdims=False) for t in terms)) for side in (own, 1 - own)
    )


def start_spread(routes):
    return [
        tuple(t.reshape((2,) * (t.shape[0].bit_length() - 1) + t.shape[1:]) for t in terms) for terms in routes
    ]


def step_spread(routes, stage, dp_size, dp_place):
    bits = list(range(1, dp_size.bit_length() - 1))
    kept, sent = [], []
    for terms, order in zip(routes, (bits, bits[::-1])):
        left = [bit for bit in bits[::-1] if bit not in order[:stage]]
        keep, send = halve(terms, order[stage], left, dp_place)
        kept.append(keep)
        sent.append(flip(send, 1 << order[stage], dp_size))
    sent = lax.optimization_barrier(tuple(sent))
    return list(zip(kept, sent))


def start_dense(terms):
    half = terms[0].shape[2] // 2 // LANES * LANES
    return start_spread([tuple(t[..., :half] for t in terms), tuple(t[..., half:] for t in terms)])


def pass_line(routes, place, size):
    block = jnp.concatenate([add_low(*terms) for terms in routes], axis=-1)
    parts = block.reshape(size, -1, block.shape[-1])
    passed = [lax.dynamic_index_in_dim(parts, place, 0, keepdims=False)]
    for k in range(1, size):
        part = lax.dynamic_index_in_dim(parts, (place + k) % size, 0, keepdims=False)
        passed.append(lax.ppermute(part, "expert", [(i, (i + k) % size) for i in range(size)]))
    return passed


def total_of(parts):
    total = parts[0].astype(F32)
    for part in parts[1:]:
        total = total + part.astype(F32)
    return total


def swap_top(top, axis, size):
    for bit in range(size.bit_length() - 1):
        top = jnp.maximum(top, lax.ppermute(top, axis, [(i, i ^ (1 << bit)) for i in range(size)]))
    return top


def gather_and_top(value, top, dp_size, size):
    below, above = [], []
    up, down = value, value
    for k in range(1, size):
        up, down = line_up(up, size), line_down(down, size)
        if k == 1:
            up, down, top = lax.optimization_barrier((up, down, swap_top(top, "dp", dp_size)))
        below.append(up)
        above.append(down)
    return [value] + below + above, top


def arrival_order(size):
    sources, places = np.zeros((size, size), np.int32), np.zeros((size, size), np.int32)
    for place in range(size):
        spots = [(0, place)]
        for k in range(1, size):
            if place - k >= 0:
                spots.append((k, place - k))
            if place + k < size:
                spots.append((size - 1 + k, place + k))
        sources[place], places[place] = zip(*spots)
    return sources, places


def norm_backward(hidden, factor, gain_vec, grad_in):
    scaled = grad_in * gain_vec
    hidden_grad = factor * scaled - hidden * factor**3 * jnp.mean(
        scaled * hidden, axis=-1, keepdims=True
    )
    return hidden_grad, jnp.sum(grad_in * hidden * factor, axis=0)


def local(
    tokens,
    first_gain,
    query_weight,
    key_weight,
    value_weight,
    output_weight,
    second_gain,
    router_weight,
    gate_weight,
    up_weight,
    down_weight,
    cotangent,
    routes,
    segments,
    threshold,
):
    rows, width = tokens.shape
    query_width, kv_width = query_weight.shape[1], key_weight.shape[1]
    heads, groups = query_width // HDIM, kv_width // HDIM
    ratio = heads // groups
    local_experts = gate_weight.shape[0]
    size, dp_size = lax.axis_size("expert"), lax.axis_size("dp")
    place, dp_place = lax.axis_index("expert"), lax.axis_index("dp")
    experts = local_experts * size
    expert_pad = round_up(experts, 16)
    capacity = rows * routes.shape[1] * 9 // (experts * 8)
    slot_rows = round_up(capacity, 64)

    tables = tuple(
        lax.dynamic_slice_in_dim(jnp.asarray(table), place * rows, rows, 0) for table in rotary_tables(rows * size)
    )
    seg_block = jnp.pad(segments.reshape(rows // LANES, LANES).astype(BF16), ((0, 16 - rows // LANES), (0, 0)))

    normed, first_factor, kv_own = pl.pallas_call(
        front_kernel,
        out_shape=(
            jax.ShapeDtypeStruct((rows, width), BF16),
            jax.ShapeDtypeStruct((rows, 1), F32),
            jax.ShapeDtypeStruct((groups * rows + 16, LANES), BF16),
        ),
        in_specs=[vmem()] * 7,
        out_specs=(vmem(),) * 3,
        compiler_params=params(),
        cost_estimate=cost(4),
        name="front",
    )(tokens, first_gain.reshape(1, width), key_weight, value_weight, *tables, seg_block)
    kv_slots = [kv_own]
    for _ in range(size - 1):
        kv_slots.append(line_up(kv_slots[-1], size))

    cot_own = pl.pallas_call(
        extend_kernel,
        out_shape=jax.ShapeDtypeStruct((rows, width + LANES), BF16),
        in_specs=[vmem()] * 2,
        out_specs=vmem(),
        compiler_params=params(),
        cost_estimate=cost(2),
        name="extend",
    )(cotangent, routes)
    cots = line_gather(cot_own, size)

    query_block = 512
    queries = pl.pallas_call(
        query_kernel,
        out_shape=jax.ShapeDtypeStruct((rows, query_width), BF16),
        grid=(query_width // query_block,),
        in_specs=[
            pl.BlockSpec((rows, width), lambda s: (0, 0)),
            pl.BlockSpec((width, query_block), lambda s: (0, s)),
            pl.BlockSpec((rows, LANES), lambda s: (0, 0)),
            pl.BlockSpec((rows, LANES), lambda s: (0, 0)),
        ],
        out_specs=pl.BlockSpec((rows, query_block), lambda s: (0, s)),
        compiler_params=params(),
        cost_estimate=cost(5),
        name="queries",
    )(normed, query_weight, *tables)

    place_word = place.reshape(1).astype(jnp.int32)
    attended, lse, top = attend(queries, kv_slots, place_word, groups)
    head_top = jnp.max(top.reshape(heads, rows), axis=1).reshape(1, heads)

    hidden_in = tokens.astype(F32)
    hidden_mid = hidden_in + RESIDUAL_SCALE * dot(attended, output_weight, NT)
    second_factor = lax.rsqrt(jnp.mean(hidden_mid * hidden_mid, axis=-1, keepdims=True) + NORM_EPSILON)
    second_normed = (hidden_mid * second_factor * second_gain).astype(BF16)
    normed_blocks, head_top = gather_and_top(second_normed, head_top, dp_size, size)

    router_t = jnp.pad(router_weight.T, ((0, expert_pad - experts), (0, 0)))
    sources, blocks_of = (jnp.asarray(table)[place] for table in arrival_order(size))
    expert_place = jnp.concatenate([(place * local_experts).reshape(1), sources, blocks_of]).astype(jnp.int32)
    saved, grad_blocks, router_part = run_experts(
        expert_place, router_t, gate_weight, up_weight, down_weight, normed_blocks, cots, slot_rows
    )
    grad_blocks = lax.all_to_all(grad_blocks, "expert", 0, 0, tiled=True)

    dp_word = dp_place.reshape(1).astype(jnp.int32)
    mixture = run_mixture(blocks_of, down_weight, saved, slot_rows)
    received = [flip(part, 1, dp_size) for part in run_expert_grads(dp_word, saved, dp_size)]
    keep_a, send_a, keep_b, send_b = run_expert_grads(dp_word, saved, dp_size, received)
    mixture, grad_blocks, send_a, send_b = lax.optimization_barrier((mixture, grad_blocks, send_a, send_b))
    normed_grad = jnp.sum(grad_blocks.astype(F32), axis=0)
    passed = (flip(send_a, 2, dp_size), flip(send_b, dp_size // 2, dp_size))
    mix_one = lax.all_to_all(mixture[0], "expert", 0, 0, tiled=True)

    out_grad = cotangent.astype(F32)
    mid_back, second_gain_part = norm_backward(hidden_mid, second_factor, second_gain, normed_grad)
    mid_grad = out_grad + mid_back
    branch_grad = (RESIDUAL_SCALE * mid_grad).astype(BF16)
    attended_grad = dot(branch_grad, output_weight).astype(BF16)
    query_back, dkv = attend_back(
        queries, attended, attended_grad, lse, tables, kv_slots, place_word, groups
    )
    keep, send = dense_grads(dp_word, [(branch_grad, attended), (normed, query_back)], dp_size)
    stages = dp_size.bit_length() - 2
    from_above = line_down(dkv[size - 1], size)
    from_above, passed, mix_one, keep, send = lax.optimization_barrier((from_above, passed, mix_one, keep, send))
    wide = start_dense((keep, flip(send, 1, dp_size)))
    for k in range(1, size):
        if k > 1:
            from_above = line_down(down, size)
        if k == size - 2:
            from_above, wide = lax.optimization_barrier((from_above, wide))
        if k < size - 1:
            down = add_low(from_above, dkv[size - 1 - k])
    from_above, passed, head_top = lax.optimization_barrier((from_above, passed, head_top))
    head_top = swap_top(head_top, "expert", size)
    mix_two, head_top = lax.optimization_barrier((mixture[1], head_top))
    head_top = head_top.reshape(heads)
    expert_sums = step_spread(start_spread([(keep_a, passed[0]), (keep_b, passed[1])]), 1, dp_size, dp_place)
    mix_two = lax.all_to_all(mix_two, "expert", 0, 0, tiled=True)
    for stage in range(stages):
        wide = step_spread(wide, stage, dp_size, dp_place)
    key_back, value_back = pl.pallas_call(
        unpack_kernel,
        out_shape=(jax.ShapeDtypeStruct((rows, kv_width), BF16),) * 2,
        in_specs=[vmem()] * 4,
        out_specs=(vmem(),) * 2,
        compiler_params=params(),
        cost_estimate=cost(2),
        name="unpack",
    )(dkv[0], from_above, *tables)

    first_grad = dot(query_back, query_weight, NT)
    first_grad = first_grad + dot(key_back, key_weight, NT)
    first_grad = first_grad + dot(value_back, value_weight, NT)
    input_back, first_gain_part = norm_backward(hidden_in, first_factor, first_gain, first_grad)
    input_grad = mid_grad + input_back
    keep, send = dense_grads(
        dp_word,
        [(normed, key_back), (normed, value_back)],
        dp_size,
        (router_part, second_gain_part[None], first_gain_part[None]),
    )
    keep, send, wide, expert_sums = lax.optimization_barrier((keep, send, wide, expert_sums))
    for stage in range(2, stages):
        expert_sums = step_spread(expert_sums, stage, dp_size, dp_place)
    expert_sums = [
        jnp.concatenate([a[w].astype(F32) + b[w].astype(F32) for a, b in expert_sums], axis=-1) for w in range(3)
    ]
    rest = start_dense((keep, flip(send, 1, dp_size)))
    rest = step_spread(rest, 0, dp_size, dp_place)
    wide_parts, rest, mix_two = lax.optimization_barrier((pass_line(wide, place, size), rest, mix_two))
    for stage in range(1, stages):
        rest = step_spread(rest, stage, dp_size, dp_place)
    rest_parts = lax.optimization_barrier(pass_line(rest, place, size))
    wide_grad, rest_grad = total_of(wide_parts), total_of(rest_parts)
    mixture = jnp.concatenate([jnp.sum(part.astype(F32), axis=0) for part in (mix_one, mix_two)], axis=1)
    block_out = (hidden_mid + mixture).astype(BF16)
    projection_grad, query_grad = wide_grad[:, :query_width], wide_grad[:, query_width:]
    key_grad = rest_grad[:, :kv_width]
    value_grad = rest_grad[:, kv_width : 2 * kv_width]
    small_grad = rest_grad[:, 2 * kv_width :]

    head_scale = threshold / jnp.maximum(head_top, threshold)
    group_scale = jnp.min(head_scale.reshape(groups, ratio), axis=1)
    row_count = width // (dp_size * size)
    row_start = (dp_place * size + place) * row_count
    query_rows = lax.dynamic_slice_in_dim(query_weight, row_start, row_count, 0).astype(F32)
    key_rows = lax.dynamic_slice_in_dim(key_weight, row_start, row_count, 0).astype(F32)
    query_clipped = (query_rows * jnp.repeat(jnp.sqrt(head_scale), HDIM)[None, :]).astype(BF16)
    key_clipped = (key_rows * jnp.repeat(jnp.sqrt(group_scale), HDIM)[None, :]).astype(BF16)
    return (
        block_out,
        input_grad,
        small_grad[:, expert_pad + 1],
        query_grad,
        key_grad,
        value_grad,
        projection_grad,
        small_grad[:, expert_pad],
        small_grad[:, :experts],
        expert_sums[0],
        expert_sums[1],
        expert_sums[2],
        head_scale,
        query_clipped,
        key_clipped,
    )


def solution(mesh):
    row = P(("dp", "expert"), None)
    vector = P(("dp", "expert"))
    expert_in = P("expert", None, None)
    expert_out = P("expert", "dp", None)
    return jax.shard_map(
        local,
        mesh=mesh,
        in_specs=(row,) + (P(),) * 7 + (expert_in,) * 3 + (row, row, vector, P()),
        out_specs=(row, row, vector)
        + (row,) * 4
        + (vector, row)
        + (expert_out,) * 3
        + (P(), row, row),
        check_vma=False,
    )
```
